32 devices in a mesh: seq: 16 (over z, y, x), dp: 2 (over core).
Axes of the slice: x: 2, y: 2, z: 4, core: 2. Of those that a mesh axis runs over, the one named last changes fastest.
Arguments:
- tokens: bfloat16 [2, 8192, 1280], P('dp', 'seq'), may hold values from -6 to 6
- cotangent: bfloat16 [2, 8192, 1280], P('dp', 'seq'), may hold values from -1.5 to 1.5
- router: bfloat16 [1280, 2], replicated, may hold values from -0.15625 to 0.15625
- logit_scale: float32 [1], replicated, may hold values from 40 to 60
- expert_in: bfloat16 [1280, 10240], P(None, 'seq'), may hold values from -12 to 12
- expert_out: bfloat16 [10240, 1280], P('seq'), may hold values from -0.078125 to 0.078125
Outputs:
- mixed: bfloat16 [2, 8192, 1280], P('dp', 'seq')
- grad_tokens: bfloat16 [2, 8192, 1280], P('dp', 'seq')
- grad_expert_in: float32 [1280, 10240], P('dp', 'seq')
- grad_expert_out: float32 [10240, 1280], P('seq', 'dp')
- grad_router: float32 [1280, 2], replicated
The draws below stay inside these ranges and needn't reach their ends.
All inputs are finite; a program needn't handle non-finite values.
Results may differ from the reference program's by a relative error of at most 0.0085.
The reference program's roundings to bfloat16 on the way count: a program that leaves them out, or rounds other values in their place, can miss the bound.
Values may be sent and summed in bfloat16 or wider, within the bound.
No kernel may reach another device: no remote copies, remote signals or barrier semaphores. Data moves between devices by JAX's collectives and lax.ppermute only.
A program may use at most 64 MiB of HBM per device.

```python
import jax
import jax.numpy as jnp
from jax import lax

D = 1280
FF = 5120
EXPERTS = 2
TOKENS = 8192
CLIPS = 2


def block_levels(rng, extent, pieces, least, largest):
    factor_of, own = 1.0, jax.random.fold_in(rng, 6)
    for axis_at, parts in pieces:
        heights = jnp.exp(jax.random.uniform(jax.random.fold_in(own, axis_at), (parts,), jnp.float32, least / len(pieces), largest / len(pieces)))
        factor_of = factor_of * jnp.repeat(heights, extent[axis_at] // parts).reshape([-1 if axis == axis_at else 1 for axis in range(len(extent))])
    return factor_of


def normal_values(key, dims, width, reach, split=(), held_as=jnp.bfloat16):
    gain = block_levels(key, dims, split, -0.22, 0.18) if split else 1.0
    entries = jax.random.normal(key, dims, jnp.float32) * width * gain
    return jnp.minimum(jnp.maximum(entries, -reach), reach).astype(held_as)


def setup_inputs(seed: int = 0) -> dict:
    streams_of = jax.random.split(jax.random.key(seed), 7)
    tokens = normal_values(streams_of[0], (CLIPS, TOKENS, D), 1.0, 6.0, ((0, 2), (1, 16)))
    cotangent = normal_values(streams_of[1], (CLIPS, TOKENS, D), 0.25, 1.5, ((0, 2), (1, 16)))
    router = normal_values(streams_of[2], (D, EXPERTS), D ** -0.5, 0.15625)
    logit_scale = jnp.clip(jax.random.uniform(streams_of[3], (1,), jnp.float32, 40.0, 60.0), 40.0, 60.0)
    expert_in = normal_values(streams_of[4], (D, EXPERTS * FF), 2.0, 12.0, ((1, 16),))
    expert_out = normal_values(streams_of[5], (EXPERTS * FF, D), FF ** -0.5, 0.078125, ((0, 16),))
    return {"tokens": tokens, "cotangent": cotangent, "router": router, "logit_scale": logit_scale, "expert_in": expert_in, "expert_out": expert_out}


epsilon = 1e-06

def gelu_slope(pre_act):
    cdf = 0.5 * (1.0 + lax.erf(pre_act * 0.7071067811865476))
    return cdf + pre_act * jnp.exp(-0.5 * pre_act * pre_act) * 0.3989422804014327

def reference(tokens, cotangent, router, logit_scale, expert_in, expert_out):
    clip_count = tokens.shape[0]
    phi_f32 = router.astype(jnp.float32)
    phi_scale = lax.rsqrt(lax.optimization_barrier(jnp.sum(phi_f32 * phi_f32, axis=0, keepdims=True)) + epsilon)
    phi_unit = phi_f32 * phi_scale
    phi_norm = phi_unit.astype(jnp.bfloat16)
    weight_in = expert_in.reshape(D, EXPERTS, FF).astype(jnp.float32)
    weight_out = expert_out.reshape(EXPERTS, FF, D).astype(jnp.float32)
    mixed_list = []
    grad_list = []
    grad_w_in = jnp.zeros((D, EXPERTS, FF), jnp.float32)
    grad_w_out = jnp.zeros((EXPERTS, FF, D), jnp.float32)
    phi_grad = jnp.zeros((D, EXPERTS), jnp.float32)
    for clip_index in range(clip_count):
        tok_in = tokens[clip_index]
        tok_cot = cotangent[clip_index]
        tok_f32 = tok_in.astype(jnp.float32)
        tok_scale = lax.rsqrt(lax.optimization_barrier(jnp.sum(tok_f32 * tok_f32, axis=1, keepdims=True)) + epsilon)
        tok_unit = tok_f32 * tok_scale
        tok_norm = tok_unit.astype(jnp.bfloat16)
        logits = logit_scale[0] * jnp.dot(tok_norm, phi_norm, preferred_element_type=jnp.float32)
        exp_scores = jnp.exp(logits)
        totals = lax.optimization_barrier(jnp.sum(exp_scores, axis=0, keepdims=True))
        dispatch_f = exp_scores / totals
        dispatch = dispatch_f.astype(jnp.bfloat16)
        slot_in = jnp.dot(dispatch.T, tok_in, preferred_element_type=jnp.float32)
        slot_x = slot_in.astype(jnp.bfloat16)
        pre_act = jnp.einsum('sd,dsf->sf', slot_x.astype(jnp.float32), weight_in)
        hidden = jax.nn.gelu(pre_act, approximate=False).astype(jnp.bfloat16)
        slot_y = jnp.einsum('sf,sfd->sd', hidden.astype(jnp.float32), weight_out).astype(jnp.bfloat16)
        combine_f = exp_scores / lax.optimization_barrier(jnp.sum(exp_scores, axis=1, keepdims=True))
        combine = combine_f.astype(jnp.bfloat16)
        mixed_list.append(jnp.dot(combine, slot_y, preferred_element_type=jnp.float32).astype(jnp.bfloat16))
        slot_cot = jnp.dot(combine.T, tok_cot, preferred_element_type=jnp.float32).astype(jnp.bfloat16)
        comb_dot = jnp.dot(tok_cot, slot_y.T, preferred_element_type=jnp.float32)
        grad_comb = combine_f * (comb_dot - lax.optimization_barrier(jnp.sum(combine_f * comb_dot, axis=1, keepdims=True)))
        hid_grad = jnp.einsum('sd,sfd->sf', slot_cot.astype(jnp.float32), weight_out)
        pre_grad = (hid_grad * gelu_slope(pre_act)).astype(jnp.bfloat16)
        grad_w_in = grad_w_in + jnp.einsum('sd,sf->dsf', slot_x.astype(jnp.float32), pre_grad.astype(jnp.float32))
        grad_w_out = grad_w_out + jnp.einsum('sf,sd->sfd', hidden.astype(jnp.float32), slot_cot.astype(jnp.float32))
        slot_dx = jnp.einsum('sf,dsf->sd', pre_grad.astype(jnp.float32), weight_in).astype(jnp.bfloat16)
        disp_dot = jnp.dot(tok_in, slot_dx.T, preferred_element_type=jnp.float32)
        column_stat = lax.optimization_barrier(jnp.sum(dispatch.astype(jnp.float32) * disp_dot, axis=0, keepdims=True))
        grad_disp = dispatch_f * (disp_dot - column_stat)
        score_grad = (logit_scale[0] * (grad_comb + grad_disp)).astype(jnp.bfloat16)
        norm_grad = jnp.dot(score_grad, phi_norm.T, preferred_element_type=jnp.float32)
        phi_grad = phi_grad + jnp.dot(tok_norm.T, score_grad, preferred_element_type=jnp.float32)
        through = jnp.dot(dispatch, slot_dx, preferred_element_type=jnp.float32)
        back_norm = tok_scale * (norm_grad - tok_unit * lax.optimization_barrier(jnp.sum(tok_unit * norm_grad, axis=1, keepdims=True)))
        grad_list.append((through + back_norm).astype(jnp.bfloat16))
    grad_router = phi_scale * (phi_grad - phi_unit * lax.optimization_barrier(jnp.sum(phi_unit * phi_grad, axis=0, keepdims=True)))
    return (jnp.stack(mixed_list), jnp.stack(grad_list), grad_w_in.reshape(D, EXPERTS * FF), grad_w_out.reshape(EXPERTS * FF, D), grad_router)
```

```python
import jax
import jax.numpy as jnp
from jax import lax
from jax.sharding import PartitionSpec as P

epsilon = 1e-06


def gelu_slope(pre_act):
    cdf = 0.5 * (1.0 + lax.erf(pre_act * 0.7071067811865476))
    return cdf + pre_act * jnp.exp(-0.5 * pre_act * pre_act) * 0.3989422804014327


def swap(value, axis, mask):
    size = lax.axis_size(axis)
    return lax.ppermute(value, axis, [(i, i ^ mask) for i in range(size)])


def sum_over(value, axis, low, high):
    mask = low
    while mask < high:
        value = value + swap(value, axis, mask)
        mask *= 2
    return value


def scatter_slots(value, axis, group, size):
    mask = size // 2
    while mask >= group:
        half = value.shape[0] // 2
        upper = (lax.axis_index(axis) & mask) != 0
        low, high = value[:half], value[half:]
        keep = jnp.where(upper, high, low)
        give = jnp.where(upper, low, high)
        value = keep + swap(give, axis, mask)
        mask //= 2
    return value


def gather_slots(value, axis, group, size):
    mask = group
    while mask < size:
        upper = (lax.axis_index(axis) & mask) != 0
        other = swap(value, axis, mask)
        value = jnp.where(
            upper, jnp.concatenate([other, value]), jnp.concatenate([value, other])
        )
        mask *= 2
    return value


def per_device(tokens, cotangent, router, logit_scale, expert_in, expert_out):
    f32, bf16 = jnp.float32, jnp.bfloat16
    tok_in = tokens[0]
    tok_cot = cotangent[0]
    experts = router.shape[1]
    width = router.shape[0]
    size = lax.axis_size("seq")
    group = size // experts
    phi_f32 = router.astype(f32)
    phi_scale = lax.rsqrt(jnp.sum(phi_f32 * phi_f32, axis=0, keepdims=True) + epsilon)
    phi_unit = phi_f32 * phi_scale
    phi_norm = phi_unit.astype(bf16)
    tok_f32 = tok_in.astype(f32)
    tok_scale = lax.rsqrt(jnp.sum(tok_f32 * tok_f32, axis=1, keepdims=True) + epsilon)
    tok_unit = tok_f32 * tok_scale
    tok_norm = tok_unit.astype(bf16)
    logits = logit_scale[0] * jnp.dot(tok_norm, phi_norm, preferred_element_type=f32)
    exp_scores = jnp.exp(logits)
    combine_f = exp_scores / jnp.sum(exp_scores, axis=1, keepdims=True)
    combine = combine_f.astype(bf16)
    exp_high = exp_scores.astype(bf16)
    exp_low = (exp_scores - exp_high.astype(f32)).astype(bf16)
    both = jnp.einsum(
        "ns,nd->sd",
        jnp.concatenate([exp_high, exp_low], axis=1),
        tok_in,
        preferred_element_type=f32,
    )
    in_part = both[:experts] + both[experts:]
    cot_part = jnp.einsum("ns,nd->sd", combine, tok_cot, preferred_element_type=f32)
    local_total = jnp.sum(exp_scores, axis=0)
    all_totals = jnp.broadcast_to(local_total[None, :], (experts, experts))
    packed = jnp.concatenate([in_part, cot_part, all_totals], axis=1)
    packed = scatter_slots(packed, "seq", group, size)
    packed = sum_over(packed, "seq", 1, group)
    owned = lax.axis_index("seq") // group
    totals = packed[:, 2 * width :]
    own_total = lax.dynamic_slice_in_dim(totals, owned, 1, 1)
    own_in = packed[:, :width] / own_total
    row_x = own_in.astype(bf16)
    row_cot = packed[:, width : 2 * width].astype(bf16)
    pre_act = jnp.dot(row_x, expert_in, preferred_element_type=f32)
    hidden = jax.nn.gelu(pre_act, approximate=False).astype(bf16)
    part_out = jnp.dot(hidden, expert_out, preferred_element_type=f32)
    hid_grad = jnp.einsum("od,hd->oh", row_cot, expert_out, preferred_element_type=f32)
    pre_grad = (hid_grad * gelu_slope(pre_act)).astype(bf16)
    part_dx = jnp.einsum("oh,dh->od", pre_grad, expert_in, preferred_element_type=f32)
    rows = jnp.concatenate([row_x, row_cot, hidden, pre_grad], axis=1)
    clips = lax.axis_size("dp")
    me = lax.axis_index("dp")
    all_rows = [rows] + [
        lax.ppermute(rows, "dp", [(i, (i + step) % clips) for i in range(clips)])
        for step in range(1, clips)
    ]
    all_rows = jnp.concatenate(all_rows, axis=0)
    units = expert_in.shape[1]
    all_x, all_cot = all_rows[:, :width], all_rows[:, width : 2 * width]
    all_hidden = all_rows[:, 2 * width : 2 * width + units]
    all_grad = all_rows[:, 2 * width + units :]
    share = width // clips
    mine_x = lax.dynamic_slice_in_dim(all_x, me * share, share, 1)
    mine_cot = lax.dynamic_slice_in_dim(all_cot, me * share, share, 1)
    grad_expert_in = jnp.einsum("od,oh->dh", mine_x, all_grad, preferred_element_type=f32)
    grad_expert_out = jnp.einsum("oh,od->hd", all_hidden, mine_cot, preferred_element_type=f32)
    sums = sum_over(jnp.concatenate([part_out, part_dx], axis=1), "seq", 1, group)
    stat = jnp.sum(own_in * sums[:, width:].astype(bf16).astype(f32), axis=1, keepdims=True)
    sums = gather_slots(
        jnp.concatenate([sums, stat], axis=1), "seq", group, size
    )
    slot_y = sums[:, :width].astype(bf16)
    slot_dx = sums[:, width : 2 * width].astype(bf16)
    column_stat = sums[:, 2 * width :].T
    mixed = jnp.dot(combine, slot_y, preferred_element_type=f32).astype(bf16)
    comb_dot = jnp.einsum("nd,sd->ns", tok_cot, slot_y, preferred_element_type=f32)
    grad_comb = combine_f * (comb_dot - jnp.sum(combine_f * comb_dot, axis=1, keepdims=True))
    dispatch_f = exp_scores / totals
    dispatch = dispatch_f.astype(bf16)
    disp_dot = jnp.einsum("nd,sd->ns", tok_in, slot_dx, preferred_element_type=f32)
    grad_disp = dispatch_f * (disp_dot - column_stat)
    score_grad = (logit_scale[0] * (grad_comb + grad_disp)).astype(bf16)
    norm_grad = jnp.einsum("ns,ds->nd", score_grad, phi_norm, preferred_element_type=f32)
    phi_part = jnp.einsum("nd,ns->sd", tok_norm, score_grad, preferred_element_type=f32)
    phi_grad = sum_over(phi_part, "dp", 1, clips)
    phi_grad = sum_over(phi_grad, "seq", 1, size).T
    through = jnp.dot(dispatch, slot_dx, preferred_element_type=f32)
    back_norm = tok_scale * (
        norm_grad - tok_unit * jnp.sum(tok_unit * norm_grad, axis=1, keepdims=True)
    )
    grad_tokens = (through + back_norm).astype(bf16)
    grad_router = phi_scale * (
        phi_grad - phi_unit * jnp.sum(phi_unit * phi_grad, axis=0, keepdims=True)
    )
    return (mixed[None], grad_tokens[None], grad_expert_in, grad_expert_out, grad_router)


def solution(mesh):
    return jax.shard_map(
        per_device,
        mesh=mesh,
        in_specs=(
            P("dp", "seq", None),
            P("dp", "seq", None),
            P(),
            P(),
            P(None, "seq"),
            P("seq", None),
        ),
        out_specs=(P("dp", "seq", None), P("dp", "seq", None), P("dp", "seq"), P("seq", "dp"), P()),
        check_vma=False,
    )
```

```python
import jax
import jax.numpy as jnp
from jax import lax
from jax.sharding import PartitionSpec as P

epsilon = 1e-06


def gelu_slope(pre_act):
    cdf = 0.5 * (1.0 + lax.erf(pre_act * 0.7071067811865476))
    return cdf + pre_act * jnp.exp(-0.5 * pre_act * pre_act) * 0.3989422804014327


LANES = 128


def packed_rows(parts, rows):
    flat = jnp.concatenate([part.reshape(part.shape[0], -1) for part in parts], axis=1)
    flat = jnp.pad(flat, ((0, 0), (0, rows * LANES - flat.shape[1])))
    return flat.reshape(flat.shape[0], rows, LANES)


def row_count(values):
    return -(-values // (8 * LANES)) * 8


def to_each(value, axis):
    return lax.all_to_all(value, axis, split_axis=0, concat_axis=0)


def per_device(tokens, cotangent, router, logit_scale, expert_in, expert_out):
    f32, bf16 = jnp.float32, jnp.bfloat16
    tok_in = tokens[0]
    tok_cot = cotangent[0]
    experts = router.shape[1]
    width = router.shape[0]
    size = lax.axis_size("seq")
    group = size // experts
    phi_f32 = router.astype(f32)
    phi_scale = lax.rsqrt(jnp.sum(phi_f32 * phi_f32, axis=0, keepdims=True) + epsilon)
    phi_unit = phi_f32 * phi_scale
    phi_norm = phi_unit.astype(bf16)
    tok_f32 = tok_in.astype(f32)
    tok_scale = lax.rsqrt(jnp.sum(tok_f32 * tok_f32, axis=1, keepdims=True) + epsilon)
    tok_unit = tok_f32 * tok_scale
    tok_norm = tok_unit.astype(bf16)
    logits = logit_scale[0] * jnp.dot(tok_norm, phi_norm, preferred_element_type=f32)
    exp_scores = jnp.exp(logits)
    combine_f = exp_scores / jnp.sum(exp_scores, axis=1, keepdims=True)
    combine = combine_f.astype(bf16)
    exp_high = exp_scores.astype(bf16)
    exp_low = (exp_scores - exp_high.astype(f32)).astype(bf16)
    both = jnp.einsum(
        "ns,nd->sd",
        jnp.concatenate([exp_high, exp_low], axis=1),
        tok_in,
        preferred_element_type=f32,
    )
    in_part = both[:experts] + both[experts:]
    cot_part = jnp.einsum("ns,nd->sd", combine, tok_cot, preferred_element_type=f32)
    local_total = jnp.sum(exp_scores, axis=0)
    all_totals = jnp.broadcast_to(local_total[None, :], (experts, experts))
    rows_a = row_count(2 * width + experts)
    packed = packed_rows([in_part, cot_part, all_totals], rows_a)
    packed = jnp.repeat(packed, group, axis=0)
    packed = jnp.sum(to_each(packed, "seq"), axis=0).reshape(1, -1)
    owned = lax.axis_index("seq") // group
    totals = packed[:, 2 * width : 2 * width + experts]
    own_total = lax.dynamic_slice_in_dim(totals, owned, 1, 1)
    own_in = packed[:, :width] / own_total
    row_x = own_in.astype(bf16)
    row_cot = packed[:, width : 2 * width].astype(bf16)
    pre_act = jnp.dot(row_x, expert_in, preferred_element_type=f32)
    hidden = jax.nn.gelu(pre_act, approximate=False).astype(bf16)
    part_out = jnp.dot(hidden, expert_out, preferred_element_type=f32)
    hid_grad = jnp.einsum("od,hd->oh", row_cot, expert_out, preferred_element_type=f32)
    pre_grad = (hid_grad * gelu_slope(pre_act)).astype(bf16)
    part_dx = jnp.einsum("oh,dh->od", pre_grad, expert_in, preferred_element_type=f32)
    rows = jnp.concatenate([row_x, row_cot, hidden, pre_grad], axis=1)
    clips = lax.axis_size("dp")
    me = lax.axis_index("dp")
    all_rows = [rows] + [
        lax.ppermute(rows, "dp", [(i, (i + step) % clips) for i in range(clips)])
        for step in range(1, clips)
    ]
    all_rows = jnp.concatenate(all_rows, axis=0)
    units = expert_in.shape[1]
    all_x, all_cot = all_rows[:, :width], all_rows[:, width : 2 * width]
    all_hidden = all_rows[:, 2 * width : 2 * width + units]
    all_grad = all_rows[:, 2 * width + units :]
    share = width // clips
    mine_x = lax.dynamic_slice_in_dim(all_x, me * share, share, 1)
    mine_cot = lax.dynamic_slice_in_dim(all_cot, me * share, share, 1)
    grad_expert_in = jnp.einsum("od,oh->dh", mine_x, all_grad, preferred_element_type=f32)
    grad_expert_out = jnp.einsum("oh,od->hd", all_hidden, mine_cot, preferred_element_type=f32)
    dot_part = jnp.sum(own_in * part_dx, axis=1, keepdims=True)
    rows_b = row_count(2 * width + 1)
    sums = packed_rows([part_out, part_dx, dot_part], rows_b)
    sums = to_each(jnp.broadcast_to(sums, (size,) + sums.shape[1:]), "seq")
    sums = jnp.sum(sums.reshape(experts, group, rows_b * LANES), axis=1)
    slot_y = sums[:, :width].astype(bf16)
    slot_dx = sums[:, width : 2 * width].astype(bf16)
    column_stat = sums[:, 2 * width : 2 * width + 1].T
    mixed = jnp.dot(combine, slot_y, preferred_element_type=f32).astype(bf16)
    comb_dot = jnp.einsum("nd,sd->ns", tok_cot, slot_y, preferred_element_type=f32)
    grad_comb = combine_f * (comb_dot - jnp.sum(combine_f * comb_dot, axis=1, keepdims=True))
    dispatch_f = exp_scores / totals
    dispatch = dispatch_f.astype(bf16)
    disp_dot = jnp.einsum("nd,sd->ns", tok_in, slot_dx, preferred_element_type=f32)
    grad_disp = dispatch_f * (disp_dot - column_stat)
    score_grad = (logit_scale[0] * (grad_comb + grad_disp)).astype(bf16)
    norm_grad = jnp.einsum("ns,ds->nd", score_grad, phi_norm, preferred_element_type=f32)
    phi_part = jnp.einsum("nd,ns->sd", tok_norm, score_grad, preferred_element_type=f32)
    devices = size * clips
    share_d = -(-experts * width // (devices * LANES)) * LANES
    phi_flat = jnp.pad(phi_part.reshape(-1), (0, devices * share_d - experts * width))
    both_axes = ("seq", "dp")
    phi_sum = jnp.sum(to_each(phi_flat.reshape(devices, 1, share_d), both_axes), axis=0)
    phi_all = to_each(jnp.broadcast_to(phi_sum, (devices, 1, share_d)), both_axes)
    phi_grad = phi_all.reshape(-1)[: experts * width].reshape(experts, width).T
    through = jnp.dot(dispatch, slot_dx, preferred_element_type=f32)
    back_norm = tok_scale * (
        norm_grad - tok_unit * jnp.sum(tok_unit * norm_grad, axis=1, keepdims=True)
    )
    grad_tokens = (through + back_norm).astype(bf16)
    grad_router = phi_scale * (
        phi_grad - phi_unit * jnp.sum(phi_unit * phi_grad, axis=0, keepdims=True)
    )
    return (mixed[None], grad_tokens[None], grad_expert_in, grad_expert_out, grad_router)


def solution(mesh):
    return jax.shard_map(
        per_device,
        mesh=mesh,
        in_specs=(
            P("dp", "seq", None),
            P("dp", "seq", None),
            P(),
            P(),
            P(None, "seq"),
            P("seq", None),
        ),
        out_specs=(P("dp", "seq", None), P("dp", "seq", None), P("dp", "seq"), P("seq", "dp"), P()),
        check_vma=False,
    )
```

```python
import jax
import jax.numpy as jnp
from jax import lax
from jax.sharding import PartitionSpec as P

epsilon = 1e-06


def gelu_slope(pre_act):
    cdf = 0.5 * (1.0 + lax.erf(pre_act * 0.7071067811865476))
    return cdf + pre_act * jnp.exp(-0.5 * pre_act * pre_act) * 0.3989422804014327


LANES = 128


def packed_rows(parts, rows):
    flat = jnp.concatenate([part.reshape(part.shape[0], -1) for part in parts], axis=1)
    flat = jnp.pad(flat, ((0, 0), (0, rows * LANES - flat.shape[1])))
    return flat.reshape(flat.shape[0], rows, LANES)


def row_count(values):
    return -(-values // (8 * LANES)) * 8


def to_each(value, axis):
    return lax.all_to_all(value, axis, split_axis=0, concat_axis=0)


def per_device(tokens, cotangent, router, logit_scale, expert_in, expert_out):
    f32, bf16 = jnp.float32, jnp.bfloat16
    tok_in = tokens[0]
    tok_cot = cotangent[0]
    experts = router.shape[1]
    width = router.shape[0]
    size = lax.axis_size("seq")
    group = size // experts
    phi_f32 = router.astype(f32)
    phi_scale = lax.rsqrt(jnp.sum(phi_f32 * phi_f32, axis=0, keepdims=True) + epsilon)
    phi_unit = phi_f32 * phi_scale
    phi_norm = phi_unit.astype(bf16)
    tok_f32 = tok_in.astype(f32)
    tok_scale = lax.rsqrt(jnp.sum(tok_f32 * tok_f32, axis=1, keepdims=True) + epsilon)
    tok_unit = tok_f32 * tok_scale
    tok_norm = tok_unit.astype(bf16)
    logits = logit_scale[0] * jnp.dot(tok_norm, phi_norm, preferred_element_type=f32)
    exp_scores = jnp.exp(logits)
    combine_f = exp_scores / jnp.sum(exp_scores, axis=1, keepdims=True)
    combine = combine_f.astype(bf16)
    exp_high = exp_scores.astype(bf16)
    exp_low = (exp_scores - exp_high.astype(f32)).astype(bf16)
    both = jnp.einsum(
        "ns,nd->sd",
        jnp.concatenate([exp_high, exp_low], axis=1),
        tok_in,
        preferred_element_type=f32,
    )
    in_part = both[:experts] + both[experts:]
    cot_part = jnp.einsum("ns,nd->sd", combine, tok_cot, preferred_element_type=f32)
    local_total = jnp.sum(exp_scores, axis=0)
    total_high = local_total.astype(bf16)
    total_low = (local_total - total_high.astype(f32)).astype(bf16)
    all_totals = jnp.tile(jnp.concatenate([total_high, total_low])[None, :], (experts, 1))
    rows_a = row_count(2 * width + 2 * experts)
    packed = packed_rows([in_part.astype(bf16), cot_part.astype(bf16), all_totals], rows_a)
    packed = jnp.repeat(packed, group, axis=0)
    packed = jnp.sum(to_each(packed, "seq").astype(f32), axis=0).reshape(1, -1)
    owned = lax.axis_index("seq") // group
    totals = packed[:, 2 * width : 2 * width + experts]
    totals = totals + packed[:, 2 * width + experts : 2 * width + 2 * experts]
    own_total = lax.dynamic_slice_in_dim(totals, owned, 1, 1)
    own_in = packed[:, :width] / own_total
    row_x = own_in.astype(bf16)
    row_cot = packed[:, width : 2 * width].astype(bf16)
    pre_act = jnp.dot(row_x, expert_in, preferred_element_type=f32)
    hidden = jax.nn.gelu(pre_act, approximate=False).astype(bf16)
    part_out = jnp.dot(hidden, expert_out, preferred_element_type=f32)
    hid_grad = jnp.einsum("od,hd->oh", row_cot, expert_out, preferred_element_type=f32)
    pre_grad = (hid_grad * gelu_slope(pre_act)).astype(bf16)
    part_dx = jnp.einsum("oh,dh->od", pre_grad, expert_in, preferred_element_type=f32)
    rows = jnp.concatenate([row_x, row_cot, hidden, pre_grad], axis=1)
    clips = lax.axis_size("dp")
    me = lax.axis_index("dp")
    all_rows = [rows] + [
        lax.ppermute(rows, "dp", [(i, (i + step) % clips) for i in range(clips)])
        for step in range(1, clips)
    ]
    all_rows = jnp.concatenate(all_rows, axis=0)
    units = expert_in.shape[1]
    all_x, all_cot = all_rows[:, :width], all_rows[:, width : 2 * width]
    all_hidden = all_rows[:, 2 * width : 2 * width + units]
    all_grad = all_rows[:, 2 * width + units :]
    share = width // clips
    mine_x = lax.dynamic_slice_in_dim(all_x, me * share, share, 1)
    mine_cot = lax.dynamic_slice_in_dim(all_cot, me * share, share, 1)
    grad_expert_in = jnp.einsum("od,oh->dh", mine_x, all_grad, preferred_element_type=f32)
    grad_expert_out = jnp.einsum("oh,od->hd", all_hidden, mine_cot, preferred_element_type=f32)
    dot_part = jnp.sum(own_in * part_dx, axis=1, keepdims=True)
    rows_b = row_count(2 * width + 1)
    sums = packed_rows([part_out, part_dx, dot_part], rows_b).astype(bf16)
    sums = to_each(jnp.broadcast_to(sums, (size,) + sums.shape[1:]), "seq")
    sums = jnp.sum(sums.reshape(experts, group, rows_b * LANES).astype(f32), axis=1)
    slot_y = sums[:, :width].astype(bf16)
    slot_dx = sums[:, width : 2 * width].astype(bf16)
    column_stat = sums[:, 2 * width : 2 * width + 1].T
    mixed = jnp.dot(combine, slot_y, preferred_element_type=f32).astype(bf16)
    comb_dot = jnp.einsum("nd,sd->ns", tok_cot, slot_y, preferred_element_type=f32)
    grad_comb = combine_f * (comb_dot - jnp.sum(combine_f * comb_dot, axis=1, keepdims=True))
    dispatch_f = exp_scores / totals
    dispatch = dispatch_f.astype(bf16)
    disp_dot = jnp.einsum("nd,sd->ns", tok_in, slot_dx, preferred_element_type=f32)
    grad_disp = dispatch_f * (disp_dot - column_stat)
    score_grad = (logit_scale[0] * (grad_comb + grad_disp)).astype(bf16)
    norm_grad = jnp.einsum("ns,ds->nd", score_grad, phi_norm, preferred_element_type=f32)
    phi_part = jnp.einsum("nd,ns->sd", tok_norm, score_grad, preferred_element_type=f32)
    phi_rows = phi_part.reshape(1, -1, LANES)
    for step in range(1, clips):
        phi_rows = phi_rows + lax.ppermute(
            phi_part.reshape(1, -1, LANES), "dp", [(i, (i + step) % clips) for i in range(clips)]
        )
    stride = 1
    while stride < size:
        radix = min(4, size // stride)
        groups = [
            [base + low + stride * i for i in range(radix)]
            for base in range(0, size, stride * radix)
            for low in range(stride)
        ]
        spread = jnp.broadcast_to(phi_rows, (radix,) + phi_rows.shape[1:])
        spread = lax.all_to_all(
            spread, "seq", split_axis=0, concat_axis=0, axis_index_groups=groups
        )
        phi_rows = jnp.sum(spread, axis=0, keepdims=True)
        stride *= radix
    phi_grad = phi_rows.reshape(experts, width).T
    through = jnp.dot(dispatch, slot_dx, preferred_element_type=f32)
    back_norm = tok_scale * (
        norm_grad - tok_unit * jnp.sum(tok_unit * norm_grad, axis=1, keepdims=True)
    )
    grad_tokens = (through + back_norm).astype(bf16)
    grad_router = phi_scale * (
        phi_grad - phi_unit * jnp.sum(phi_unit * phi_grad, axis=0, keepdims=True)
    )
    return (mixed[None], grad_tokens[None], grad_expert_in, grad_expert_out, grad_router)


def solution(mesh):
    return jax.shard_map(
        per_device,
        mesh=mesh,
        in_specs=(
            P("dp", "seq", None),
            P("dp", "seq", None),
            P(),
            P(),
            P(None, "seq"),
            P("seq", None),
        ),
        out_specs=(P("dp", "seq", None), P("dp", "seq", None), P("dp", "seq"), P("seq", "dp"), P()),
        check_vma=False,
    )
```

```python
import jax
import jax.numpy as jnp
from jax import lax
from jax.sharding import PartitionSpec as P

epsilon = 1e-06


def gelu_slope(pre_act):
    cdf = 0.5 * (1.0 + lax.erf(pre_act * 0.7071067811865476))
    return cdf + pre_act * jnp.exp(-0.5 * pre_act * pre_act) * 0.3989422804014327


LANES = 128
AXES = ("seq", "dp")


def send(value, pairs):
    return lax.ppermute(value, AXES, pairs)


def total_of(terms):
    terms = list(terms)
    while len(terms) > 1:
        pairs = [terms[i] + terms[i + 1] for i in range(0, len(terms) - 1, 2)]
        terms = pairs + terms[len(terms) - len(terms) % 2 :]
    return terms[0]


def in_parts(value):
    parts = []
    for _ in range(3):
        high = lax.reduce_precision(value, 8, 7)
        parts.append(high.astype(jnp.bfloat16))
        value = value - high
    return parts


def root_member(clip, slot, group):
    return (group // 2 * ((slot + 1) % 2) + 3 * (clip % 2)) % group


def flat(seq, clip, clips):
    return seq * clips + clip


def gather_pairs(size, clips, group, across, step):
    pairs = []
    for clip in range(clips):
        for slot in range(size // group):
            root = root_member(clip, slot, group)
            source = (slot ^ across) * group + (root ^ step)
            pairs.append((flat(source, clip, clips), flat(slot * group + root, clip, clips)))
    return pairs


def turned(pairs):
    return [(there, here) for here, there in pairs]


def per_device(tokens, cotangent, router, logit_scale, expert_in, expert_out):
    f32, bf16 = jnp.float32, jnp.bfloat16
    tok_in = tokens[0]
    tok_cot = cotangent[0]
    experts = router.shape[1]
    width = router.shape[0]
    size = lax.axis_size("seq")
    group = size // experts
    phi_f32 = router.astype(f32)
    phi_scale = lax.rsqrt(jnp.sum(phi_f32 * phi_f32, axis=0, keepdims=True) + epsilon)
    phi_unit = phi_f32 * phi_scale
    phi_norm = phi_unit.astype(bf16)
    tok_f32 = tok_in.astype(f32)
    tok_scale = lax.rsqrt(jnp.sum(tok_f32 * tok_f32, axis=1, keepdims=True) + epsilon)
    tok_unit = tok_f32 * tok_scale
    tok_norm = tok_unit.astype(bf16)
    logits = logit_scale[0] * jnp.dot(tok_norm, phi_norm, preferred_element_type=f32)
    exp_scores = jnp.exp(logits)
    combine_f = exp_scores / jnp.sum(exp_scores, axis=1, keepdims=True)
    combine = combine_f.astype(bf16)
    exp_high = lax.reduce_precision(exp_scores, 8, 7)
    exp_low = (exp_scores - exp_high).astype(bf16)
    exp_high = exp_high.astype(bf16)
    both = jnp.einsum(
        "ns,nd->sd",
        jnp.concatenate([exp_high, exp_low], axis=1),
        tok_in,
        preferred_element_type=f32,
    )
    in_part = both[:experts] + both[experts:]
    cot_part = jnp.einsum("ns,nd->sd", combine, tok_cot, preferred_element_type=f32)
    local_total = jnp.sum(exp_scores, axis=0)
    clips = lax.axis_size("dp")
    clip = lax.axis_index("dp")
    place = lax.axis_index("seq")
    owned = place // group
    roots = jnp.array(
        [[slot * group + root_member(c, slot, group) for slot in range(experts)] for c in range(clips)]
    )
    is_root = jnp.any(roots[clip] == place)
    messages = jnp.concatenate(
        [in_part, cot_part, jnp.pad(local_total[:, None], ((0, 0), (0, LANES - 1)))], axis=1
    )

    def part_for(slot):
        return lax.dynamic_slice_in_dim(messages, slot, 1, 0)

    def steps(across):
        return [step for step in range(group - 1, -1, -1) if across or step]

    arrived = [part_for(owned)]
    for across in range(experts):
        message = part_for(owned ^ across)
        for step in steps(across):
            arrived.append(send(message, gather_pairs(size, clips, group, across, step)))
    arrived = total_of(arrived)
    root_total = arrived[:, 2 * width : 2 * width + 1]
    root_in = arrived[:, :width] / root_total
    root_rows = jnp.concatenate([root_in, arrived[:, width : 2 * width]], axis=1).astype(bf16)
    own_rows = jnp.where(is_root, root_rows, jnp.zeros_like(root_rows))
    for step in steps(0):
        own_rows = own_rows + send(root_rows, turned(gather_pairs(size, clips, group, 0, step)))
    row_x = own_rows[:, :width]
    row_cot = own_rows[:, width:]
    pre_act = jnp.dot(row_x, expert_in, preferred_element_type=f32)
    hidden = jax.nn.gelu(pre_act, approximate=False).astype(bf16)
    part_out = jnp.dot(hidden, expert_out, preferred_element_type=f32)
    hid_grad = jnp.einsum("od,hd->oh", row_cot, expert_out, preferred_element_type=f32)
    pre_grad = (hid_grad * gelu_slope(pre_act)).astype(bf16)
    part_dx = jnp.einsum("oh,dh->od", pre_grad, expert_in, preferred_element_type=f32)
    message = jnp.concatenate([part_out, part_dx], axis=1)
    arrived = [message]
    for step in steps(0):
        arrived.append(send(message, gather_pairs(size, clips, group, 0, step)))
    arrived = total_of(arrived)
    root_rows = arrived.astype(bf16)
    root_stat = jnp.sum(
        root_in * root_rows[:, width:].astype(f32), axis=1, keepdims=True
    )
    extra = jnp.concatenate(in_parts(root_stat) + in_parts(root_total), axis=1)
    extra = jnp.pad(extra, ((0, 0), (0, LANES - extra.shape[1])))
    root_rows = jnp.concatenate([root_rows, extra], axis=1)
    by_slot = []
    for across in range(experts):
        got = [send(root_rows, turned(gather_pairs(size, clips, group, across, step))) for step in steps(across)]
        if not across:
            got.append(jnp.where(is_root, root_rows, jnp.zeros_like(root_rows)))
        by_slot.append(total_of(got))
    by_slot = jnp.concatenate(by_slot, axis=0)
    by_slot = jnp.concatenate(
        [lax.dynamic_slice_in_dim(by_slot, owned ^ slot, 1, 0) for slot in range(experts)], axis=0
    )
    slot_y = by_slot[:, :width]
    slot_dx = by_slot[:, width : 2 * width]
    extra = by_slot[:, 2 * width :].astype(f32)
    column_stat = (extra[:, 0:1] + extra[:, 1:2] + extra[:, 2:3]).T
    totals = (extra[:, 3:4] + extra[:, 4:5] + extra[:, 5:6]).T
    rows = jnp.concatenate([row_x, row_cot, hidden, pre_grad], axis=1)
    rows, slot_y, slot_dx = lax.optimization_barrier((rows, slot_y, slot_dx))
    all_rows = [rows] + [
        lax.ppermute(rows, "dp", [(i, (i + step) % clips) for i in range(clips)])
        for step in range(1, clips)
    ]
    all_rows = jnp.concatenate(all_rows, axis=0)
    units = expert_in.shape[1]
    all_x, all_cot = all_rows[:, :width], all_rows[:, width : 2 * width]
    all_hidden = all_rows[:, 2 * width : 2 * width + units]
    all_grad = all_rows[:, 2 * width + units :]
    share = width // clips
    mine_x = lax.dynamic_slice_in_dim(all_x, clip * share, share, 1)
    mine_cot = lax.dynamic_slice_in_dim(all_cot, clip * share, share, 1)
    grad_expert_in = jnp.einsum("od,oh->dh", mine_x, all_grad, preferred_element_type=f32)
    grad_expert_out = jnp.einsum("oh,od->hd", all_hidden, mine_cot, preferred_element_type=f32)
    mixed = jnp.dot(combine, slot_y, preferred_element_type=f32).astype(bf16)
    comb_dot = jnp.einsum("nd,sd->ns", tok_cot, slot_y, preferred_element_type=f32)
    grad_comb = combine_f * (comb_dot - jnp.sum(combine_f * comb_dot, axis=1, keepdims=True))
    dispatch_f = exp_scores / totals
    dispatch = dispatch_f.astype(bf16)
    disp_dot = jnp.einsum("nd,sd->ns", tok_in, slot_dx, preferred_element_type=f32)
    grad_disp = dispatch_f * (disp_dot - column_stat)
    score_grad = (logit_scale[0] * (grad_comb + grad_disp)).astype(bf16)
    norm_grad = jnp.einsum("ns,ds->nd", score_grad, phi_norm, preferred_element_type=f32)
    phi_part = jnp.einsum("nd,ns->sd", tok_norm, score_grad, preferred_element_type=f32)
    last = clips - 1
    phi_flat = phi_part.reshape(1, -1)
    hops = [[(flat(p, c, clips), flat(p, last, clips)) for p in range(size)] for c in range(last)]
    phi_flat = total_of([phi_flat] + [send(phi_flat, hop) for hop in hops])
    top = (experts - 1) // 2 * group + root_member(last, (experts - 1) // 2, group)
    lines = [[(flat(top ^ step, last, clips), flat(top, last, clips))] for step in range(1, size)]
    phi_flat = total_of([phi_flat] + [send(phi_flat, line) for line in lines])
    phi_back = total_of(
        [jnp.where(place == top, phi_flat, jnp.zeros_like(phi_flat))]
        + [send(phi_flat, turned(line)) for line in lines]
    )
    phi_back = total_of(
        [jnp.where(clip == last, phi_back, jnp.zeros_like(phi_back))]
        + [send(phi_back, turned(hop)) for hop in hops]
    )
    phi_grad = phi_back.reshape(experts, width).T
    through = jnp.dot(dispatch, slot_dx, preferred_element_type=f32)
    back_norm = tok_scale * (
        norm_grad - tok_unit * jnp.sum(tok_unit * norm_grad, axis=1, keepdims=True)
    )
    grad_tokens = (through + back_norm).astype(bf16)
    grad_router = phi_scale * (
        phi_grad - phi_unit * jnp.sum(phi_unit * phi_grad, axis=0, keepdims=True)
    )
    return (mixed[None], grad_tokens[None], grad_expert_in, grad_expert_out, grad_router)


def solution(mesh):
    return jax.shard_map(
        per_device,
        mesh=mesh,
        in_specs=(
            P("dp", "seq", None),
            P("dp", "seq", None),
            P(),
            P(),
            P(None, "seq"),
            P("seq", None),
        ),
        out_specs=(P("dp", "seq", None), P("dp", "seq", None), P("dp", "seq"), P("seq", "dp"), P()),
        check_vma=False,
    )
```

```python
import jax
import jax.numpy as jnp
from jax import lax
from jax.sharding import PartitionSpec as P

epsilon = 1e-06
AXES = ("seq", "dp")


def gelu_slope(pre_act):
    cdf = 0.5 * (1.0 + lax.erf(pre_act * 0.7071067811865476))
    return cdf + pre_act * jnp.exp(-0.5 * pre_act * pre_act) * 0.3989422804014327


def exchange(value, mask):
    clips = lax.axis_size("dp")
    pairs = []
    for place in range(lax.axis_size("seq")):
        for clip in range(clips):
            there = place ^ mask if clip == clips - 1 else place
            pairs.append((place * clips + clip, there * clips + clip))
    return lax.ppermute(value, AXES, pairs)


def hop(value, step):
    return lax.ppermute(value, "dp", [(i, i ^ step) for i in range(lax.axis_size("dp"))])


def of_clips(value):
    clips = lax.axis_size("dp")
    clip = lax.axis_index("dp")
    got = [value] + [hop(value, step) for step in range(1, clips)]
    ordered = []
    for index in range(clips):
        picked = got[0]
        for step in range(1, clips):
            picked = jnp.where(clip ^ step == index, got[step], picked)
        ordered.append(picked)
    return ordered


def rounds(size):
    masks = [1 << bit for bit in range(size.bit_length() - 1)]
    return [masks[i : i + 2] for i in range(0, len(masks), 2)]


def round_masks(pair):
    return pair if len(pair) == 1 else [pair[0], pair[1], pair[0] | pair[1]]


def sum_to_owner(value, group):
    place = lax.axis_index("seq")
    for pair in reversed(rounds(lax.axis_size("seq"))):
        owner_masks = [mask for mask in pair if mask >= group]
        blocks = value.reshape((1 << len(owner_masks), -1) + value.shape[1:])

        def block_for(mask):
            index = 0
            for bit, owner_mask in enumerate(owner_masks):
                index = index + jnp.where((place ^ mask) & owner_mask != 0, 1 << bit, 0)
            return lax.dynamic_index_in_dim(blocks, index, 0, keepdims=False)

        got = [block_for(0)] + [exchange(block_for(mask), mask) for mask in round_masks(pair)]
        value = got[0] + got[1] if len(got) == 2 else (got[0] + got[1]) + (got[2] + got[3])
    return value


def sum_to_all(value, group):
    place = lax.axis_index("seq")
    for pair in rounds(lax.axis_size("seq")):
        terms = {0: value}
        for mask in round_masks(pair):
            terms[mask] = exchange(value, mask)
        for mask in pair:
            upper = (place & mask) != 0
            merged = {}
            for key in terms:
                if key & mask:
                    continue
                near, far = terms[key], terms[key | mask]
                if mask < group:
                    merged[key] = near + far
                else:
                    merged[key] = jnp.where(
                        upper, jnp.concatenate([far, near]), jnp.concatenate([near, far])
                    )
            terms = merged
        value = terms[0]
    return value


def per_device(tokens, cotangent, router, logit_scale, expert_in, expert_out):
    f32, bf16 = jnp.float32, jnp.bfloat16
    tok_in = tokens[0]
    tok_cot = cotangent[0]
    experts = router.shape[1]
    width = router.shape[0]
    size = lax.axis_size("seq")
    group = size // experts
    clips = lax.axis_size("dp")
    clip = lax.axis_index("dp")
    owned = lax.axis_index("seq") // group
    phi_f32 = router.astype(f32)
    phi_scale = lax.rsqrt(jnp.sum(phi_f32 * phi_f32, axis=0, keepdims=True) + epsilon)
    phi_unit = phi_f32 * phi_scale
    phi_norm = phi_unit.astype(bf16)
    tok_f32 = tok_in.astype(f32)
    tok_scale = lax.rsqrt(jnp.sum(tok_f32 * tok_f32, axis=1, keepdims=True) + epsilon)
    tok_unit = tok_f32 * tok_scale
    tok_norm = tok_unit.astype(bf16)
    logits = logit_scale[0] * jnp.dot(tok_norm, phi_norm, preferred_element_type=f32)
    exp_scores = jnp.exp(logits)
    combine_f = exp_scores / jnp.sum(exp_scores, axis=1, keepdims=True)
    combine = combine_f.astype(bf16)
    exp_high = lax.reduce_precision(exp_scores, 8, 7)
    exp_low = (exp_scores - exp_high).astype(bf16)
    exp_high = exp_high.astype(bf16)
    both = jnp.einsum(
        "ns,nd->sd",
        jnp.concatenate([exp_high, exp_low], axis=1),
        tok_in,
        preferred_element_type=f32,
    )
    in_part = both[:experts] + both[experts:]
    cot_part = jnp.einsum("ns,nd->sd", combine, tok_cot, preferred_element_type=f32)
    local_total = jnp.sum(exp_scores, axis=0)
    all_totals = jnp.broadcast_to(local_total[None, :], (experts, experts))
    message = jnp.stack(
        of_clips(jnp.concatenate([in_part, cot_part, all_totals], axis=1)), axis=1
    )
    message = sum_to_owner(message, group)[0]
    totals = message[:, 2 * width :]
    own_total = lax.dynamic_slice_in_dim(totals, owned, 1, 1)
    own_in = message[:, :width] / own_total
    row_x = own_in.astype(bf16)
    row_cot = message[:, width : 2 * width].astype(bf16)
    pre_act = jnp.dot(row_x, expert_in, preferred_element_type=f32)
    hidden = jax.nn.gelu(pre_act, approximate=False).astype(bf16)
    part_out = jnp.dot(hidden, expert_out, preferred_element_type=f32)
    hid_grad = jnp.einsum("od,hd->oh", row_cot, expert_out, preferred_element_type=f32)
    pre_grad = (hid_grad * gelu_slope(pre_act)).astype(bf16)
    part_dx = jnp.einsum("oh,dh->od", pre_grad, expert_in, preferred_element_type=f32)
    dot_part = jnp.sum(own_in * part_dx, axis=1, keepdims=True)
    message = jnp.concatenate([part_out, part_dx, dot_part], axis=1)[None]
    message = sum_to_all(message, group)
    whole_totals = jnp.broadcast_to(totals.T[:, :, None], (experts, clips, 1))
    message = jnp.concatenate([message, whole_totals], axis=2)
    handed = message[:, clips - 1]
    for step in range(1, clips):
        got = hop(message[:, (clips - 1) ^ step], step)
        handed = jnp.where(clip ^ step == clips - 1, got, handed)
    slot_y = handed[:, :width].astype(bf16)
    slot_dx = handed[:, width : 2 * width].astype(bf16)
    column_stat = handed[:, 2 * width : 2 * width + 1].T
    totals = handed[:, 2 * width + 1 :].T
    rows = jnp.concatenate([row_x, row_cot, hidden, pre_grad], axis=1)
    rows, slot_y, slot_dx = lax.optimization_barrier((rows, slot_y, slot_dx))
    all_rows = of_clips(rows)[clips - 1]
    units = expert_in.shape[1]
    all_x, all_cot = all_rows[:, :width], all_rows[:, width : 2 * width]
    all_hidden = all_rows[:, 2 * width : 2 * width + units]
    all_grad = all_rows[:, 2 * width + units :]
    share = width // clips
    mine_x = lax.dynamic_slice_in_dim(all_x, clip * share, share, 1)
    mine_cot = lax.dynamic_slice_in_dim(all_cot, clip * share, share, 1)
    grad_expert_in = jnp.einsum("od,oh->dh", mine_x, all_grad, preferred_element_type=f32)
    grad_expert_out = jnp.einsum("oh,od->hd", all_hidden, mine_cot, preferred_element_type=f32)
    mixed = jnp.dot(combine, slot_y, preferred_element_type=f32).astype(bf16)
    comb_dot = jnp.einsum("nd,sd->ns", tok_cot, slot_y, preferred_element_type=f32)
    grad_comb = combine_f * (comb_dot - jnp.sum(combine_f * comb_dot, axis=1, keepdims=True))
    dispatch_f = exp_scores / totals
    dispatch = dispatch_f.astype(bf16)
    disp_dot = jnp.einsum("nd,sd->ns", tok_in, slot_dx, preferred_element_type=f32)
    grad_disp = dispatch_f * (disp_dot - column_stat)
    score_grad = (logit_scale[0] * (grad_comb + grad_disp)).astype(bf16)
    norm_grad = jnp.einsum("ns,ds->nd", score_grad, phi_norm, preferred_element_type=f32)
    phi_part = jnp.einsum("nd,ns->sd", tok_norm, score_grad, preferred_element_type=f32)
    phi_flat = sum(of_clips(phi_part.reshape(1, 1, -1)))
    phi_flat = sum_to_all(phi_flat, size)
    phi_grad = of_clips(phi_flat)[clips - 1].reshape(experts, width).T
    through = jnp.dot(dispatch, slot_dx, preferred_element_type=f32)
    back_norm = tok_scale * (
        norm_grad - tok_unit * jnp.sum(tok_unit * norm_grad, axis=1, keepdims=True)
    )
    grad_tokens = (through + back_norm).astype(bf16)
    grad_router = phi_scale * (
        phi_grad - phi_unit * jnp.sum(phi_unit * phi_grad, axis=0, keepdims=True)
    )
    return (mixed[None], grad_tokens[None], grad_expert_in, grad_expert_out, grad_router)


def solution(mesh):
    return jax.shard_map(
        per_device,
        mesh=mesh,
        in_specs=(
            P("dp", "seq", None),
            P("dp", "seq", None),
            P(),
            P(),
            P(None, "seq"),
            P("seq", None),
        ),
        out_specs=(P("dp", "seq", None), P("dp", "seq", None), P("dp", "seq"), P("seq", "dp"), P()),
        check_vma=False,
    )
```

```python
import jax
import jax.numpy as jnp
from jax import lax
from jax.sharding import PartitionSpec as P

epsilon = 1e-06
AXES = ("seq", "dp")


def gelu_slope(pre_act):
    cdf = 0.5 * (1.0 + lax.erf(pre_act * 0.7071067811865476))
    return cdf + pre_act * jnp.exp(-0.5 * pre_act * pre_act) * 0.3989422804014327


def exchange(value, mask):
    clips = lax.axis_size("dp")
    pairs = []
    for place in range(lax.axis_size("seq")):
        for clip in range(clips):
            there = (place ^ mask) * clips + (clip ^ 1 if clips % 2 == 0 else clip)
            pairs.append((place * clips + clip, there))
    return lax.ppermute(value, AXES, pairs)


def hop(value, step):
    return lax.ppermute(value, "dp", [(i, i ^ step) for i in range(lax.axis_size("dp"))])


def of_clips(value):
    clips = lax.axis_size("dp")
    clip = lax.axis_index("dp")
    got = [value] + [hop(value, step) for step in range(1, clips)]
    ordered = []
    for index in range(clips):
        picked = got[0]
        for step in range(1, clips):
            picked = jnp.where(clip ^ step == index, got[step], picked)
        ordered.append(picked)
    return ordered


def rounds(size):
    masks = [1 << bit for bit in range(size.bit_length() - 1)]
    return [masks[i : i + 2] for i in range(0, len(masks), 2)]


def round_masks(pair):
    return pair if len(pair) == 1 else [pair[0], pair[1], pair[0] | pair[1]]


def sum_to_owner(value, group):
    place = lax.axis_index("seq")
    for pair in reversed(rounds(lax.axis_size("seq"))):
        owner_masks = [mask for mask in pair if mask >= group]
        blocks = value.reshape((1 << len(owner_masks), -1) + value.shape[1:])

        def block_for(mask):
            index = 0
            for bit, owner_mask in enumerate(owner_masks):
                index = index + jnp.where((place ^ mask) & owner_mask != 0, 1 << bit, 0)
            return lax.dynamic_index_in_dim(blocks, index, 0, keepdims=False)

        got = [block_for(0)] + [exchange(block_for(mask), mask) for mask in round_masks(pair)]
        value = got[0] + got[1] if len(got) == 2 else (got[0] + got[1]) + (got[2] + got[3])
    return value


def sum_to_all(value, group):
    place = lax.axis_index("seq")
    for pair in rounds(lax.axis_size("seq")):
        terms = {0: value}
        for mask in round_masks(pair):
            terms[mask] = exchange(value, mask)
        for mask in pair:
            upper = (place & mask) != 0
            merged = {}
            for key in terms:
                if key & mask:
                    continue
                near, far = terms[key], terms[key | mask]
                if mask < group:
                    merged[key] = near + far
                else:
                    merged[key] = jnp.where(
                        upper, jnp.concatenate([far, near]), jnp.concatenate([near, far])
                    )
            terms = merged
        value = terms[0]
    return value


def per_device(tokens, cotangent, router, logit_scale, expert_in, expert_out):
    f32, bf16 = jnp.float32, jnp.bfloat16
    tok_in = tokens[0]
    tok_cot = cotangent[0]
    experts = router.shape[1]
    width = router.shape[0]
    size = lax.axis_size("seq")
    group = size // experts
    clips = lax.axis_size("dp")
    clip = lax.axis_index("dp")
    owned = lax.axis_index("seq") // group
    phi_f32 = router.astype(f32)
    phi_scale = lax.rsqrt(jnp.sum(phi_f32 * phi_f32, axis=0, keepdims=True) + epsilon)
    phi_unit = phi_f32 * phi_scale
    phi_norm = phi_unit.astype(bf16)
    tok_f32 = tok_in.astype(f32)
    tok_scale = lax.rsqrt(jnp.sum(tok_f32 * tok_f32, axis=1, keepdims=True) + epsilon)
    tok_unit = tok_f32 * tok_scale
    tok_norm = tok_unit.astype(bf16)
    logits = logit_scale[0] * jnp.dot(tok_norm, phi_norm, preferred_element_type=f32)
    exp_scores = jnp.exp(logits)
    combine_f = exp_scores / jnp.sum(exp_scores, axis=1, keepdims=True)
    combine = combine_f.astype(bf16)
    exp_high = lax.reduce_precision(exp_scores, 8, 7)
    exp_low = (exp_scores - exp_high).astype(bf16)
    exp_high = exp_high.astype(bf16)
    both = jnp.einsum(
        "ns,nd->sd",
        jnp.concatenate([exp_high, exp_low], axis=1),
        tok_in,
        preferred_element_type=f32,
    )
    in_part = both[:experts] + both[experts:]
    cot_part = jnp.einsum("ns,nd->sd", combine, tok_cot, preferred_element_type=f32)
    local_total = jnp.sum(exp_scores, axis=0)
    all_totals = jnp.broadcast_to(local_total[None, :], (experts, experts))
    message = jnp.stack(
        of_clips(jnp.concatenate([in_part, cot_part, all_totals], axis=1)), axis=1
    )
    message = sum_to_owner(message, group)[0]
    totals = message[:, 2 * width :]
    own_total = lax.dynamic_slice_in_dim(totals, owned, 1, 1)
    own_in = message[:, :width] / own_total
    row_x = own_in.astype(bf16)
    row_cot = message[:, width : 2 * width].astype(bf16)
    pre_act = jnp.dot(row_x, expert_in, preferred_element_type=f32)
    hidden = jax.nn.gelu(pre_act, approximate=False).astype(bf16)
    part_out = jnp.dot(hidden, expert_out, preferred_element_type=f32)
    hid_grad = jnp.einsum("od,hd->oh", row_cot, expert_out, preferred_element_type=f32)
    pre_grad = (hid_grad * gelu_slope(pre_act)).astype(bf16)
    part_dx = jnp.einsum("oh,dh->od", pre_grad, expert_in, preferred_element_type=f32)
    dot_part = jnp.sum(own_in * part_dx, axis=1, keepdims=True)
    message = jnp.concatenate([part_out, part_dx, dot_part], axis=1)[None]
    message = sum_to_all(message, group)
    whole_totals = jnp.broadcast_to(totals.T[:, :, None], (experts, clips, 1))
    message = jnp.concatenate([message, whole_totals], axis=2)
    handed = lax.dynamic_index_in_dim(message, clip, 1, keepdims=False)
    slot_y = handed[:, :width].astype(bf16)
    slot_dx = handed[:, width : 2 * width].astype(bf16)
    column_stat = handed[:, 2 * width : 2 * width + 1].T
    totals = handed[:, 2 * width + 1 :].T
    share = width // clips
    mine_x = lax.dynamic_slice_in_dim(row_x, clip * share, share, 1)
    mine_cot = lax.dynamic_slice_in_dim(row_cot, clip * share, share, 1)
    grad_expert_in = jnp.einsum("od,oh->dh", mine_x, pre_grad, preferred_element_type=f32)
    grad_expert_out = jnp.einsum("oh,od->hd", hidden, mine_cot, preferred_element_type=f32)
    mixed = jnp.dot(combine, slot_y, preferred_element_type=f32).astype(bf16)
    comb_dot = jnp.einsum("nd,sd->ns", tok_cot, slot_y, preferred_element_type=f32)
    grad_comb = combine_f * (comb_dot - jnp.sum(combine_f * comb_dot, axis=1, keepdims=True))
    dispatch_f = exp_scores / totals
    dispatch = dispatch_f.astype(bf16)
    disp_dot = jnp.einsum("nd,sd->ns", tok_in, slot_dx, preferred_element_type=f32)
    grad_disp = dispatch_f * (disp_dot - column_stat)
    score_grad = (logit_scale[0] * (grad_comb + grad_disp)).astype(bf16)
    norm_grad = jnp.einsum("ns,ds->nd", score_grad, phi_norm, preferred_element_type=f32)
    phi_part = jnp.einsum("nd,ns->sd", tok_norm, score_grad, preferred_element_type=f32)
    phi_flat = sum(of_clips(phi_part.reshape(1, 1, -1)))
    phi_flat = sum_to_all(phi_flat, size)
    phi_grad = phi_flat.reshape(experts, width).T
    through = jnp.dot(dispatch, slot_dx, preferred_element_type=f32)
    back_norm = tok_scale * (
        norm_grad - tok_unit * jnp.sum(tok_unit * norm_grad, axis=1, keepdims=True)
    )
    grad_tokens = (through + back_norm).astype(bf16)
    grad_router = phi_scale * (
        phi_grad - phi_unit * jnp.sum(phi_unit * phi_grad, axis=0, keepdims=True)
    )
    return (mixed[None], grad_tokens[None], grad_expert_in, grad_expert_out, grad_router)


def solution(mesh):
    return jax.shard_map(
        per_device,
        mesh=mesh,
        in_specs=(
            P("dp", "seq", None),
            P("dp", "seq", None),
            P(),
            P(),
            P(None, "seq"),
            P("seq", None),
        ),
        out_specs=(P("dp", "seq", None), P("dp", "seq", None), P("dp", "seq"), P("seq", "dp"), P()),
        check_vma=False,
    )
```

```python
import jax
import jax.numpy as jnp
from jax import lax
from jax.experimental import pallas as pl
from jax.experimental.pallas import tpu as pltpu
from jax.sharding import PartitionSpec as P

epsilon = 1e-06
AXES = ("seq", "dp")
LANES = 128
BLOCK = 128
VMEM_BYTES = 24 * 2**20
ROWS = (((1,), (1,)), ((), ()))
COLUMNS = (((0,), (0,)), ((), ()))
f32, bf16 = jnp.float32, jnp.bfloat16


def exchange(value, mask):
    clips = lax.axis_size("dp")
    pairs = []
    for place in range(lax.axis_size("seq")):
        for clip in range(clips):
            there = (place ^ mask) * clips + (clip ^ 1 if clips % 2 == 0 else clip)
            pairs.append((place * clips + clip, there))
    return lax.ppermute(value, AXES, pairs)


def hop(value, step):
    return lax.ppermute(value, "dp", [(i, i ^ step) for i in range(lax.axis_size("dp"))])


def of_clips(value):
    clips = lax.axis_size("dp")
    clip = lax.axis_index("dp")
    got = [value] + [hop(value, step) for step in range(1, clips)]
    ordered = []
    for index in range(clips):
        picked = got[0]
        for step in range(1, clips):
            picked = jnp.where(clip ^ step == index, got[step], picked)
        ordered.append(picked)
    return ordered


def rounds(size):
    masks = [1 << bit for bit in range(size.bit_length() - 1)]
    return [masks[i : i + 2] for i in range(0, len(masks), 2)]


def round_masks(pair):
    return pair if len(pair) == 1 else [pair[0], pair[1], pair[0] | pair[1]]


def sum_to_owner(value, group):
    place = lax.axis_index("seq")
    for pair in reversed(rounds(lax.axis_size("seq"))):
        owner_masks = [mask for mask in pair if mask >= group]
        blocks = value.reshape((1 << len(owner_masks), -1) + value.shape[1:])

        def block_for(mask):
            index = 0
            for bit, owner_mask in enumerate(owner_masks):
                index = index + jnp.where((place ^ mask) & owner_mask != 0, 1 << bit, 0)
            return lax.dynamic_index_in_dim(blocks, index, 0, keepdims=False)

        got = [block_for(0)] + [exchange(block_for(mask), mask) for mask in round_masks(pair)]
        value = got[0] + got[1] if len(got) == 2 else (got[0] + got[1]) + (got[2] + got[3])
    return value


def sum_to_all(value, group):
    place = lax.axis_index("seq")
    for pair in rounds(lax.axis_size("seq")):
        terms = {0: value}
        for mask in round_masks(pair):
            terms[mask] = exchange(value, mask)
        for mask in pair:
            upper = (place & mask) != 0
            merged = {}
            for key in terms:
                if key & mask:
                    continue
                near, far = terms[key], terms[key | mask]
                if mask < group:
                    merged[key] = near + far
                else:
                    merged[key] = jnp.where(
                        upper, jnp.concatenate([far, near]), jnp.concatenate([near, far])
                    )
            terms = merged
        value = terms[0]
    return value


def token_sums(scale_ref, phi_ref, tok_ref, cot_ref, message_ref, exp_ref, tok_scale_ref, norm_ref):
    experts, width = phi_ref.shape[1], phi_ref.shape[0]

    @pl.when(pl.program_id(0) == 0)
    def _():
        phi = phi_ref[...].astype(f32)
        phi_scale = lax.rsqrt(jnp.sum(phi * phi, axis=0, keepdims=True) + epsilon)
        norm_ref[...] = (phi * phi_scale).astype(bf16)
        message_ref[...] = jnp.zeros_like(message_ref)

    tok_in = tok_ref[...]
    tok_f32 = tok_in.astype(f32)
    tok_scale = lax.rsqrt(jnp.sum(tok_f32 * tok_f32, axis=1, keepdims=True) + epsilon)
    tok_norm = (tok_f32 * tok_scale).astype(bf16)
    logits = scale_ref[0] * jnp.dot(tok_norm, norm_ref[...], preferred_element_type=f32)
    exp_scores = jnp.exp(logits)
    combine = (exp_scores / jnp.sum(exp_scores, axis=1, keepdims=True)).astype(bf16)
    exp_high = exp_scores.astype(bf16)
    exp_low = (exp_scores - exp_high.astype(f32)).astype(bf16)
    in_part = lax.dot_general(exp_high, tok_in, COLUMNS, preferred_element_type=f32)
    in_part = in_part + lax.dot_general(exp_low, tok_in, COLUMNS, preferred_element_type=f32)
    cot_part = lax.dot_general(combine, cot_ref[...], COLUMNS, preferred_element_type=f32)
    message_ref[:, :width] += in_part
    message_ref[:, width : 2 * width] += cot_part
    total = jnp.sum(exp_scores, axis=0, keepdims=True)
    message_ref[:, 2 * width : 2 * width + experts] += jnp.broadcast_to(total, (experts, experts))
    exp_ref[...] = exp_scores
    tok_scale_ref[...] = tok_scale


def expert_rows(owned_ref, sums_ref, in_ref, out_ref, message_ref, row_x_ref, row_cot_ref, hidden_ref, pre_grad_ref):
    width, units = in_ref.shape
    spare = sums_ref[:, 2 * width :]
    lane = lax.broadcasted_iota(jnp.int32, spare.shape, 1)
    own_total = jnp.sum(jnp.where(lane == owned_ref[0], spare, 0.0), axis=1, keepdims=True)
    own_in = sums_ref[:, :width] / own_total
    row_x = own_in.astype(bf16)
    row_cot = sums_ref[:, width : 2 * width].astype(bf16)
    pre_act = jnp.dot(row_x, in_ref[...], preferred_element_type=f32)
    hid_grad = lax.dot_general(row_cot, out_ref[...], ROWS, preferred_element_type=f32)
    cdf = 0.5 * (1.0 + lax.erf(pre_act * 0.7071067811865476))
    hidden = (pre_act * cdf).astype(bf16)
    slope = cdf + pre_act * jnp.exp(-0.5 * pre_act * pre_act) * 0.3989422804014327
    pre_grad = (hid_grad * slope).astype(bf16)
    part_out = jnp.dot(hidden, out_ref[...], preferred_element_type=f32)
    part_dx = lax.dot_general(pre_grad, in_ref[...], ROWS, preferred_element_type=f32)
    message_ref[:, :width] = part_out
    message_ref[:, width : 2 * width] = part_dx
    dot_part = jnp.sum(own_in * part_dx, axis=1, keepdims=True)
    message_ref[:, 2 * width :] = jnp.broadcast_to(dot_part, spare.shape)
    row_x_ref[...] = row_x
    row_cot_ref[...] = row_cot
    hidden_ref[...] = hidden
    pre_grad_ref[...] = pre_grad


def as_row(column):
    slots = column.shape[0]
    shape = (slots, slots)
    same = lax.broadcasted_iota(jnp.int32, shape, 0) == lax.broadcasted_iota(jnp.int32, shape, 1)
    return jnp.sum(jnp.where(same, column, 0.0), axis=0, keepdims=True)


def score_grads(scale_ref, slots_ref, totals_ref, tok_ref, cot_ref, exp_ref, tok_scale_ref, grad_ref, phi_ref):
    width = tok_ref.shape[1]

    @pl.when(pl.program_id(0) == 0)
    def _():
        phi_ref[...] = jnp.zeros_like(phi_ref)

    slot_y = slots_ref[:, :width].astype(bf16)
    slot_dx = slots_ref[:, width : 2 * width].astype(bf16)
    column_stat = as_row(slots_ref[:, 2 * width : 2 * width + 1])
    totals = totals_ref[:, : slot_y.shape[0]]
    tok_in = tok_ref[...]
    exp_scores = exp_ref[...]
    combine_f = exp_scores / jnp.sum(exp_scores, axis=1, keepdims=True)
    comb_dot = lax.dot_general(cot_ref[...], slot_y, ROWS, preferred_element_type=f32)
    grad_comb = combine_f * (comb_dot - jnp.sum(combine_f * comb_dot, axis=1, keepdims=True))
    disp_dot = lax.dot_general(tok_in, slot_dx, ROWS, preferred_element_type=f32)
    grad_disp = exp_scores / totals * (disp_dot - column_stat)
    score_grad = (scale_ref[0] * (grad_comb + grad_disp)).astype(bf16)
    tok_norm = (tok_in.astype(f32) * tok_scale_ref[...]).astype(bf16)
    phi_ref[...] += lax.dot_general(score_grad, tok_norm, COLUMNS, preferred_element_type=f32)
    grad_ref[...] = score_grad.astype(f32)


def whole(shape):
    return pl.BlockSpec(shape, lambda *_: (0,) * len(shape))


def block_of(rows, columns):
    return pl.BlockSpec((rows, columns), lambda i: (i, 0))


def per_device(tokens, cotangent, router, logit_scale, expert_in, expert_out):
    tok_in = tokens[0]
    tok_cot = cotangent[0]
    count = tok_in.shape[0]
    width, experts = router.shape
    units = expert_in.shape[1]
    size = lax.axis_size("seq")
    group = size // experts
    clips = lax.axis_size("dp")
    clip = lax.axis_index("dp")
    owned = lax.axis_index("seq") // group
    length = 2 * width + -(-experts // LANES) * LANES
    rows = min(BLOCK, count)
    scalar = pl.BlockSpec(memory_space=pltpu.SMEM)
    params = pltpu.CompilerParams(vmem_limit_bytes=VMEM_BYTES)
    message, exp_scores, tok_scale = pl.pallas_call(
        token_sums,
        grid=(count // rows,),
        in_specs=[scalar, whole((width, experts)), block_of(rows, width), block_of(rows, width)],
        out_specs=[whole((experts, length)), block_of(rows, experts), block_of(rows, 1)],
        out_shape=[
            jax.ShapeDtypeStruct((experts, length), f32),
            jax.ShapeDtypeStruct((count, experts), f32),
            jax.ShapeDtypeStruct((count, 1), f32),
        ],
        scratch_shapes=[pltpu.VMEM((width, experts), bf16)],
        compiler_params=params,
        name="token_sums",
    )(logit_scale, router, tok_in, tok_cot)
    message = sum_to_owner(jnp.stack(of_clips(message), axis=1), group)[0]
    totals = message[:, 2 * width :]
    message, row_x, row_cot, hidden, pre_grad = pl.pallas_call(
        expert_rows,
        in_specs=[scalar] + [pl.BlockSpec(memory_space=pltpu.VMEM)] * 3,
        out_shape=[
            jax.ShapeDtypeStruct((clips, length), f32),
            jax.ShapeDtypeStruct((clips, width), bf16),
            jax.ShapeDtypeStruct((clips, width), bf16),
            jax.ShapeDtypeStruct((clips, units), bf16),
            jax.ShapeDtypeStruct((clips, units), bf16),
        ],
        compiler_params=params,
        name="expert_rows",
    )(owned[None], message, expert_in, expert_out)
    message = sum_to_all(message[None], group)
    slots = lax.dynamic_index_in_dim(message, clip, 1, keepdims=False)
    totals = lax.dynamic_index_in_dim(totals, clip, 0, keepdims=True)
    share = width // clips
    mine_x = lax.dynamic_slice_in_dim(row_x, clip * share, share, 1)
    mine_cot = lax.dynamic_slice_in_dim(row_cot, clip * share, share, 1)
    grad_expert_in = jnp.einsum("od,oh->dh", mine_x, pre_grad, preferred_element_type=f32)
    grad_expert_out = jnp.einsum("oh,od->hd", hidden, mine_cot, preferred_element_type=f32)
    score_grad, phi_part = pl.pallas_call(
        score_grads,
        grid=(count // rows,),
        in_specs=[
            scalar,
            whole((experts, length)),
            whole((1, length - 2 * width)),
            block_of(rows, width),
            block_of(rows, width),
            block_of(rows, experts),
            block_of(rows, 1),
        ],
        out_specs=[block_of(rows, experts), whole((experts, width))],
        out_shape=[
            jax.ShapeDtypeStruct((count, experts), f32),
            jax.ShapeDtypeStruct((experts, width), f32),
        ],
        compiler_params=params,
        name="score_grads",
    )(logit_scale, slots, totals, tok_in, tok_cot, exp_scores, tok_scale)
    phi_flat = sum(of_clips(phi_part.reshape(1, 1, -1)))
    phi_grad = sum_to_all(phi_flat, size).reshape(experts, width).T
    phi_f32 = router.astype(f32)
    phi_scale = lax.rsqrt(jnp.sum(phi_f32 * phi_f32, axis=0, keepdims=True) + epsilon)
    phi_unit = phi_f32 * phi_scale
    phi_norm = phi_unit.astype(bf16)
    slot_y = slots[:, :width].astype(bf16)
    slot_dx = slots[:, width : 2 * width].astype(bf16)
    combine = (exp_scores / jnp.sum(exp_scores, axis=1, keepdims=True)).astype(bf16)
    dispatch = (exp_scores / totals[:, :experts]).astype(bf16)
    mixed = jnp.dot(combine, slot_y, preferred_element_type=f32).astype(bf16)
    norm_grad = jnp.einsum(
        "ns,ds->nd", score_grad.astype(bf16), phi_norm, preferred_element_type=f32
    )
    through = jnp.dot(dispatch, slot_dx, preferred_element_type=f32)
    tok_unit = tok_in.astype(f32) * tok_scale
    back_norm = tok_scale * (
        norm_grad - tok_unit * jnp.sum(tok_unit * norm_grad, axis=1, keepdims=True)
    )
    grad_tokens = (through + back_norm).astype(bf16)
    grad_router = phi_scale * (
        phi_grad - phi_unit * jnp.sum(phi_unit * phi_grad, axis=0, keepdims=True)
    )
    return (mixed[None], grad_tokens[None], grad_expert_in, grad_expert_out, grad_router)


def solution(mesh):
    return jax.shard_map(
        per_device,
        mesh=mesh,
        in_specs=(
            P("dp", "seq", None),
            P("dp", "seq", None),
            P(),
            P(),
            P(None, "seq"),
            P("seq", None),
        ),
        out_specs=(P("dp", "seq", None), P("dp", "seq", None), P("dp", "seq"), P("seq", "dp"), P()),
        check_vma=False,
    )
```

```python
import jax
import jax.numpy as jnp
from jax import lax
from jax.experimental import pallas as pl
from jax.experimental.pallas import tpu as pltpu
from jax.sharding import PartitionSpec as P

epsilon = 1e-06
AXES = ("seq", "dp")
LANES = 128
PIECES = 4
VMEM_BYTES = 20 * 2**20
ROWS = (((1,), (1,)), ((), ()))
COLUMNS = (((0,), (0,)), ((), ()))
f32, bf16 = jnp.float32, jnp.bfloat16


def exchange(value, mask):
    clips = lax.axis_size("dp")
    pairs = []
    for place in range(lax.axis_size("seq")):
        for clip in range(clips):
            there = (place ^ mask) * clips + (clip ^ 1 if clips % 2 == 0 else clip)
            pairs.append((place * clips + clip, there))
    return lax.ppermute(value, AXES, pairs)


def hop(value, step):
    return lax.ppermute(value, "dp", [(i, i ^ step) for i in range(lax.axis_size("dp"))])


def of_clips(value):
    clips = lax.axis_size("dp")
    clip = lax.axis_index("dp")
    got = [value] + [hop(value, step) for step in range(1, clips)]
    ordered = []
    for index in range(clips):
        picked = got[0]
        for step in range(1, clips):
            picked = jnp.where(clip ^ step == index, got[step], picked)
        ordered.append(picked)
    return ordered


def rounds(size):
    masks = [1 << bit for bit in range(size.bit_length() - 1)]
    return [masks[i : i + 2] for i in range(0, len(masks), 2)]


def round_masks(pair):
    return pair if len(pair) == 1 else [pair[0], pair[1], pair[0] | pair[1]]


def sum_to_owner(value, group):
    place = lax.axis_index("seq")
    for pair in reversed(rounds(lax.axis_size("seq"))):
        owner_masks = [mask for mask in pair if mask >= group]
        blocks = value.reshape((1 << len(owner_masks), -1) + value.shape[1:])

        def block_for(mask):
            index = 0
            for bit, owner_mask in enumerate(owner_masks):
                index = index + jnp.where((place ^ mask) & owner_mask != 0, 1 << bit, 0)
            return lax.dynamic_index_in_dim(blocks, index, 0, keepdims=False)

        got = [block_for(0)] + [exchange(block_for(mask), mask) for mask in round_masks(pair)]
        value = got[0] + got[1] if len(got) == 2 else (got[0] + got[1]) + (got[2] + got[3])
    return value


def sum_to_all(value, group, later=()):
    place = lax.axis_index("seq")
    for pair in rounds(lax.axis_size("seq")):
        terms = {0: value}
        for mask in round_masks(pair):
            terms[mask] = exchange(value, mask)
        for mask in pair:
            upper = (place & mask) != 0
            merged = {}
            for key in terms:
                if key & mask:
                    continue
                near, far = terms[key], terms[key | mask]
                if mask < group:
                    merged[key] = near + far
                else:
                    merged[key] = jnp.where(
                        upper, jnp.concatenate([far, near]), jnp.concatenate([near, far])
                    )
            terms = merged
        value = terms[0]
        if later and pair[0] == 1:
            value, *later = lax.optimization_barrier((value, *later))
    return (value, *later) if later else value


def token_sums(scale_ref, phi_ref, tok_ref, cot_ref, message_ref, exp_ref, combine_ref, tok_scale_ref, norm_ref, tok_buf, cot_buf, sems):
    experts, width = phi_ref.shape
    blocks = sems.shape[1]
    rows = tok_buf.shape[0] // blocks
    pieces = [pl.ds(index * rows, rows) for index in range(blocks)]
    tok_copies = [
        pltpu.make_async_copy(tok_ref.at[piece], tok_buf.at[piece], sems.at[0, index])
        for index, piece in enumerate(pieces)
    ]
    cot_copies = [
        pltpu.make_async_copy(cot_ref.at[piece], cot_buf.at[piece], sems.at[1, index])
        for index, piece in enumerate(pieces)
    ]
    for copy in tok_copies + cot_copies:
        copy.start()
    phi = phi_ref[...].astype(f32)
    phi_scale = lax.rsqrt(jnp.sum(phi * phi, axis=1, keepdims=True) + epsilon)
    phi_norm = (phi * phi_scale).astype(bf16)
    for copy, piece in zip(tok_copies, pieces):
        copy.wait()
        tok_f32 = tok_buf[piece, :].astype(f32)
        tok_scale = lax.rsqrt(jnp.sum(tok_f32 * tok_f32, axis=1, keepdims=True) + epsilon)
        norm_ref[piece, :] = (tok_f32 * tok_scale).astype(bf16)
        tok_scale_ref[piece, :] = tok_scale
    logits = scale_ref[0] * lax.dot_general(phi_norm, norm_ref[...], ROWS, preferred_element_type=f32)
    exp_scores = jnp.exp(logits)
    combine = (exp_scores / jnp.sum(exp_scores, axis=0, keepdims=True)).astype(bf16)
    exp_high = exp_scores.astype(bf16).astype(f32)
    halves = jnp.concatenate([exp_high, exp_scores - exp_high], axis=0).astype(bf16)
    in_parts = jnp.dot(halves, tok_buf[...], preferred_element_type=f32)
    message_ref[:, :width] = in_parts[:experts] + in_parts[experts:]
    spare = message_ref.shape[1] - 2 * width
    total = as_row(jnp.sum(exp_scores, axis=1, keepdims=True), spare)
    message_ref[:, 2 * width :] = jnp.broadcast_to(total, (experts, spare))
    exp_ref[...] = exp_scores
    combine_ref[...] = combine
    for copy in cot_copies:
        copy.wait()
    message_ref[:, width : 2 * width] = jnp.dot(combine, cot_buf[...], preferred_element_type=f32)


def expert_rows(owned_ref, sums_ref, in_ref, out_ref, message_ref, row_x_ref, row_cot_ref, hidden_ref, pre_grad_ref):
    width, units = in_ref.shape
    spare = sums_ref[:, 2 * width :]
    lane = lax.broadcasted_iota(jnp.int32, spare.shape, 1)
    own_total = jnp.sum(jnp.where(lane == owned_ref[0], spare, 0.0), axis=1, keepdims=True)
    own_in = sums_ref[:, :width] / own_total
    row_x = own_in.astype(bf16)
    row_cot = sums_ref[:, width : 2 * width].astype(bf16)
    pre_act = jnp.dot(row_x, in_ref[...], preferred_element_type=f32)
    hid_grad = lax.dot_general(row_cot, out_ref[...], ROWS, preferred_element_type=f32)
    cdf = 0.5 * (1.0 + lax.erf(pre_act * 0.7071067811865476))
    hidden = (pre_act * cdf).astype(bf16)
    slope = cdf + pre_act * jnp.exp(-0.5 * pre_act * pre_act) * 0.3989422804014327
    pre_grad = (hid_grad * slope).astype(bf16)
    part_out = jnp.dot(hidden, out_ref[...], preferred_element_type=f32)
    part_dx = lax.dot_general(pre_grad, in_ref[...], ROWS, preferred_element_type=f32)
    message_ref[:, :width] = part_out
    message_ref[:, width : 2 * width] = part_dx
    dot_part = jnp.sum(own_in * part_dx, axis=1, keepdims=True)
    message_ref[:, 2 * width :] = jnp.broadcast_to(dot_part, spare.shape)
    row_x_ref[...] = row_x
    row_cot_ref[...] = row_cot
    hidden_ref[...] = hidden
    pre_grad_ref[...] = pre_grad


def as_row(column, lanes):
    shape = (column.shape[0], lanes)
    same = lax.broadcasted_iota(jnp.int32, shape, 0) == lax.broadcasted_iota(jnp.int32, shape, 1)
    return jnp.sum(jnp.where(same, column, 0.0), axis=0, keepdims=True)


def as_column(row, slots):
    shape = (slots, row.shape[1])
    same = lax.broadcasted_iota(jnp.int32, shape, 0) == lax.broadcasted_iota(jnp.int32, shape, 1)
    return jnp.sum(jnp.where(same, row, 0.0), axis=1, keepdims=True)


def score_grads(scale_ref, slots_ref, totals_ref, tok_ref, cot_ref, norm_ref, exp_ref, grad_ref, dispatch_ref, phi_ref):
    width = tok_ref.shape[1]
    slot_y = slots_ref[:, :width].astype(bf16)
    slot_dx = slots_ref[:, width : 2 * width].astype(bf16)
    column_stat = slots_ref[:, 2 * width : 2 * width + 1]
    totals = as_column(totals_ref[...], slot_y.shape[0])
    exp_scores = exp_ref[...]
    combine_f = exp_scores / jnp.sum(exp_scores, axis=0, keepdims=True)
    comb_dot = lax.dot_general(slot_y, cot_ref[...], ROWS, preferred_element_type=f32)
    grad_comb = combine_f * (comb_dot - jnp.sum(combine_f * comb_dot, axis=0, keepdims=True))
    disp_dot = lax.dot_general(slot_dx, tok_ref[...], ROWS, preferred_element_type=f32)
    dispatch_f = exp_scores / totals
    grad_disp = dispatch_f * (disp_dot - column_stat)
    score_grad = (scale_ref[0] * (grad_comb + grad_disp)).astype(bf16)
    phi_ref[...] = jnp.dot(score_grad, norm_ref[...], preferred_element_type=f32)
    grad_ref[...] = score_grad
    dispatch_ref[...] = dispatch_f.astype(bf16)


def per_device(tokens, cotangent, router, logit_scale, expert_in, expert_out):
    tok_in = tokens[0]
    tok_cot = cotangent[0]
    count = tok_in.shape[0]
    width, experts = router.shape
    units = expert_in.shape[1]
    size = lax.axis_size("seq")
    group = size // experts
    clips = lax.axis_size("dp")
    clip = lax.axis_index("dp")
    owned = lax.axis_index("seq") // group
    length = 2 * width + -(-experts // LANES) * LANES
    scalar = pl.BlockSpec(memory_space=pltpu.SMEM)
    in_vmem = pl.BlockSpec(memory_space=pltpu.VMEM)
    in_hbm = pl.BlockSpec(memory_space=pltpu.HBM)
    params = pltpu.CompilerParams(vmem_limit_bytes=VMEM_BYTES)
    phi = router.T
    message, exp_scores, combine, tok_scale, tok_norm = pl.pallas_call(
        token_sums,
        in_specs=[scalar, in_vmem, in_hbm, in_hbm],
        out_shape=[
            jax.ShapeDtypeStruct((experts, length), f32),
            jax.ShapeDtypeStruct((experts, count), f32),
            jax.ShapeDtypeStruct((experts, count), bf16),
            jax.ShapeDtypeStruct((count, 1), f32),
            jax.ShapeDtypeStruct((count, width), bf16),
        ],
        scratch_shapes=[
            pltpu.VMEM((count, width), bf16),
            pltpu.VMEM((count, width), bf16),
            pltpu.SemaphoreType.DMA((2, PIECES)),
        ],
        compiler_params=params,
        name="token_sums",
    )(logit_scale, phi, *[pltpu.with_memory_space_constraint(x, pltpu.HBM) for x in (tok_in, tok_cot)])
    message = sum_to_owner(jnp.stack(of_clips(message), axis=1), group)[0]
    totals = message[:, 2 * width :]
    message, row_x, row_cot, hidden, pre_grad = pl.pallas_call(
        expert_rows,
        in_specs=[scalar] + [in_vmem] * 3,
        out_shape=[
            jax.ShapeDtypeStruct((clips, length), f32),
            jax.ShapeDtypeStruct((clips, width), bf16),
            jax.ShapeDtypeStruct((clips, width), bf16),
            jax.ShapeDtypeStruct((clips, units), bf16),
            jax.ShapeDtypeStruct((clips, units), bf16),
        ],
        compiler_params=params,
        name="expert_rows",
    )(owned[None], message, expert_in, expert_out)
    message, hidden, row_cot = sum_to_all(message[None], group, (hidden, row_cot))
    slots = lax.dynamic_index_in_dim(message, clip, 1, keepdims=False)
    totals = lax.dynamic_index_in_dim(totals, clip, 0, keepdims=True)
    share = width // clips
    mine_x = lax.dynamic_slice_in_dim(row_x, clip * share, share, 1)
    mine_cot = lax.dynamic_slice_in_dim(row_cot, clip * share, share, 1)
    grad_expert_in = jnp.einsum("od,oh->dh", mine_x, pre_grad, preferred_element_type=f32)
    grad_expert_out = jnp.einsum("oh,od->hd", hidden, mine_cot, preferred_element_type=f32)
    score_grad, dispatch, phi_part = pl.pallas_call(
        score_grads,
        in_specs=[scalar] + [in_vmem] * 6,
        out_shape=[
            jax.ShapeDtypeStruct((experts, count), bf16),
            jax.ShapeDtypeStruct((experts, count), bf16),
            jax.ShapeDtypeStruct((experts, width), f32),
        ],
        compiler_params=params,
        name="score_grads",
    )(logit_scale, slots, totals, tok_in, tok_cot, tok_norm, exp_scores)
    phi_flat = sum(of_clips(phi_part.reshape(1, 1, -1)))
    phi_grad = sum_to_all(phi_flat, size).reshape(experts, width)
    phi_f32 = phi.astype(f32)
    phi_scale = lax.rsqrt(jnp.sum(phi_f32 * phi_f32, axis=1, keepdims=True) + epsilon)
    phi_unit = phi_f32 * phi_scale
    phi_norm = phi_unit.astype(bf16)
    slot_y = slots[:, :width].astype(bf16)
    slot_dx = slots[:, width : 2 * width].astype(bf16)
    mixed = jnp.einsum("sn,sd->nd", combine, slot_y, preferred_element_type=f32).astype(bf16)
    norm_grad = jnp.einsum("sn,sd->nd", score_grad, phi_norm, preferred_element_type=f32)
    through = jnp.einsum("sn,sd->nd", dispatch, slot_dx, preferred_element_type=f32)
    tok_unit = tok_in.astype(f32) * tok_scale
    back_norm = tok_scale * (
        norm_grad - tok_unit * jnp.sum(tok_unit * norm_grad, axis=1, keepdims=True)
    )
    grad_tokens = (through + back_norm).astype(bf16)
    grad_router = phi_scale * (
        phi_grad - phi_unit * jnp.sum(phi_unit * phi_grad, axis=1, keepdims=True)
    )
    return (mixed[None], grad_tokens[None], grad_expert_in, grad_expert_out, grad_router.T)


def solution(mesh):
    return jax.shard_map(
        per_device,
        mesh=mesh,
        in_specs=(
            P("dp", "seq", None),
            P("dp", "seq", None),
            P(),
            P(),
            P(None, "seq"),
            P("seq", None),
        ),
        out_specs=(P("dp", "seq", None), P("dp", "seq", None), P("dp", "seq"), P("seq", "dp"), P()),
        check_vma=False,
    )
```

```python
import jax
import jax.numpy as jnp
from jax import lax
from jax.experimental import pallas as pl
from jax.experimental.pallas import tpu as pltpu
from jax.sharding import PartitionSpec as P

epsilon = 1e-06
AXES = ("seq", "dp")
LANES = 128
PIECES = 4
VMEM_BYTES = 10 * 2**20
ROWS = (((1,), (1,)), ((), ()))
COLUMNS = (((0,), (0,)), ((), ()))
f32, bf16 = jnp.float32, jnp.bfloat16


def exchange(value, mask):
    clips = lax.axis_size("dp")
    pairs = []
    for place in range(lax.axis_size("seq")):
        for clip in range(clips):
            there = (place ^ mask) * clips + (clip ^ 1 if clips % 2 == 0 else clip)
            pairs.append((place * clips + clip, there))
    return lax.ppermute(value, AXES, pairs)


def hop(value, step):
    return lax.ppermute(value, "dp", [(i, i ^ step) for i in range(lax.axis_size("dp"))])


def of_clips(value):
    clips = lax.axis_size("dp")
    clip = lax.axis_index("dp")
    got = [value] + [hop(value, step) for step in range(1, clips)]
    ordered = []
    for index in range(clips):
        picked = got[0]
        for step in range(1, clips):
            picked = jnp.where(clip ^ step == index, got[step], picked)
        ordered.append(picked)
    return ordered


def rounds(size):
    masks = [1 << bit for bit in range(size.bit_length() - 1)]
    return [masks[i : i + 2] for i in range(0, len(masks), 2)]


def round_masks(pair):
    return pair if len(pair) == 1 else [pair[0], pair[1], pair[0] | pair[1]]


def sum_to_owner(value, group):
    place = lax.axis_index("seq")
    for pair in reversed(rounds(lax.axis_size("seq"))):
        owner_masks = [mask for mask in pair if mask >= group]
        blocks = value.reshape((1 << len(owner_masks), -1) + value.shape[1:])

        def block_for(mask):
            index = 0
            for bit, owner_mask in enumerate(owner_masks):
                index = index + jnp.where((place ^ mask) & owner_mask != 0, 1 << bit, 0)
            return lax.dynamic_index_in_dim(blocks, index, 0, keepdims=False)

        got = [block_for(0)] + [exchange(block_for(mask), mask) for mask in round_masks(pair)]
        value = got[0] + got[1] if len(got) == 2 else (got[0] + got[1]) + (got[2] + got[3])
    return value


def sum_to_all(value, group, later=()):
    place = lax.axis_index("seq")
    for pair in rounds(lax.axis_size("seq")):
        terms = {0: value}
        for mask in round_masks(pair):
            terms[mask] = exchange(value, mask)
        for mask in pair:
            upper = (place & mask) != 0
            merged = {}
            for key in terms:
                if key & mask:
                    continue
                near, far = terms[key], terms[key | mask]
                if mask < group:
                    merged[key] = near + far
                else:
                    merged[key] = jnp.where(
                        upper, jnp.concatenate([far, near]), jnp.concatenate([near, far])
                    )
            terms = merged
        value = terms[0]
        if later and pair[0] == 1:
            value, *later = lax.optimization_barrier((value, *later))
    return (value, *later) if later else value


def token_sums(scale_ref, phi_ref, tok_ref, cot_ref, message_ref, exp_ref, combine_ref, tok_scale_ref, norm_ref, tok_buf, cot_buf, sems):
    experts, width = phi_ref.shape
    blocks = sems.shape[1]
    rows = tok_buf.shape[0] // blocks
    pieces = [pl.ds(index * rows, rows) for index in range(blocks)]
    tok_copies = [
        pltpu.make_async_copy(tok_ref.at[piece], tok_buf.at[piece], sems.at[0, index])
        for index, piece in enumerate(pieces)
    ]
    cot_copies = [
        pltpu.make_async_copy(cot_ref.at[piece], cot_buf.at[piece], sems.at[1, index])
        for index, piece in enumerate(pieces)
    ]
    for copy in tok_copies + cot_copies:
        copy.start()
    phi = phi_ref[...].astype(f32)
    phi_scale = lax.rsqrt(jnp.sum(phi * phi, axis=1, keepdims=True) + epsilon)
    phi_norm = (phi * phi_scale).astype(bf16)
    for copy, piece in zip(tok_copies, pieces):
        copy.wait()
        tok_f32 = tok_buf[piece, :].astype(f32)
        tok_scale = lax.rsqrt(jnp.sum(tok_f32 * tok_f32, axis=1, keepdims=True) + epsilon)
        norm_ref[piece, :] = (tok_f32 * tok_scale).astype(bf16)
        tok_scale_ref[piece, :] = tok_scale
    logits = scale_ref[0] * lax.dot_general(phi_norm, norm_ref[...], ROWS, preferred_element_type=f32)
    exp_scores = jnp.exp(logits)
    combine = (exp_scores / jnp.sum(exp_scores, axis=0, keepdims=True)).astype(bf16)
    exp_high = exp_scores.astype(bf16).astype(f32)
    halves = jnp.concatenate([exp_high, exp_scores - exp_high], axis=0).astype(bf16)
    in_parts = jnp.dot(halves, tok_buf[...], preferred_element_type=f32)
    message_ref[:, :width] = in_parts[:experts] + in_parts[experts:]
    spare = message_ref.shape[1] - 2 * width
    total = as_row(jnp.sum(exp_scores, axis=1, keepdims=True), spare)
    message_ref[:, 2 * width :] = jnp.broadcast_to(total, (experts, spare))
    exp_ref[...] = exp_scores
    combine_ref[...] = combine
    for copy in cot_copies:
        copy.wait()
    message_ref[:, width : 2 * width] = jnp.dot(combine, cot_buf[...], preferred_element_type=f32)


def fetch(in_ref, out_ref, in_buf, out_buf, sems):
    copies = []
    for which, (source, target) in enumerate([(in_ref, in_buf), (out_ref, out_buf)]):
        rows = source.shape[0] // sems.shape[1]
        for index in range(sems.shape[1]):
            piece = pl.ds(index * rows, rows)
            copies.append(
                pltpu.make_async_copy(source.at[piece], target.at[piece], sems.at[which, index])
            )
    for copy in copies:
        copy.start()
    for copy in copies:
        copy.wait()


def expert_rows(owned_ref, sums_ref, in_ref, out_ref, message_ref, row_x_ref, row_cot_ref, hidden_ref, pre_grad_ref):
    width, units = in_ref.shape
    spare = sums_ref[:, 2 * width :]
    lane = lax.broadcasted_iota(jnp.int32, spare.shape, 1)
    own_total = jnp.sum(jnp.where(lane == owned_ref[0], spare, 0.0), axis=1, keepdims=True)
    own_in = sums_ref[:, :width] / own_total
    row_x = own_in.astype(bf16)
    row_cot = sums_ref[:, width : 2 * width].astype(bf16)
    pre_act = jnp.dot(row_x, in_ref[...], preferred_element_type=f32)
    hid_grad = lax.dot_general(row_cot, out_ref[...], ROWS, preferred_element_type=f32)
    cdf = 0.5 * (1.0 + lax.erf(pre_act * 0.7071067811865476))
    hidden = (pre_act * cdf).astype(bf16)
    slope = cdf + pre_act * jnp.exp(-0.5 * pre_act * pre_act) * 0.3989422804014327
    pre_grad = (hid_grad * slope).astype(bf16)
    part_out = jnp.dot(hidden, out_ref[...], preferred_element_type=f32)
    part_dx = lax.dot_general(pre_grad, in_ref[...], ROWS, preferred_element_type=f32)
    message_ref[:, :width] = part_out
    message_ref[:, width : 2 * width] = part_dx
    dot_part = jnp.sum(own_in * part_dx, axis=1, keepdims=True)
    message_ref[:, 2 * width :] = jnp.broadcast_to(dot_part, spare.shape)
    row_x_ref[...] = row_x
    row_cot_ref[...] = row_cot
    hidden_ref[...] = hidden
    pre_grad_ref[...] = pre_grad


def as_row(column, lanes):
    shape = (column.shape[0], lanes)
    same = lax.broadcasted_iota(jnp.int32, shape, 0) == lax.broadcasted_iota(jnp.int32, shape, 1)
    return jnp.sum(jnp.where(same, column, 0.0), axis=0, keepdims=True)


def as_column(row, slots):
    shape = (slots, row.shape[1])
    same = lax.broadcasted_iota(jnp.int32, shape, 0) == lax.broadcasted_iota(jnp.int32, shape, 1)
    return jnp.sum(jnp.where(same, row, 0.0), axis=1, keepdims=True)


def score_grads(scale_ref, slots_ref, totals_ref, tok_ref, cot_ref, norm_ref, exp_ref, grad_ref, dispatch_ref, phi_ref):
    width = tok_ref.shape[1]
    slot_y = slots_ref[:, :width].astype(bf16)
    slot_dx = slots_ref[:, width : 2 * width].astype(bf16)
    column_stat = slots_ref[:, 2 * width : 2 * width + 1]
    totals = as_column(totals_ref[...], slot_y.shape[0])
    exp_scores = exp_ref[...]
    combine_f = exp_scores / jnp.sum(exp_scores, axis=0, keepdims=True)
    comb_dot = lax.dot_general(slot_y, cot_ref[...], ROWS, preferred_element_type=f32)
    grad_comb = combine_f * (comb_dot - jnp.sum(combine_f * comb_dot, axis=0, keepdims=True))
    disp_dot = lax.dot_general(slot_dx, tok_ref[...], ROWS, preferred_element_type=f32)
    dispatch_f = exp_scores / totals
    grad_disp = dispatch_f * (disp_dot - column_stat)
    score_grad = (scale_ref[0] * (grad_comb + grad_disp)).astype(bf16)
    phi_ref[...] = jnp.dot(score_grad, norm_ref[...], preferred_element_type=f32)
    grad_ref[...] = score_grad
    dispatch_ref[...] = dispatch_f.astype(bf16)


def in_place(operand):
    return pltpu.with_memory_space_constraint(operand, pltpu.HBM)


def per_device(tokens, cotangent, router, logit_scale, expert_in, expert_out):
    tok_in = tokens[0]
    tok_cot = cotangent[0]
    count = tok_in.shape[0]
    width, experts = router.shape
    units = expert_in.shape[1]
    size = lax.axis_size("seq")
    group = size // experts
    clips = lax.axis_size("dp")
    clip = lax.axis_index("dp")
    owned = lax.axis_index("seq") // group
    length = 2 * width + -(-experts // LANES) * LANES
    scalar = pl.BlockSpec(memory_space=pltpu.SMEM)
    in_vmem = pl.BlockSpec(memory_space=pltpu.VMEM)
    in_hbm = pl.BlockSpec(memory_space=pltpu.HBM)
    params = pltpu.CompilerParams(vmem_limit_bytes=VMEM_BYTES)
    phi = router.T
    message, exp_scores, combine, tok_scale, tok_norm = pl.pallas_call(
        token_sums,
        in_specs=[scalar, in_vmem, in_hbm, in_hbm],
        out_shape=[
            jax.ShapeDtypeStruct((experts, length), f32),
            jax.ShapeDtypeStruct((experts, count), f32),
            jax.ShapeDtypeStruct((experts, count), bf16),
            jax.ShapeDtypeStruct((count, 1), f32),
            jax.ShapeDtypeStruct((count, width), bf16),
        ],
        scratch_shapes=[
            pltpu.VMEM((count, width), bf16),
            pltpu.VMEM((count, width), bf16),
            pltpu.SemaphoreType.DMA((2, PIECES)),
        ],
        compiler_params=params,
        name="token_sums",
    )(logit_scale, phi, in_place(tok_in), in_place(tok_cot))
    message = jnp.stack(of_clips(message), axis=1)
    message, expert_in, expert_out = lax.optimization_barrier((message, expert_in, expert_out))
    expert_in, expert_out = pl.pallas_call(
        fetch,
        in_specs=[in_hbm] * 2,
        out_specs=[in_vmem] * 2,
        out_shape=[
            jax.ShapeDtypeStruct(expert_in.shape, bf16),
            jax.ShapeDtypeStruct(expert_out.shape, bf16),
        ],
        scratch_shapes=[pltpu.SemaphoreType.DMA((2, PIECES))],
        compiler_params=params,
        cost_estimate=pl.CostEstimate(
            flops=0, bytes_accessed=4 * expert_in.size + 4 * expert_out.size, transcendentals=0
        ),
        name="fetch_weights",
    )(in_place(expert_in), in_place(expert_out))
    message = sum_to_owner(message, group)[0]
    totals = message[:, 2 * width :]
    message, row_x, row_cot, hidden, pre_grad = pl.pallas_call(
        expert_rows,
        in_specs=[scalar] + [in_vmem] * 3,
        out_shape=[
            jax.ShapeDtypeStruct((clips, length), f32),
            jax.ShapeDtypeStruct((clips, width), bf16),
            jax.ShapeDtypeStruct((clips, width), bf16),
            jax.ShapeDtypeStruct((clips, units), bf16),
            jax.ShapeDtypeStruct((clips, units), bf16),
        ],
        compiler_params=params,
        name="expert_rows",
    )(owned[None], message, expert_in, expert_out)
    message, hidden, row_cot = sum_to_all(message[None], group, (hidden, row_cot))
    slots = lax.dynamic_index_in_dim(message, clip, 1, keepdims=False)
    totals = lax.dynamic_index_in_dim(totals, clip, 0, keepdims=True)
    share = width // clips
    mine_x = lax.dynamic_slice_in_dim(row_x, clip * share, share, 1)
    mine_cot = lax.dynamic_slice_in_dim(row_cot, clip * share, share, 1)
    grad_expert_in = jnp.einsum("od,oh->dh", mine_x, pre_grad, preferred_element_type=f32)
    grad_expert_out = jnp.einsum("oh,od->hd", hidden, mine_cot, preferred_element_type=f32)
    score_grad, dispatch, phi_part = pl.pallas_call(
        score_grads,
        in_specs=[scalar] + [in_vmem] * 6,
        out_shape=[
            jax.ShapeDtypeStruct((experts, count), bf16),
            jax.ShapeDtypeStruct((experts, count), bf16),
            jax.ShapeDtypeStruct((experts, width), f32),
        ],
        compiler_params=params,
        name="score_grads",
    )(logit_scale, slots, totals, tok_in, tok_cot, tok_norm, exp_scores)
    phi_flat = sum(of_clips(phi_part.reshape(1, 1, -1)))
    phi_grad = sum_to_all(phi_flat, size).reshape(experts, width)
    phi_f32 = phi.astype(f32)
    phi_scale = lax.rsqrt(jnp.sum(phi_f32 * phi_f32, axis=1, keepdims=True) + epsilon)
    phi_unit = phi_f32 * phi_scale
    phi_norm = phi_unit.astype(bf16)
    slot_y = slots[:, :width].astype(bf16)
    slot_dx = slots[:, width : 2 * width].astype(bf16)
    mixed = jnp.einsum("sn,sd->nd", combine, slot_y, preferred_element_type=f32).astype(bf16)
    norm_grad = jnp.einsum("sn,sd->nd", score_grad, phi_norm, preferred_element_type=f32)
    through = jnp.einsum("sn,sd->nd", dispatch, slot_dx, preferred_element_type=f32)
    tok_unit = tok_in.astype(f32) * tok_scale
    back_norm = tok_scale * (
        norm_grad - tok_unit * jnp.sum(tok_unit * norm_grad, axis=1, keepdims=True)
    )
    grad_tokens = (through + back_norm).astype(bf16)
    grad_router = phi_scale * (
        phi_grad - phi_unit * jnp.sum(phi_unit * phi_grad, axis=1, keepdims=True)
    )
    return (mixed[None], grad_tokens[None], grad_expert_in, grad_expert_out, grad_router.T)


def solution(mesh):
    return jax.shard_map(
        per_device,
        mesh=mesh,
        in_specs=(
            P("dp", "seq", None),
            P("dp", "seq", None),
            P(),
            P(),
            P(None, "seq"),
            P("seq", None),
        ),
        out_specs=(P("dp", "seq", None), P("dp", "seq", None), P("dp", "seq"), P("seq", "dp"), P()),
        check_vma=False,
    )
```

```python
import jax
import jax.numpy as jnp
from jax import lax
from jax.experimental import pallas as pl
from jax.experimental.pallas import tpu as pltpu
from jax.sharding import PartitionSpec as P

epsilon = 1e-06
AXES = ("seq", "dp")
LANES = 128
PIECES = 4
VMEM_BYTES = 10 * 2**20
ROWS = (((1,), (1,)), ((), ()))
COLUMNS = (((0,), (0,)), ((), ()))
f32, bf16 = jnp.float32, jnp.bfloat16


def exchange(value, mask):
    clips = lax.axis_size("dp")
    pairs = []
    for place in range(lax.axis_size("seq")):
        for clip in range(clips):
            there = (place ^ mask) * clips + (clip ^ 1 if clips % 2 == 0 else clip)
            pairs.append((place * clips + clip, there))
    return lax.ppermute(value, AXES, pairs)


def hop(value, step):
    return lax.ppermute(value, "dp", [(i, i ^ step) for i in range(lax.axis_size("dp"))])


def of_clips(value):
    clips = lax.axis_size("dp")
    clip = lax.axis_index("dp")
    got = [value] + [hop(value, step) for step in range(1, clips)]
    ordered = []
    for index in range(clips):
        picked = got[0]
        for step in range(1, clips):
            picked = jnp.where(clip ^ step == index, got[step], picked)
        ordered.append(picked)
    return ordered


def rounds(size):
    masks = [1 << bit for bit in range(size.bit_length() - 1)]
    return [masks[i : i + 2] for i in range(0, len(masks), 2)]


def swaps(pair):
    return pair if len(pair) == 1 else [pair[0], pair[0] | pair[1], pair[1]]


def added(terms, masks):
    if len(masks) == 1:
        return terms[masks[0]] + terms[0]
    low, high = masks
    return (terms[0] + terms[low]) + (terms[low | high] + terms[high])


def sum_to_owner(value, group):
    place = lax.axis_index("seq")
    for pair in reversed(rounds(lax.axis_size("seq"))):
        owner_masks = [mask for mask in pair if mask >= group]
        blocks = value.reshape((1 << len(owner_masks), -1) + value.shape[1:])

        def block_for(mask):
            index = 0
            for bit, owner_mask in enumerate(owner_masks):
                index = index + jnp.where((place ^ mask) & owner_mask != 0, 1 << bit, 0)
            return lax.dynamic_index_in_dim(blocks, index, 0, keepdims=False)

        terms = {0: block_for(0)}
        for mask in swaps(pair):
            terms[mask] = exchange(block_for(mask), mask)
        value = added(terms, pair)
    return value


def round_terms(value, pair):
    terms = {0: value}
    for mask in swaps(pair):
        terms[mask] = exchange(value, mask)
    return terms


def sum_to_all(value, group, later=()):
    place = lax.axis_index("seq")
    for pair in rounds(lax.axis_size("seq")):
        terms = round_terms(value, pair)
        inner = [mask for mask in pair if mask < group]
        outer = [mask for mask in pair if mask >= group]
        if inner:
            merged = {}
            for far in [0] + outer if len(outer) == 1 else [0]:
                merged[far] = added({mask ^ far: terms[mask] for mask in terms}, inner)
            terms = merged
        value = terms[0]
        for mask in outer:
            kept = {}
            for key in terms:
                if key & mask:
                    continue
                side = lax.broadcasted_iota(jnp.int32, (2,) + (1,) * value.ndim, 0)
                same = side == jnp.where((place & mask) != 0, 1, 0)
                both = jnp.where(same, terms[key][None], terms[key | mask][None])
                kept[key] = both.reshape((-1,) + both.shape[2:])
            terms = kept
            value = terms[0]
        if later and pair[0] == 1:
            value, *later = lax.optimization_barrier((value, *later))
    return (value, *later) if later else value


def token_sums(scale_ref, phi_ref, tok_ref, cot_ref, message_ref, exp_ref, combine_ref, tok_scale_ref, norm_ref, phi_buf, tok_buf, cot_buf, phi_sem, sems):
    experts, width = phi_ref.shape
    blocks = sems.shape[1]
    rows = tok_buf.shape[0] // blocks
    pieces = [pl.ds(index * rows, rows) for index in range(blocks)]
    phi_copy = pltpu.make_async_copy(phi_ref, phi_buf, phi_sem)
    tok_copies = [
        pltpu.make_async_copy(tok_ref.at[piece], tok_buf.at[piece], sems.at[0, index])
        for index, piece in enumerate(pieces)
    ]
    cot_copies = [
        pltpu.make_async_copy(cot_ref.at[piece], cot_buf.at[piece], sems.at[1, index])
        for index, piece in enumerate(pieces)
    ]
    for copy in [phi_copy] + tok_copies + cot_copies:
        copy.start()
    phi_copy.wait()
    phi = phi_buf[...].astype(f32)
    phi_scale = lax.rsqrt(jnp.sum(phi * phi, axis=1, keepdims=True) + epsilon)
    phi_norm = (phi * phi_scale).astype(bf16)
    in_parts = 0.0
    totals = 0.0
    for copy, piece in zip(tok_copies, pieces):
        copy.wait()
        tok_in = tok_buf[piece, :]
        tok_f32 = tok_in.astype(f32)
        tok_scale = lax.rsqrt(jnp.sum(tok_f32 * tok_f32, axis=1, keepdims=True) + epsilon)
        tok_norm = (tok_f32 * tok_scale).astype(bf16)
        norm_ref[piece, :] = tok_norm
        tok_scale_ref[piece, :] = tok_scale
        logits = scale_ref[0] * lax.dot_general(phi_norm, tok_norm, ROWS, preferred_element_type=f32)
        exp_scores = jnp.exp(logits)
        exp_high = exp_scores.astype(bf16).astype(f32)
        halves = jnp.concatenate([exp_high, exp_scores - exp_high], axis=0).astype(bf16)
        in_parts += jnp.dot(halves, tok_in, preferred_element_type=f32)
        totals += jnp.sum(exp_scores, axis=1, keepdims=True)
        exp_ref[:, piece] = exp_scores
        combine_ref[:, piece] = (exp_scores / jnp.sum(exp_scores, axis=0, keepdims=True)).astype(bf16)
    message_ref[:, :width] = in_parts[:experts] + in_parts[experts:]
    spare = message_ref.shape[1] - 2 * width
    message_ref[:, 2 * width :] = jnp.broadcast_to(as_row(totals, spare), (experts, spare))
    for copy in cot_copies:
        copy.wait()
    message_ref[:, width : 2 * width] = jnp.dot(combine_ref[...], cot_buf[...], preferred_element_type=f32)


def fetch(in_ref, out_ref, in_buf, out_buf, sems):
    copies = []
    for which, (source, target) in enumerate([(in_ref, in_buf), (out_ref, out_buf)]):
        rows = source.shape[0] // sems.shape[1]
        for index in range(sems.shape[1]):
            piece = pl.ds(index * rows, rows)
            copies.append(
                pltpu.make_async_copy(source.at[piece], target.at[piece], sems.at[which, index])
            )
    for copy in copies:
        copy.start()
    for copy in copies:
        copy.wait()


def expert_rows(owned_ref, sums_ref, in_ref, out_ref, message_ref, row_x_ref, row_cot_ref, hidden_ref, pre_grad_ref):
    width, units = in_ref.shape
    spare = sums_ref[:, 2 * width :]
    lane = lax.broadcasted_iota(jnp.int32, spare.shape, 1)
    own_total = jnp.sum(jnp.where(lane == owned_ref[0], spare, 0.0), axis=1, keepdims=True)
    own_in = sums_ref[:, :width] / own_total
    row_x = own_in.astype(bf16)
    row_cot = sums_ref[:, width : 2 * width].astype(bf16)
    pre_act = jnp.dot(row_x, in_ref[...], preferred_element_type=f32)
    hid_grad = lax.dot_general(row_cot, out_ref[...], ROWS, preferred_element_type=f32)
    cdf = 0.5 * (1.0 + lax.erf(pre_act * 0.7071067811865476))
    hidden = (pre_act * cdf).astype(bf16)
    slope = cdf + pre_act * jnp.exp(-0.5 * pre_act * pre_act) * 0.3989422804014327
    pre_grad = (hid_grad * slope).astype(bf16)
    part_out = jnp.dot(hidden, out_ref[...], preferred_element_type=f32)
    part_dx = lax.dot_general(pre_grad, in_ref[...], ROWS, preferred_element_type=f32)
    message_ref[:, :width] = part_out
    message_ref[:, width : 2 * width] = part_dx
    dot_part = jnp.sum(own_in * part_dx, axis=1, keepdims=True)
    message_ref[:, 2 * width :] = jnp.broadcast_to(dot_part, spare.shape)
    row_x_ref[...] = row_x
    row_cot_ref[...] = row_cot
    hidden_ref[...] = hidden
    pre_grad_ref[...] = pre_grad


def as_row(column, lanes):
    shape = (column.shape[0], lanes)
    same = lax.broadcasted_iota(jnp.int32, shape, 0) == lax.broadcasted_iota(jnp.int32, shape, 1)
    return jnp.sum(jnp.where(same, column, 0.0), axis=0, keepdims=True)


def as_column(row, slots):
    shape = (slots, row.shape[1])
    same = lax.broadcasted_iota(jnp.int32, shape, 0) == lax.broadcasted_iota(jnp.int32, shape, 1)
    return jnp.sum(jnp.where(same, row, 0.0), axis=1, keepdims=True)


def score_grads(scale_ref, slots_ref, totals_ref, tok_ref, cot_ref, norm_ref, exp_ref, grad_ref, dispatch_ref, phi_ref):
    width = tok_ref.shape[1]
    slot_y = slots_ref[:, :width].astype(bf16)
    slot_dx = slots_ref[:, width : 2 * width].astype(bf16)
    column_stat = slots_ref[:, 2 * width : 2 * width + 1]
    totals = as_column(totals_ref[...], slot_y.shape[0])
    exp_scores = exp_ref[...]
    combine_f = exp_scores / jnp.sum(exp_scores, axis=0, keepdims=True)
    comb_dot = lax.dot_general(slot_y, cot_ref[...], ROWS, preferred_element_type=f32)
    grad_comb = combine_f * (comb_dot - jnp.sum(combine_f * comb_dot, axis=0, keepdims=True))
    disp_dot = lax.dot_general(slot_dx, tok_ref[...], ROWS, preferred_element_type=f32)
    dispatch_f = exp_scores / totals
    grad_disp = dispatch_f * (disp_dot - column_stat)
    score_grad = (scale_ref[0] * (grad_comb + grad_disp)).astype(bf16)
    phi_ref[...] = jnp.dot(score_grad, norm_ref[...], preferred_element_type=f32)
    grad_ref[...] = score_grad
    dispatch_ref[...] = dispatch_f.astype(bf16)


def finish(phi_ref, *refs):
    *term_refs, grad_ref = refs
    own, *others = [ref[0] for ref in term_refs]
    phi_grad = own + others[-1]
    if len(others) > 1:
        phi_grad = phi_grad + (others[0] + others[1])
    phi = phi_ref[...].astype(f32)
    phi_scale = lax.rsqrt(jnp.sum(phi * phi, axis=1, keepdims=True) + epsilon)
    phi_unit = phi * phi_scale
    along = jnp.sum(phi_unit * phi_grad, axis=1, keepdims=True)
    grad_ref[...] = phi_scale * (phi_grad - phi_unit * along)


def in_place(operand):
    return pltpu.with_memory_space_constraint(operand, pltpu.HBM)


def per_device(tokens, cotangent, router, logit_scale, expert_in, expert_out):
    tok_in = tokens[0]
    tok_cot = cotangent[0]
    count = tok_in.shape[0]
    width, experts = router.shape
    units = expert_in.shape[1]
    size = lax.axis_size("seq")
    group = size // experts
    clips = lax.axis_size("dp")
    clip = lax.axis_index("dp")
    owned = lax.axis_index("seq") // group
    length = 2 * width + -(-experts // LANES) * LANES
    scalar = pl.BlockSpec(memory_space=pltpu.SMEM)
    in_vmem = pl.BlockSpec(memory_space=pltpu.VMEM)
    in_hbm = pl.BlockSpec(memory_space=pltpu.HBM)
    params = pltpu.CompilerParams(vmem_limit_bytes=VMEM_BYTES)
    phi = router.T
    message, exp_scores, combine, tok_scale, tok_norm = pl.pallas_call(
        token_sums,
        in_specs=[scalar, in_hbm, in_hbm, in_hbm],
        out_shape=[
            jax.ShapeDtypeStruct((experts, length), f32),
            jax.ShapeDtypeStruct((experts, count), f32),
            jax.ShapeDtypeStruct((experts, count), bf16),
            jax.ShapeDtypeStruct((count, 1), f32),
            jax.ShapeDtypeStruct((count, width), bf16),
        ],
        scratch_shapes=[
            pltpu.VMEM((experts, width), bf16),
            pltpu.VMEM((count, width), bf16),
            pltpu.VMEM((count, width), bf16),
            pltpu.SemaphoreType.DMA,
            pltpu.SemaphoreType.DMA((2, 2)),
        ],
        compiler_params=params,
        name="token_sums",
    )(logit_scale, in_place(phi), in_place(tok_in), in_place(tok_cot))
    message = jnp.stack(of_clips(message), axis=1)
    message, expert_in, expert_out = lax.optimization_barrier((message, expert_in, expert_out))
    expert_in, expert_out = pl.pallas_call(
        fetch,
        in_specs=[in_hbm] * 2,
        out_specs=[in_vmem] * 2,
        out_shape=[
            jax.ShapeDtypeStruct(expert_in.shape, bf16),
            jax.ShapeDtypeStruct(expert_out.shape, bf16),
        ],
        scratch_shapes=[pltpu.SemaphoreType.DMA((2, PIECES))],
        compiler_params=params,
        cost_estimate=pl.CostEstimate(
            flops=0, bytes_accessed=4 * expert_in.size + 4 * expert_out.size, transcendentals=0
        ),
        name="fetch_weights",
    )(in_place(expert_in), in_place(expert_out))
    message = sum_to_owner(message, group)[0]
    totals = message[:, 2 * width :]
    message, row_x, row_cot, hidden, pre_grad = pl.pallas_call(
        expert_rows,
        in_specs=[scalar] + [in_vmem] * 3,
        out_shape=[
            jax.ShapeDtypeStruct((clips, length), f32),
            jax.ShapeDtypeStruct((clips, width), bf16),
            jax.ShapeDtypeStruct((clips, width), bf16),
            jax.ShapeDtypeStruct((clips, units), bf16),
            jax.ShapeDtypeStruct((clips, units), bf16),
        ],
        compiler_params=params,
        name="expert_rows",
    )(owned[None], message, expert_in, expert_out)
    message, hidden, row_cot = sum_to_all(message[None], group, (hidden, row_cot))
    slots = lax.dynamic_index_in_dim(message, clip, 1, keepdims=False)
    totals = lax.dynamic_index_in_dim(totals, clip, 0, keepdims=True)
    share = width // clips
    mine_x = lax.dynamic_slice_in_dim(row_x, clip * share, share, 1)
    mine_cot = lax.dynamic_slice_in_dim(row_cot, clip * share, share, 1)
    grad_expert_in = jnp.einsum("od,oh->dh", mine_x, pre_grad, preferred_element_type=f32)
    grad_expert_out = jnp.einsum("oh,od->hd", hidden, mine_cot, preferred_element_type=f32)
    score_grad, dispatch, phi_part = pl.pallas_call(
        score_grads,
        in_specs=[scalar] + [in_vmem] * 6,
        out_shape=[
            jax.ShapeDtypeStruct((experts, count), bf16),
            jax.ShapeDtypeStruct((experts, count), bf16),
            jax.ShapeDtypeStruct((experts, width), f32),
        ],
        compiler_params=params,
        name="score_grads",
    )(logit_scale, slots, totals, tok_in, tok_cot, tok_norm, exp_scores)
    phi_sum = sum(of_clips(phi_part[None]))
    *earlier, final = rounds(size)
    for pair in earlier:
        phi_sum = added(round_terms(phi_sum, pair), pair)
    terms = round_terms(phi_sum, final)
    grad_router = pl.pallas_call(
        finish,
        in_specs=[in_vmem] * (1 + len(terms)),
        out_shape=jax.ShapeDtypeStruct((experts, width), f32),
        compiler_params=params,
        name="finish",
    )(phi, terms.pop(0), *[terms[mask] for mask in sorted(terms, reverse=True)])
    phi_f32 = phi.astype(f32)
    phi_scale = lax.rsqrt(jnp.sum(phi_f32 * phi_f32, axis=1, keepdims=True) + epsilon)
    phi_unit = phi_f32 * phi_scale
    phi_norm = phi_unit.astype(bf16)
    slot_y = slots[:, :width].astype(bf16)
    slot_dx = slots[:, width : 2 * width].astype(bf16)
    mixed = jnp.einsum("sn,sd->nd", combine, slot_y, preferred_element_type=f32).astype(bf16)
    norm_grad = jnp.einsum("sn,sd->nd", score_grad, phi_norm, preferred_element_type=f32)
    through = jnp.einsum("sn,sd->nd", dispatch, slot_dx, preferred_element_type=f32)
    tok_unit = tok_in.astype(f32) * tok_scale
    back_norm = tok_scale * (
        norm_grad - tok_unit * jnp.sum(tok_unit * norm_grad, axis=1, keepdims=True)
    )
    grad_tokens = (through + back_norm).astype(bf16)
    return (mixed[None], grad_tokens[None], grad_expert_in, grad_expert_out, grad_router.T)


def solution(mesh):
    return jax.shard_map(
        per_device,
        mesh=mesh,
        in_specs=(
            P("dp", "seq", None),
            P("dp", "seq", None),
            P(),
            P(),
            P(None, "seq"),
            P("seq", None),
        ),
        out_specs=(P("dp", "seq", None), P("dp", "seq", None), P("dp", "seq"), P("seq", "dp"), P()),
        check_vma=False,
    )
```

```python
import jax
import jax.numpy as jnp
from jax import lax
from jax.experimental import pallas as pl
from jax.experimental.pallas import tpu as pltpu
from jax.sharding import PartitionSpec as P

epsilon = 1e-06
AXES = ("seq", "dp")
LANES = 128
PIECES = 4
VMEM_BYTES = 10 * 2**20
ROWS = (((1,), (1,)), ((), ()))
COLUMNS = (((0,), (0,)), ((), ()))
f32, bf16 = jnp.float32, jnp.bfloat16


def exchange(value, mask):
    clips = lax.axis_size("dp")
    pairs = []
    for place in range(lax.axis_size("seq")):
        for clip in range(clips):
            there = (place ^ mask) * clips + (clip ^ 1 if clips % 2 == 0 else clip)
            pairs.append((place * clips + clip, there))
    return lax.ppermute(value, AXES, pairs)


def hop(value, step):
    return lax.ppermute(value, "dp", [(i, i ^ step) for i in range(lax.axis_size("dp"))])


def of_clips(value):
    clips = lax.axis_size("dp")
    clip = lax.axis_index("dp")
    got = [value] + [hop(value, step) for step in range(1, clips)]
    ordered = []
    for index in range(clips):
        picked = got[0]
        for step in range(1, clips):
            picked = jnp.where(clip ^ step == index, got[step], picked)
        ordered.append(picked)
    return ordered


def rounds(size):
    masks = [1 << bit for bit in range(size.bit_length() - 1)]
    return [masks[i : i + 2] for i in range(0, len(masks), 2)]


def swaps(pair):
    return pair if len(pair) == 1 else [pair[0], pair[0] | pair[1], pair[1]]


def added(terms, masks):
    if len(masks) == 1:
        return terms[masks[0]] + terms[0]
    low, high = masks
    return (terms[0] + terms[low]) + (terms[low | high] + terms[high])


def sum_to_owner(value, group):
    place = lax.axis_index("seq")
    for pair in reversed(rounds(lax.axis_size("seq"))):
        owner_masks = [mask for mask in pair if mask >= group]
        blocks = value.reshape((1 << len(owner_masks), -1) + value.shape[1:])

        def block_for(mask):
            index = 0
            for bit, owner_mask in enumerate(owner_masks):
                index = index + jnp.where((place ^ mask) & owner_mask != 0, 1 << bit, 0)
            return lax.dynamic_index_in_dim(blocks, index, 0, keepdims=False)

        terms = {0: block_for(0)}
        for mask in swaps(pair):
            terms[mask] = exchange(block_for(mask), mask)
        value = added(terms, pair)
    return value


def round_terms(value, pair):
    terms = {0: value}
    for mask in swaps(pair):
        terms[mask] = exchange(value, mask)
    return terms


def sum_to_all(value, group, later=()):
    place = lax.axis_index("seq")
    for pair in rounds(lax.axis_size("seq")):
        terms = round_terms(value, pair)
        inner = [mask for mask in pair if mask < group]
        outer = [mask for mask in pair if mask >= group]
        if inner:
            merged = {}
            for far in [0] + outer if len(outer) == 1 else [0]:
                merged[far] = added({mask ^ far: terms[mask] for mask in terms}, inner)
            terms = merged
        value = terms[0]
        for mask in outer:
            kept = {}
            for key in terms:
                if key & mask:
                    continue
                side = lax.broadcasted_iota(jnp.int32, (2,) + (1,) * value.ndim, 0)
                same = side == jnp.where((place & mask) != 0, 1, 0)
                both = jnp.where(same, terms[key][None], terms[key | mask][None])
                kept[key] = both.reshape((-1,) + both.shape[2:])
            terms = kept
            value = terms[0]
        if later and pair[0] == 1:
            value, *later = lax.optimization_barrier((value, *later))
    return (value, *later) if later else value


def token_sums(scale_ref, phi_ref, tok_ref, cot_ref, message_ref, exp_ref, combine_ref, tok_scale_ref, norm_ref, phi_buf, tok_buf, cot_buf, phi_sem, sems):
    experts, width = phi_ref.shape
    blocks = sems.shape[1]
    rows = tok_buf.shape[0] // blocks
    pieces = [pl.ds(index * rows, rows) for index in range(blocks)]
    phi_copy = pltpu.make_async_copy(phi_ref, phi_buf, phi_sem)
    tok_copies = [
        pltpu.make_async_copy(tok_ref.at[piece], tok_buf.at[piece], sems.at[0, index])
        for index, piece in enumerate(pieces)
    ]
    cot_copies = [
        pltpu.make_async_copy(cot_ref.at[piece], cot_buf.at[piece], sems.at[1, index])
        for index, piece in enumerate(pieces)
    ]
    for copy in [phi_copy] + tok_copies:
        copy.start()
    phi_copy.wait()
    phi = phi_buf[...].astype(f32)
    phi_scale = lax.rsqrt(jnp.sum(phi * phi, axis=1, keepdims=True) + epsilon)
    phi_norm = (phi * phi_scale).astype(bf16)
    for tok_copy, cot_copy, piece in zip(tok_copies, cot_copies, pieces):
        tok_copy.wait()
        cot_copy.start()
        tok_f32 = tok_buf[piece, :].astype(f32)
        tok_scale = lax.rsqrt(jnp.sum(tok_f32 * tok_f32, axis=1, keepdims=True) + epsilon)
        norm_ref[piece, :] = (tok_f32 * tok_scale).astype(bf16)
        tok_scale_ref[piece, :] = tok_scale
    logits = scale_ref[0] * lax.dot_general(phi_norm, norm_ref[...], ROWS, preferred_element_type=f32)
    exp_scores = jnp.exp(logits)
    combine = (exp_scores / jnp.sum(exp_scores, axis=0, keepdims=True)).astype(bf16)
    exp_high = exp_scores.astype(bf16).astype(f32)
    halves = jnp.concatenate([exp_high, exp_scores - exp_high], axis=0).astype(bf16)
    in_parts = jnp.dot(halves, tok_buf[...], preferred_element_type=f32)
    message_ref[:, :width] = in_parts[:experts] + in_parts[experts:]
    spare = message_ref.shape[1] - 2 * width
    total = as_row(jnp.sum(exp_scores, axis=1, keepdims=True), spare)
    message_ref[:, 2 * width :] = jnp.broadcast_to(total, (experts, spare))
    exp_ref[...] = exp_scores
    combine_ref[...] = combine
    for copy in cot_copies:
        copy.wait()
    message_ref[:, width : 2 * width] = jnp.dot(combine, cot_buf[...], preferred_element_type=f32)


def fetch(in_ref, out_ref, in_buf, out_buf, sems):
    copies = []
    for which, (source, target) in enumerate([(in_ref, in_buf), (out_ref, out_buf)]):
        rows = source.shape[0] // sems.shape[1]
        for index in range(sems.shape[1]):
            piece = pl.ds(index * rows, rows)
            copies.append(
                pltpu.make_async_copy(source.at[piece], target.at[piece], sems.at[which, index])
            )
    for copy in copies:
        copy.start()
    for copy in copies:
        copy.wait()


def expert_rows(owned_ref, sums_ref, in_ref, out_ref, message_ref, row_x_ref, row_cot_ref, hidden_ref, pre_grad_ref):
    width, units = in_ref.shape
    spare = sums_ref[:, 2 * width :]
    lane = lax.broadcasted_iota(jnp.int32, spare.shape, 1)
    own_total = jnp.sum(jnp.where(lane == owned_ref[0], spare, 0.0), axis=1, keepdims=True)
    own_in = sums_ref[:, :width] / own_total
    row_x = own_in.astype(bf16)
    row_cot = sums_ref[:, width : 2 * width].astype(bf16)
    pre_act = jnp.dot(row_x, in_ref[...], preferred_element_type=f32)
    hid_grad = lax.dot_general(row_cot, out_ref[...], ROWS, preferred_element_type=f32)
    cdf = 0.5 * (1.0 + lax.erf(pre_act * 0.7071067811865476))
    hidden = (pre_act * cdf).astype(bf16)
    slope = cdf + pre_act * jnp.exp(-0.5 * pre_act * pre_act) * 0.3989422804014327
    pre_grad = (hid_grad * slope).astype(bf16)
    part_out = jnp.dot(hidden, out_ref[...], preferred_element_type=f32)
    part_dx = lax.dot_general(pre_grad, in_ref[...], ROWS, preferred_element_type=f32)
    message_ref[:, :width] = part_out
    message_ref[:, width : 2 * width] = part_dx
    dot_part = jnp.sum(own_in * part_dx, axis=1, keepdims=True)
    message_ref[:, 2 * width :] = jnp.broadcast_to(dot_part, spare.shape)
    row_x_ref[...] = row_x
    row_cot_ref[...] = row_cot
    hidden_ref[...] = hidden
    pre_grad_ref[...] = pre_grad


def as_row(column, lanes):
    shape = (column.shape[0], lanes)
    same = lax.broadcasted_iota(jnp.int32, shape, 0) == lax.broadcasted_iota(jnp.int32, shape, 1)
    return jnp.sum(jnp.where(same, column, 0.0), axis=0, keepdims=True)


def as_column(row, slots):
    shape = (slots, row.shape[1])
    same = lax.broadcasted_iota(jnp.int32, shape, 0) == lax.broadcasted_iota(jnp.int32, shape, 1)
    return jnp.sum(jnp.where(same, row, 0.0), axis=1, keepdims=True)


def score_grads(scale_ref, slots_ref, totals_ref, tok_ref, cot_ref, norm_ref, exp_ref, grad_ref, dispatch_ref, phi_ref):
    width = tok_ref.shape[1]
    slot_y = slots_ref[:, :width].astype(bf16)
    slot_dx = slots_ref[:, width : 2 * width].astype(bf16)
    column_stat = slots_ref[:, 2 * width : 2 * width + 1]
    totals = as_column(totals_ref[...], slot_y.shape[0])
    exp_scores = exp_ref[...]
    combine_f = exp_scores / jnp.sum(exp_scores, axis=0, keepdims=True)
    comb_dot = lax.dot_general(slot_y, cot_ref[...], ROWS, preferred_element_type=f32)
    grad_comb = combine_f * (comb_dot - jnp.sum(combine_f * comb_dot, axis=0, keepdims=True))
    disp_dot = lax.dot_general(slot_dx, tok_ref[...], ROWS, preferred_element_type=f32)
    dispatch_f = exp_scores / totals
    grad_disp = dispatch_f * (disp_dot - column_stat)
    score_grad = (scale_ref[0] * (grad_comb + grad_disp)).astype(bf16)
    phi_ref[...] = jnp.dot(score_grad, norm_ref[...], preferred_element_type=f32)
    grad_ref[...] = score_grad
    dispatch_ref[...] = dispatch_f.astype(bf16)


def finish(phi_ref, *refs):
    *term_refs, grad_ref = refs
    own, *others = [ref[0] for ref in term_refs]
    phi_grad = own + others[-1]
    if len(others) > 1:
        phi_grad = phi_grad + (others[0] + others[1])
    phi = phi_ref[...].astype(f32)
    phi_scale = lax.rsqrt(jnp.sum(phi * phi, axis=1, keepdims=True) + epsilon)
    phi_unit = phi * phi_scale
    along = jnp.sum(phi_unit * phi_grad, axis=1, keepdims=True)
    grad_ref[...] = phi_scale * (phi_grad - phi_unit * along)


def in_place(operand):
    return pltpu.with_memory_space_constraint(operand, pltpu.HBM)


def per_device(tokens, cotangent, router, logit_scale, expert_in, expert_out):
    tok_in = tokens[0]
    tok_cot = cotangent[0]
    count = tok_in.shape[0]
    width, experts = router.shape
    units = expert_in.shape[1]
    size = lax.axis_size("seq")
    group = size // experts
    clips = lax.axis_size("dp")
    clip = lax.axis_index("dp")
    owned = lax.axis_index("seq") // group
    length = 2 * width + -(-experts // LANES) * LANES
    scalar = pl.BlockSpec(memory_space=pltpu.SMEM)
    in_vmem = pl.BlockSpec(memory_space=pltpu.VMEM)
    in_hbm = pl.BlockSpec(memory_space=pltpu.HBM)
    params = pltpu.CompilerParams(vmem_limit_bytes=VMEM_BYTES)
    phi = router.T
    message, exp_scores, combine, tok_scale, tok_norm = pl.pallas_call(
        token_sums,
        in_specs=[scalar, in_hbm, in_hbm, in_hbm],
        out_shape=[
            jax.ShapeDtypeStruct((experts, length), f32),
            jax.ShapeDtypeStruct((experts, count), f32),
            jax.ShapeDtypeStruct((experts, count), bf16),
            jax.ShapeDtypeStruct((count, 1), f32),
            jax.ShapeDtypeStruct((count, width), bf16),
        ],
        scratch_shapes=[
            pltpu.VMEM((experts, width), bf16),
            pltpu.VMEM((count, width), bf16),
            pltpu.VMEM((count, width), bf16),
            pltpu.SemaphoreType.DMA,
            pltpu.SemaphoreType.DMA((2, PIECES)),
        ],
        compiler_params=params,
        name="token_sums",
    )(logit_scale, in_place(phi), in_place(tok_in), in_place(tok_cot))
    message = jnp.stack(of_clips(message), axis=1)
    message, expert_in, expert_out = lax.optimization_barrier((message, expert_in, expert_out))
    expert_in, expert_out = pl.pallas_call(
        fetch,
        in_specs=[in_hbm] * 2,
        out_specs=[in_vmem] * 2,
        out_shape=[
            jax.ShapeDtypeStruct(expert_in.shape, bf16),
            jax.ShapeDtypeStruct(expert_out.shape, bf16),
        ],
        scratch_shapes=[pltpu.SemaphoreType.DMA((2, PIECES))],
        compiler_params=params,
        cost_estimate=pl.CostEstimate(
            flops=0, bytes_accessed=4 * expert_in.size + 4 * expert_out.size, transcendentals=0
        ),
        name="fetch_weights",
    )(in_place(expert_in), in_place(expert_out))
    message = sum_to_owner(message, group)[0]
    totals = message[:, 2 * width :]
    message, row_x, row_cot, hidden, pre_grad = pl.pallas_call(
        expert_rows,
        in_specs=[scalar] + [in_vmem] * 3,
        out_shape=[
            jax.ShapeDtypeStruct((clips, length), f32),
            jax.ShapeDtypeStruct((clips, width), bf16),
            jax.ShapeDtypeStruct((clips, width), bf16),
            jax.ShapeDtypeStruct((clips, units), bf16),
            jax.ShapeDtypeStruct((clips, units), bf16),
        ],
        compiler_params=params,
        name="expert_rows",
    )(owned[None], message, expert_in, expert_out)
    message, hidden, row_cot = sum_to_all(message[None], group, (hidden, row_cot))
    slots = lax.dynamic_index_in_dim(message, clip, 1, keepdims=False)
    totals = lax.dynamic_index_in_dim(totals, clip, 0, keepdims=True)
    share = width // clips
    mine_x = lax.dynamic_slice_in_dim(row_x, clip * share, share, 1)
    mine_cot = lax.dynamic_slice_in_dim(row_cot, clip * share, share, 1)
    grad_expert_in = jnp.einsum("od,oh->dh", mine_x, pre_grad, preferred_element_type=f32)
    grad_expert_out = jnp.einsum("oh,od->hd", hidden, mine_cot, preferred_element_type=f32)
    score_grad, dispatch, phi_part = pl.pallas_call(
        score_grads,
        in_specs=[scalar] + [in_vmem] * 6,
        out_shape=[
            jax.ShapeDtypeStruct((experts, count), bf16),
            jax.ShapeDtypeStruct((experts, count), bf16),
            jax.ShapeDtypeStruct((experts, width), f32),
        ],
        compiler_params=params,
        name="score_grads",
    )(logit_scale, slots, totals, tok_in, tok_cot, tok_norm, exp_scores)
    phi_sum = sum(of_clips(phi_part[None]))
    *earlier, final = rounds(size)
    for pair in earlier:
        phi_sum = added(round_terms(phi_sum, pair), pair)
    terms = round_terms(phi_sum, final)
    grad_router = pl.pallas_call(
        finish,
        in_specs=[in_vmem] * (1 + len(terms)),
        out_shape=jax.ShapeDtypeStruct((experts, width), f32),
        compiler_params=params,
        name="finish",
    )(phi, terms.pop(0), *[terms[mask] for mask in sorted(terms, reverse=True)])
    phi_f32 = phi.astype(f32)
    phi_scale = lax.rsqrt(jnp.sum(phi_f32 * phi_f32, axis=1, keepdims=True) + epsilon)
    phi_unit = phi_f32 * phi_scale
    phi_norm = phi_unit.astype(bf16)
    slot_y = slots[:, :width].astype(bf16)
    slot_dx = slots[:, width : 2 * width].astype(bf16)
    mixed = jnp.einsum("sn,sd->nd", combine, slot_y, preferred_element_type=f32).astype(bf16)
    norm_grad = jnp.einsum("sn,sd->nd", score_grad, phi_norm, preferred_element_type=f32)
    through = jnp.einsum("sn,sd->nd", dispatch, slot_dx, preferred_element_type=f32)
    tok_unit = tok_in.astype(f32) * tok_scale
    back_norm = tok_scale * (
        norm_grad - tok_unit * jnp.sum(tok_unit * norm_grad, axis=1, keepdims=True)
    )
    grad_tokens = (through + back_norm).astype(bf16)
    return (mixed[None], grad_tokens[None], grad_expert_in, grad_expert_out, grad_router.T)


def solution(mesh):
    return jax.shard_map(
        per_device,
        mesh=mesh,
        in_specs=(
            P("dp", "seq", None),
            P("dp", "seq", None),
            P(),
            P(),
            P(None, "seq"),
            P("seq", None),
        ),
        out_specs=(P("dp", "seq", None), P("dp", "seq", None), P("dp", "seq"), P("seq", "dp"), P()),
        check_vma=False,
    )
```

```python
import jax
import jax.numpy as jnp
from jax import lax
from jax.experimental import pallas as pl
from jax.experimental.pallas import tpu as pltpu
from jax.sharding import PartitionSpec as P

epsilon = 1e-06
AXES = ("seq", "dp")
LANES = 128
PIECES = 4
VMEM_BYTES = 10 * 2**20
ROWS = (((1,), (1,)), ((), ()))
COLUMNS = (((0,), (0,)), ((), ()))
f32, bf16 = jnp.float32, jnp.bfloat16


def exchange(value, mask):
    clips = lax.axis_size("dp")
    pairs = []
    for place in range(lax.axis_size("seq")):
        for clip in range(clips):
            there = (place ^ mask) * clips + (clip ^ 1 if clips % 2 == 0 else clip)
            pairs.append((place * clips + clip, there))
    return lax.ppermute(value, AXES, pairs)


def hop(value, step):
    return lax.ppermute(value, "dp", [(i, i ^ step) for i in range(lax.axis_size("dp"))])


def of_clips(value):
    clips = lax.axis_size("dp")
    clip = lax.axis_index("dp")
    got = [value] + [hop(value, step) for step in range(1, clips)]
    ordered = []
    for index in range(clips):
        picked = got[0]
        for step in range(1, clips):
            picked = jnp.where(clip ^ step == index, got[step], picked)
        ordered.append(picked)
    return ordered


def rounds(size):
    masks = [1 << bit for bit in range(size.bit_length() - 1)]
    return [masks[i : i + 2] for i in range(0, len(masks), 2)]


def swaps(pair):
    return pair if len(pair) == 1 else [pair[0], pair[0] | pair[1], pair[1]]


def added(terms, masks):
    if len(masks) == 1:
        return terms[masks[0]] + terms[0]
    low, high = masks
    return (terms[0] + terms[low]) + (terms[low | high] + terms[high])


def sum_to_owner(value, group):
    place = lax.axis_index("seq")
    for pair in reversed(rounds(lax.axis_size("seq"))):
        owner_masks = [mask for mask in pair if mask >= group]
        blocks = value.reshape((1 << len(owner_masks), -1) + value.shape[1:])

        def block_for(mask):
            index = 0
            for bit, owner_mask in enumerate(owner_masks):
                index = index + jnp.where((place ^ mask) & owner_mask != 0, 1 << bit, 0)
            return lax.dynamic_index_in_dim(blocks, index, 0, keepdims=False)

        terms = {0: block_for(0)}
        for mask in swaps(pair):
            terms[mask] = exchange(block_for(mask), mask)
        value = added(terms, pair)
    return value


def round_terms(value, pair):
    terms = {0: value}
    for mask in swaps(pair):
        terms[mask] = exchange(value, mask)
    return terms


def sum_to_all(value, group, later=()):
    place = lax.axis_index("seq")
    for pair in rounds(lax.axis_size("seq")):
        terms = round_terms(value, pair)
        inner = [mask for mask in pair if mask < group]
        outer = [mask for mask in pair if mask >= group]
        if inner:
            merged = {}
            for far in [0] + outer if len(outer) == 1 else [0]:
                merged[far] = added({mask ^ far: terms[mask] for mask in terms}, inner)
            terms = merged
        value = terms[0]
        for mask in outer:
            kept = {}
            for key in terms:
                if key & mask:
                    continue
                side = lax.broadcasted_iota(jnp.int32, (2,) + (1,) * value.ndim, 0)
                same = side == jnp.where((place & mask) != 0, 1, 0)
                both = jnp.where(same, terms[key][None], terms[key | mask][None])
                kept[key] = both.reshape((-1,) + both.shape[2:])
            terms = kept
            value = terms[0]
        if later and pair[0] == 1:
            value, *later = lax.optimization_barrier((value, *later))
    return (value, *later) if later else value


def token_sums(scale_ref, phi_ref, tok_ref, cot_ref, message_ref, exp_ref, combine_ref, tok_scale_ref, norm_ref, phi_buf, tok_buf, cot_buf, phi_sem, sems):
    experts, width = phi_ref.shape
    blocks = sems.shape[1]
    rows = tok_buf.shape[0] // blocks
    pieces = [pl.ds(index * rows, rows) for index in range(blocks)]
    phi_copy = pltpu.make_async_copy(phi_ref, phi_buf, phi_sem)
    tok_copies = [
        pltpu.make_async_copy(tok_ref.at[piece], tok_buf.at[piece], sems.at[0, index])
        for index, piece in enumerate(pieces)
    ]
    cot_copies = [
        pltpu.make_async_copy(cot_ref.at[piece], cot_buf.at[piece], sems.at[1, index])
        for index, piece in enumerate(pieces)
    ]
    for copy in tok_copies + [phi_copy] + cot_copies:
        copy.start()
    for copy, piece in zip(tok_copies, pieces):
        copy.wait()
        tok_f32 = tok_buf[piece, :].astype(f32)
        tok_scale = lax.rsqrt(jnp.sum(tok_f32 * tok_f32, axis=1, keepdims=True) + epsilon)
        norm_ref[piece, :] = (tok_f32 * tok_scale).astype(bf16)
        tok_scale_ref[piece, :] = tok_scale
    phi_copy.wait()
    phi = phi_buf[...].astype(f32)
    phi_scale = lax.rsqrt(jnp.sum(phi * phi, axis=1, keepdims=True) + epsilon)
    phi_norm = (phi * phi_scale).astype(bf16)
    logits = scale_ref[0] * lax.dot_general(phi_norm, norm_ref[...], ROWS, preferred_element_type=f32)
    exp_scores = jnp.exp(logits)
    combine = (exp_scores / jnp.sum(exp_scores, axis=0, keepdims=True)).astype(bf16)
    exp_high = exp_scores.astype(bf16).astype(f32)
    halves = jnp.concatenate([exp_high, exp_scores - exp_high], axis=0).astype(bf16)
    in_parts = jnp.dot(halves, tok_buf[...], preferred_element_type=f32)
    message_ref[:, :width] = in_parts[:experts] + in_parts[experts:]
    spare = message_ref.shape[1] - 2 * width
    total = as_row(jnp.sum(exp_scores, axis=1, keepdims=True), spare)
    message_ref[:, 2 * width :] = jnp.broadcast_to(total, (experts, spare))
    exp_ref[...] = exp_scores
    combine_ref[...] = combine
    for copy in cot_copies:
        copy.wait()
    message_ref[:, width : 2 * width] = jnp.dot(combine, cot_buf[...], preferred_element_type=f32)


def fetch(in_ref, out_ref, in_buf, out_buf, sems):
    copies = []
    for which, (source, target) in enumerate([(in_ref, in_buf), (out_ref, out_buf)]):
        rows = source.shape[0] // sems.shape[1]
        for index in range(sems.shape[1]):
            piece = pl.ds(index * rows, rows)
            copies.append(
                pltpu.make_async_copy(source.at[piece], target.at[piece], sems.at[which, index])
            )
    for copy in copies:
        copy.start()
    for copy in copies:
        copy.wait()


def expert_rows(owned_ref, sums_ref, in_ref, out_ref, message_ref, row_x_ref, row_cot_ref, hidden_ref, pre_grad_ref):
    width, units = in_ref.shape
    spare = sums_ref[:, 2 * width :]
    lane = lax.broadcasted_iota(jnp.int32, spare.shape, 1)
    own_total = jnp.sum(jnp.where(lane == owned_ref[0], spare, 0.0), axis=1, keepdims=True)
    own_in = sums_ref[:, :width] / own_total
    row_x = own_in.astype(bf16)
    row_cot = sums_ref[:, width : 2 * width].astype(bf16)
    pre_act = jnp.dot(row_x, in_ref[...], preferred_element_type=f32)
    hid_grad = lax.dot_general(row_cot, out_ref[...], ROWS, preferred_element_type=f32)
    cdf = 0.5 * (1.0 + lax.erf(pre_act * 0.7071067811865476))
    hidden = (pre_act * cdf).astype(bf16)
    slope = cdf + pre_act * jnp.exp(-0.5 * pre_act * pre_act) * 0.3989422804014327
    pre_grad = (hid_grad * slope).astype(bf16)
    part_out = jnp.dot(hidden, out_ref[...], preferred_element_type=f32)
    part_dx = lax.dot_general(pre_grad, in_ref[...], ROWS, preferred_element_type=f32)
    message_ref[:, :width] = part_out
    message_ref[:, width : 2 * width] = part_dx
    dot_part = jnp.sum(own_in * part_dx, axis=1, keepdims=True)
    message_ref[:, 2 * width :] = jnp.broadcast_to(dot_part, spare.shape)
    row_x_ref[...] = row_x
    row_cot_ref[...] = row_cot
    hidden_ref[...] = hidden
    pre_grad_ref[...] = pre_grad


def as_row(column, lanes):
    shape = (column.shape[0], lanes)
    same = lax.broadcasted_iota(jnp.int32, shape, 0) == lax.broadcasted_iota(jnp.int32, shape, 1)
    return jnp.sum(jnp.where(same, column, 0.0), axis=0, keepdims=True)


def as_column(row, slots):
    shape = (slots, row.shape[1])
    same = lax.broadcasted_iota(jnp.int32, shape, 0) == lax.broadcasted_iota(jnp.int32, shape, 1)
    return jnp.sum(jnp.where(same, row, 0.0), axis=1, keepdims=True)


def score_grads(scale_ref, slots_ref, totals_ref, tok_ref, cot_ref, norm_ref, exp_ref, grad_ref, dispatch_ref, phi_ref):
    width = tok_ref.shape[1]
    slot_y = slots_ref[:, :width].astype(bf16)
    slot_dx = slots_ref[:, width : 2 * width].astype(bf16)
    column_stat = slots_ref[:, 2 * width : 2 * width + 1]
    totals = as_column(totals_ref[...], slot_y.shape[0])
    exp_scores = exp_ref[...]
    combine_f = exp_scores / jnp.sum(exp_scores, axis=0, keepdims=True)
    comb_dot = lax.dot_general(slot_y, cot_ref[...], ROWS, preferred_element_type=f32)
    grad_comb = combine_f * (comb_dot - jnp.sum(combine_f * comb_dot, axis=0, keepdims=True))
    disp_dot = lax.dot_general(slot_dx, tok_ref[...], ROWS, preferred_element_type=f32)
    dispatch_f = exp_scores / totals
    grad_disp = dispatch_f * (disp_dot - column_stat)
    score_grad = (scale_ref[0] * (grad_comb + grad_disp)).astype(bf16)
    phi_ref[...] = jnp.dot(score_grad, norm_ref[...], preferred_element_type=f32)
    grad_ref[...] = score_grad
    dispatch_ref[...] = dispatch_f.astype(bf16)


def finish(phi_ref, *refs):
    *term_refs, grad_ref = refs
    own, *others = [ref[0] for ref in term_refs]
    phi_grad = own + others[-1]
    if len(others) > 1:
        phi_grad = phi_grad + (others[0] + others[1])
    phi = phi_ref[...].astype(f32)
    phi_scale = lax.rsqrt(jnp.sum(phi * phi, axis=1, keepdims=True) + epsilon)
    phi_unit = phi * phi_scale
    along = jnp.sum(phi_unit * phi_grad, axis=1, keepdims=True)
    grad_ref[...] = phi_scale * (phi_grad - phi_unit * along)


def in_place(operand):
    return pltpu.with_memory_space_constraint(operand, pltpu.HBM)


def per_device(tokens, cotangent, router, logit_scale, expert_in, expert_out):
    tok_in = tokens[0]
    tok_cot = cotangent[0]
    count = tok_in.shape[0]
    width, experts = router.shape
    units = expert_in.shape[1]
    size = lax.axis_size("seq")
    group = size // experts
    clips = lax.axis_size("dp")
    clip = lax.axis_index("dp")
    owned = lax.axis_index("seq") // group
    length = 2 * width + -(-experts // LANES) * LANES
    scalar = pl.BlockSpec(memory_space=pltpu.SMEM)
    in_vmem = pl.BlockSpec(memory_space=pltpu.VMEM)
    in_hbm = pl.BlockSpec(memory_space=pltpu.HBM)
    params = pltpu.CompilerParams(vmem_limit_bytes=VMEM_BYTES)
    phi = router.T
    message, exp_scores, combine, tok_scale, tok_norm = pl.pallas_call(
        token_sums,
        in_specs=[scalar, in_hbm, in_hbm, in_hbm],
        out_shape=[
            jax.ShapeDtypeStruct((experts, length), f32),
            jax.ShapeDtypeStruct((experts, count), f32),
            jax.ShapeDtypeStruct((experts, count), bf16),
            jax.ShapeDtypeStruct((count, 1), f32),
            jax.ShapeDtypeStruct((count, width), bf16),
        ],
        scratch_shapes=[
            pltpu.VMEM((experts, width), bf16),
            pltpu.VMEM((count, width), bf16),
            pltpu.VMEM((count, width), bf16),
            pltpu.SemaphoreType.DMA,
            pltpu.SemaphoreType.DMA((2, PIECES)),
        ],
        compiler_params=params,
        name="token_sums",
    )(logit_scale, in_place(phi), in_place(tok_in), in_place(tok_cot))
    message = jnp.stack(of_clips(message), axis=1)
    message, expert_in, expert_out = lax.optimization_barrier((message, expert_in, expert_out))
    expert_in, expert_out = pl.pallas_call(
        fetch,
        in_specs=[in_hbm] * 2,
        out_specs=[in_vmem] * 2,
        out_shape=[
            jax.ShapeDtypeStruct(expert_in.shape, bf16),
            jax.ShapeDtypeStruct(expert_out.shape, bf16),
        ],
        scratch_shapes=[pltpu.SemaphoreType.DMA((2, PIECES))],
        compiler_params=params,
        cost_estimate=pl.CostEstimate(
            flops=0, bytes_accessed=4 * expert_in.size + 4 * expert_out.size, transcendentals=0
        ),
        name="fetch_weights",
    )(in_place(expert_in), in_place(expert_out))
    message = sum_to_owner(message, group)[0]
    totals = message[:, 2 * width :]
    message, row_x, row_cot, hidden, pre_grad = pl.pallas_call(
        expert_rows,
        in_specs=[scalar] + [in_vmem] * 3,
        out_shape=[
            jax.ShapeDtypeStruct((clips, length), f32),
            jax.ShapeDtypeStruct((clips, width), bf16),
            jax.ShapeDtypeStruct((clips, width), bf16),
            jax.ShapeDtypeStruct((clips, units), bf16),
            jax.ShapeDtypeStruct((clips, units), bf16),
        ],
        compiler_params=params,
        name="expert_rows",
    )(owned[None], message, expert_in, expert_out)
    message, hidden, row_cot = sum_to_all(message[None], group, (hidden, row_cot))
    slots = lax.dynamic_index_in_dim(message, clip, 1, keepdims=False)
    totals = lax.dynamic_index_in_dim(totals, clip, 0, keepdims=True)
    share = width // clips
    mine_x = lax.dynamic_slice_in_dim(row_x, clip * share, share, 1)
    mine_cot = lax.dynamic_slice_in_dim(row_cot, clip * share, share, 1)
    grad_expert_in = jnp.einsum("od,oh->dh", mine_x, pre_grad, preferred_element_type=f32)
    grad_expert_out = jnp.einsum("oh,od->hd", hidden, mine_cot, preferred_element_type=f32)
    score_grad, dispatch, phi_part = pl.pallas_call(
        score_grads,
        in_specs=[scalar] + [in_vmem] * 6,
        out_shape=[
            jax.ShapeDtypeStruct((experts, count), bf16),
            jax.ShapeDtypeStruct((experts, count), bf16),
            jax.ShapeDtypeStruct((experts, width), f32),
        ],
        compiler_params=params,
        name="score_grads",
    )(logit_scale, slots, totals, tok_in, tok_cot, tok_norm, exp_scores)
    phi_sum = sum(of_clips(phi_part[None]))
    *earlier, final = rounds(size)
    for pair in earlier:
        phi_sum = added(round_terms(phi_sum, pair), pair)
    terms = round_terms(phi_sum, final)
    grad_router = pl.pallas_call(
        finish,
        in_specs=[in_vmem] * (1 + len(terms)),
        out_shape=jax.ShapeDtypeStruct((experts, width), f32),
        compiler_params=params,
        name="finish",
    )(phi, terms.pop(0), *[terms[mask] for mask in sorted(terms, reverse=True)])
    phi_f32 = phi.astype(f32)
    phi_scale = lax.rsqrt(jnp.sum(phi_f32 * phi_f32, axis=1, keepdims=True) + epsilon)
    phi_unit = phi_f32 * phi_scale
    phi_norm = phi_unit.astype(bf16)
    slot_y = slots[:, :width].astype(bf16)
    slot_dx = slots[:, width : 2 * width].astype(bf16)
    mixed = jnp.einsum("sn,sd->nd", combine, slot_y, preferred_element_type=f32).astype(bf16)
    norm_grad = jnp.einsum("sn,sd->nd", score_grad, phi_norm, preferred_element_type=f32)
    through = jnp.einsum("sn,sd->nd", dispatch, slot_dx, preferred_element_type=f32)
    tok_unit = tok_in.astype(f32) * tok_scale
    back_norm = tok_scale * (
        norm_grad - tok_unit * jnp.sum(tok_unit * norm_grad, axis=1, keepdims=True)
    )
    grad_tokens = (through + back_norm).astype(bf16)
    return (mixed[None], grad_tokens[None], grad_expert_in, grad_expert_out, grad_router.T)


def solution(mesh):
    return jax.shard_map(
        per_device,
        mesh=mesh,
        in_specs=(
            P("dp", "seq", None),
            P("dp", "seq", None),
            P(),
            P(),
            P(None, "seq"),
            P("seq", None),
        ),
        out_specs=(P("dp", "seq", None), P("dp", "seq", None), P("dp", "seq"), P("seq", "dp"), P()),
        check_vma=False,
    )
```

```python
import jax
import jax.numpy as jnp
from jax import lax
from jax.experimental import pallas as pl
from jax.experimental.pallas import tpu as pltpu
from jax.sharding import PartitionSpec as P

epsilon = 1e-06
AXES = ("seq", "dp")
LANES = 128
PIECES = 4
VMEM_BYTES = 10 * 2**20
ROWS = (((1,), (1,)), ((), ()))
COLUMNS = (((0,), (0,)), ((), ()))
f32, bf16 = jnp.float32, jnp.bfloat16


def exchange(value, mask):
    clips = lax.axis_size("dp")
    pairs = []
    for place in range(lax.axis_size("seq")):
        for clip in range(clips):
            there = (place ^ mask) * clips + (clip ^ 1 if clips % 2 == 0 else clip)
            pairs.append((place * clips + clip, there))
    return lax.ppermute(value, AXES, pairs)


def hop(value, step):
    return lax.ppermute(value, "dp", [(i, i ^ step) for i in range(lax.axis_size("dp"))])


def of_clips(value):
    clips = lax.axis_size("dp")
    clip = lax.axis_index("dp")
    got = [value] + [hop(value, step) for step in range(1, clips)]
    ordered = []
    for index in range(clips):
        picked = got[0]
        for step in range(1, clips):
            picked = jnp.where(clip ^ step == index, got[step], picked)
        ordered.append(picked)
    return ordered


def rounds(size):
    masks = [1 << bit for bit in range(size.bit_length() - 1)]
    return [masks[i : i + 2] for i in range(0, len(masks), 2)]


def narrow(value):
    lane = lax.broadcasted_iota(jnp.int32, value.shape, value.ndim - 1)
    lost = value - lax.reduce_precision(value, 8, 7)
    return jnp.where(lane < value.shape[-1] - LANES, value, lost).astype(bf16)


def swaps(pair):
    return pair if len(pair) == 1 else [pair[0], pair[0] | pair[1], pair[1]]


def added(terms, masks):
    if len(masks) == 1:
        return terms[masks[0]] + terms[0]
    low, high = masks
    return (terms[0] + terms[low]) + (terms[low | high] + terms[high])


def sum_to_owner(value, group):
    place = lax.axis_index("seq")
    for pair in reversed(rounds(lax.axis_size("seq"))):
        owner_masks = [mask for mask in pair if mask >= group]
        blocks = value.reshape((1 << len(owner_masks), -1) + value.shape[1:])

        def block_for(mask):
            index = 0
            for bit, owner_mask in enumerate(owner_masks):
                index = index + jnp.where((place ^ mask) & owner_mask != 0, 1 << bit, 0)
            return lax.dynamic_index_in_dim(blocks, index, 0, keepdims=False)

        terms = {0: block_for(0)}
        for mask in swaps(pair):
            terms[mask] = exchange(block_for(mask), mask)
        value = added({mask: term.astype(f32) for mask, term in terms.items()}, pair)
    return value


def round_terms(value, pair):
    terms = {0: value}
    for mask in swaps(pair):
        terms[mask] = exchange(value, mask)
    return terms


def sum_to_all(value, group, later=()):
    place = lax.axis_index("seq")
    for pair in rounds(lax.axis_size("seq")):
        terms = round_terms(value if pair[0] == 1 else narrow(value), pair)
        terms = {mask: term.astype(f32) for mask, term in terms.items()}
        inner = [mask for mask in pair if mask < group]
        outer = [mask for mask in pair if mask >= group]
        if inner:
            merged = {}
            for far in [0] + outer if len(outer) == 1 else [0]:
                merged[far] = added({mask ^ far: terms[mask] for mask in terms}, inner)
            terms = merged
        value = terms[0]
        for mask in outer:
            kept = {}
            for key in terms:
                if key & mask:
                    continue
                side = lax.broadcasted_iota(jnp.int32, (2,) + (1,) * value.ndim, 0)
                same = side == jnp.where((place & mask) != 0, 1, 0)
                both = jnp.where(same, terms[key][None], terms[key | mask][None])
                kept[key] = both.reshape((-1,) + both.shape[2:])
            terms = kept
            value = terms[0]
        if later and pair[0] == 1:
            value, *later = lax.optimization_barrier((value, *later))
    return (value, *later) if later else value


def token_sums(scale_ref, phi_ref, tok_ref, cot_ref, message_ref, exp_ref, combine_ref, tok_scale_ref, norm_ref, phi_buf, tok_buf, cot_buf, phi_sem, sems):
    experts, width = phi_ref.shape
    blocks = sems.shape[1]
    rows = tok_buf.shape[0] // blocks
    pieces = [pl.ds(index * rows, rows) for index in range(blocks)]
    phi_copy = pltpu.make_async_copy(phi_ref, phi_buf, phi_sem)
    tok_copies = [
        pltpu.make_async_copy(tok_ref.at[piece], tok_buf.at[piece], sems.at[0, index])
        for index, piece in enumerate(pieces)
    ]
    cot_copies = [
        pltpu.make_async_copy(cot_ref.at[piece], cot_buf.at[piece], sems.at[1, index])
        for index, piece in enumerate(pieces)
    ]
    for copy in tok_copies + [phi_copy] + cot_copies:
        copy.start()
    for copy, piece in zip(tok_copies, pieces):
        copy.wait()
        tok_f32 = tok_buf[piece, :].astype(f32)
        tok_scale = lax.rsqrt(jnp.sum(tok_f32 * tok_f32, axis=1, keepdims=True) + epsilon)
        norm_ref[piece, :] = (tok_f32 * tok_scale).astype(bf16)
        tok_scale_ref[piece, :] = tok_scale
    phi_copy.wait()
    phi = phi_buf[...].astype(f32)
    phi_scale = lax.rsqrt(jnp.sum(phi * phi, axis=1, keepdims=True) + epsilon)
    phi_norm = (phi * phi_scale).astype(bf16)
    logits = scale_ref[0] * lax.dot_general(phi_norm, norm_ref[...], ROWS, preferred_element_type=f32)
    exp_scores = jnp.exp(logits)
    combine = (exp_scores / jnp.sum(exp_scores, axis=0, keepdims=True)).astype(bf16)
    exp_high = exp_scores.astype(bf16).astype(f32)
    halves = jnp.concatenate([exp_high, exp_scores - exp_high], axis=0).astype(bf16)
    in_parts = jnp.dot(halves, tok_buf[...], preferred_element_type=f32)
    message_ref[:, :width] = (in_parts[:experts] + in_parts[experts:]).astype(bf16)
    total = as_row(jnp.sum(exp_scores, axis=1, keepdims=True), LANES)
    high = total.astype(bf16).astype(f32)
    total = jnp.concatenate([high, total - high], axis=1).astype(bf16)
    message_ref[:, 2 * width :] = jnp.broadcast_to(total, (experts, 2 * LANES))
    exp_ref[...] = exp_scores
    combine_ref[...] = combine
    for copy in cot_copies:
        copy.wait()
    cot_part = jnp.dot(combine, cot_buf[...], preferred_element_type=f32)
    message_ref[:, width : 2 * width] = cot_part.astype(bf16)


def fetch(in_ref, out_ref, in_buf, out_buf, sems):
    copies = []
    for which, (source, target) in enumerate([(in_ref, in_buf), (out_ref, out_buf)]):
        rows = source.shape[0] // sems.shape[1]
        for index in range(sems.shape[1]):
            piece = pl.ds(index * rows, rows)
            copies.append(
                pltpu.make_async_copy(source.at[piece], target.at[piece], sems.at[which, index])
            )
    for copy in copies:
        copy.start()
    for copy in copies:
        copy.wait()


def expert_rows(owned_ref, sums_ref, in_ref, out_ref, message_ref, totals_ref, row_x_ref, row_cot_ref, hidden_ref, pre_grad_ref):
    width, units = in_ref.shape
    totals = sums_ref[:, 2 * width : 2 * width + LANES] + sums_ref[:, 2 * width + LANES :]
    lane = lax.broadcasted_iota(jnp.int32, totals.shape, 1)
    own_total = jnp.sum(jnp.where(lane == owned_ref[0], totals, 0.0), axis=1, keepdims=True)
    own_in = sums_ref[:, :width] / own_total
    row_x = own_in.astype(bf16)
    row_cot = sums_ref[:, width : 2 * width].astype(bf16)
    pre_act = jnp.dot(row_x, in_ref[...], preferred_element_type=f32)
    hid_grad = lax.dot_general(row_cot, out_ref[...], ROWS, preferred_element_type=f32)
    cdf = 0.5 * (1.0 + lax.erf(pre_act * 0.7071067811865476))
    hidden = (pre_act * cdf).astype(bf16)
    slope = cdf + pre_act * jnp.exp(-0.5 * pre_act * pre_act) * 0.3989422804014327
    pre_grad = (hid_grad * slope).astype(bf16)
    part_out = jnp.dot(hidden, out_ref[...], preferred_element_type=f32)
    part_dx = lax.dot_general(pre_grad, in_ref[...], ROWS, preferred_element_type=f32)
    message_ref[:, :width] = part_out
    message_ref[:, width : 2 * width] = part_dx
    dot_part = jnp.sum(own_in * part_dx, axis=1, keepdims=True)
    message_ref[:, 2 * width :] = jnp.broadcast_to(dot_part, (totals.shape[0], 2 * LANES))
    totals_ref[...] = totals
    row_x_ref[...] = row_x
    row_cot_ref[...] = row_cot
    hidden_ref[...] = hidden
    pre_grad_ref[...] = pre_grad


def as_row(column, lanes):
    shape = (column.shape[0], lanes)
    same = lax.broadcasted_iota(jnp.int32, shape, 0) == lax.broadcasted_iota(jnp.int32, shape, 1)
    return jnp.sum(jnp.where(same, column, 0.0), axis=0, keepdims=True)


def as_column(row, slots):
    shape = (slots, row.shape[1])
    same = lax.broadcasted_iota(jnp.int32, shape, 0) == lax.broadcasted_iota(jnp.int32, shape, 1)
    return jnp.sum(jnp.where(same, row, 0.0), axis=1, keepdims=True)


def score_grads(scale_ref, slots_ref, totals_ref, tok_ref, cot_ref, norm_ref, exp_ref, grad_ref, dispatch_ref, phi_ref):
    width = tok_ref.shape[1]
    slot_y = slots_ref[:, :width].astype(bf16)
    slot_dx = slots_ref[:, width : 2 * width].astype(bf16)
    low = 2 * width + LANES
    column_stat = slots_ref[:, 2 * width : 2 * width + 1] + slots_ref[:, low : low + 1]
    totals = as_column(totals_ref[...], slot_y.shape[0])
    exp_scores = exp_ref[...]
    combine_f = exp_scores / jnp.sum(exp_scores, axis=0, keepdims=True)
    comb_dot = lax.dot_general(slot_y, cot_ref[...], ROWS, preferred_element_type=f32)
    grad_comb = combine_f * (comb_dot - jnp.sum(combine_f * comb_dot, axis=0, keepdims=True))
    disp_dot = lax.dot_general(slot_dx, tok_ref[...], ROWS, preferred_element_type=f32)
    dispatch_f = exp_scores / totals
    grad_disp = dispatch_f * (disp_dot - column_stat)
    score_grad = (scale_ref[0] * (grad_comb + grad_disp)).astype(bf16)
    phi_ref[...] = jnp.dot(score_grad, norm_ref[...], preferred_element_type=f32)
    grad_ref[...] = score_grad
    dispatch_ref[...] = dispatch_f.astype(bf16)


def mix(slots_ref, combine_ref, mixed_ref):
    slot_y = slots_ref[:, : mixed_ref.shape[1]].astype(bf16)
    mixed_ref[...] = lax.dot_general(
        combine_ref[...], slot_y, COLUMNS, preferred_element_type=f32
    ).astype(bf16)


def token_grads(phi_ref, slots_ref, grad_ref, dispatch_ref, scale_ref, tok_ref, out_ref):
    width = tok_ref.shape[1]
    phi = phi_ref[...].astype(f32)
    phi_scale = lax.rsqrt(jnp.sum(phi * phi, axis=1, keepdims=True) + epsilon)
    phi_norm = (phi * phi_scale).astype(bf16)
    slot_dx = slots_ref[:, width : 2 * width].astype(bf16)
    norm_grad = lax.dot_general(grad_ref[...], phi_norm, COLUMNS, preferred_element_type=f32)
    through = lax.dot_general(dispatch_ref[...], slot_dx, COLUMNS, preferred_element_type=f32)
    tok_scale = scale_ref[...]
    tok_unit = tok_ref[...].astype(f32) * tok_scale
    along = jnp.sum(tok_unit * norm_grad, axis=1, keepdims=True)
    out_ref[...] = (through + tok_scale * (norm_grad - tok_unit * along)).astype(bf16)


def finish(phi_ref, *refs):
    *term_refs, grad_ref = refs
    own, *others = [ref[0] for ref in term_refs]
    phi_grad = own + others[-1]
    if len(others) > 1:
        phi_grad = phi_grad + (others[0] + others[1])
    phi = phi_ref[...].astype(f32)
    phi_scale = lax.rsqrt(jnp.sum(phi * phi, axis=1, keepdims=True) + epsilon)
    phi_unit = phi * phi_scale
    along = jnp.sum(phi_unit * phi_grad, axis=1, keepdims=True)
    grad_ref[...] = phi_scale * (phi_grad - phi_unit * along)


def in_place(operand):
    return pltpu.with_memory_space_constraint(operand, pltpu.HBM)


def per_device(tokens, cotangent, router, logit_scale, expert_in, expert_out):
    tok_in = tokens[0]
    tok_cot = cotangent[0]
    count = tok_in.shape[0]
    width, experts = router.shape
    units = expert_in.shape[1]
    size = lax.axis_size("seq")
    group = size // experts
    clips = lax.axis_size("dp")
    clip = lax.axis_index("dp")
    owned = lax.axis_index("seq") // group
    length = 2 * width + 2 * LANES
    scalar = pl.BlockSpec(memory_space=pltpu.SMEM)
    in_vmem = pl.BlockSpec(memory_space=pltpu.VMEM)
    in_hbm = pl.BlockSpec(memory_space=pltpu.HBM)
    params = pltpu.CompilerParams(vmem_limit_bytes=VMEM_BYTES)
    phi = router.T
    message, exp_scores, combine, tok_scale, tok_norm = pl.pallas_call(
        token_sums,
        in_specs=[scalar, in_hbm, in_hbm, in_hbm],
        out_shape=[
            jax.ShapeDtypeStruct((experts, length), bf16),
            jax.ShapeDtypeStruct((experts, count), f32),
            jax.ShapeDtypeStruct((experts, count), bf16),
            jax.ShapeDtypeStruct((count, 1), f32),
            jax.ShapeDtypeStruct((count, width), bf16),
        ],
        scratch_shapes=[
            pltpu.VMEM((experts, width), bf16),
            pltpu.VMEM((count, width), bf16),
            pltpu.VMEM((count, width), bf16),
            pltpu.SemaphoreType.DMA,
            pltpu.SemaphoreType.DMA((2, PIECES)),
        ],
        compiler_params=params,
        name="token_sums",
    )(logit_scale, in_place(phi), in_place(tok_in), in_place(tok_cot))
    message = jnp.stack(of_clips(message), axis=1)
    message, expert_in, expert_out = lax.optimization_barrier((message, expert_in, expert_out))
    expert_in, expert_out = pl.pallas_call(
        fetch,
        in_specs=[in_hbm] * 2,
        out_specs=[in_vmem] * 2,
        out_shape=[
            jax.ShapeDtypeStruct(expert_in.shape, bf16),
            jax.ShapeDtypeStruct(expert_out.shape, bf16),
        ],
        scratch_shapes=[pltpu.SemaphoreType.DMA((2, PIECES))],
        compiler_params=params,
        cost_estimate=pl.CostEstimate(
            flops=0, bytes_accessed=4 * expert_in.size + 4 * expert_out.size, transcendentals=0
        ),
        name="fetch_weights",
    )(in_place(expert_in), in_place(expert_out))
    message = sum_to_owner(message, group)[0]
    message, totals, row_x, row_cot, hidden, pre_grad = pl.pallas_call(
        expert_rows,
        in_specs=[scalar] + [in_vmem] * 3,
        out_shape=[
            jax.ShapeDtypeStruct((clips, length), f32),
            jax.ShapeDtypeStruct((clips, LANES), f32),
            jax.ShapeDtypeStruct((clips, width), bf16),
            jax.ShapeDtypeStruct((clips, width), bf16),
            jax.ShapeDtypeStruct((clips, units), bf16),
            jax.ShapeDtypeStruct((clips, units), bf16),
        ],
        compiler_params=params,
        name="expert_rows",
    )(owned[None], message, expert_in, expert_out)
    share = width // clips
    mine_x = lax.dynamic_slice_in_dim(row_x, clip * share, share, 1)
    grad_expert_in = jnp.einsum("od,oh->dh", mine_x, pre_grad, preferred_element_type=f32)
    message, grad_expert_in, hidden, row_cot = sum_to_all(
        message[None], group, (grad_expert_in, hidden, row_cot)
    )
    mine_cot = lax.dynamic_slice_in_dim(row_cot, clip * share, share, 1)
    grad_expert_out = jnp.einsum("oh,od->hd", hidden, mine_cot, preferred_element_type=f32)
    message, grad_expert_out = lax.optimization_barrier((message, grad_expert_out))
    slots = lax.dynamic_index_in_dim(message, clip, 1, keepdims=False)
    totals = lax.dynamic_index_in_dim(totals, clip, 0, keepdims=True)
    score_grad, dispatch, phi_part = pl.pallas_call(
        score_grads,
        in_specs=[scalar] + [in_vmem] * 6,
        out_shape=[
            jax.ShapeDtypeStruct((experts, count), bf16),
            jax.ShapeDtypeStruct((experts, count), bf16),
            jax.ShapeDtypeStruct((experts, width), f32),
        ],
        compiler_params=params,
        name="score_grads",
    )(logit_scale, slots, totals, tok_in, tok_cot, tok_norm, exp_scores)
    rows = count // PIECES
    whole = [pl.BlockSpec(shape, lambda i: (0, 0)) for shape in [(experts, width), (experts, length)]]
    of_slots = pl.BlockSpec((experts, rows), lambda i: (0, i))
    of_tokens = [pl.BlockSpec((rows, last), lambda i: (i, 0)) for last in (1, width)]
    token_shape = jax.ShapeDtypeStruct((count, width), bf16)
    phi_sum = sum(of_clips(phi_part[None]))
    mixed = pl.pallas_call(
        mix,
        grid=(PIECES,),
        in_specs=[whole[1], of_slots],
        out_specs=of_tokens[1],
        out_shape=token_shape,
        compiler_params=params,
        cost_estimate=pl.CostEstimate(
            flops=2 * experts * tok_in.size, bytes_accessed=2 * tok_in.size, transcendentals=0
        ),
        name="mix",
    )(slots, combine)
    phi_sum, mixed, score_grad, dispatch = lax.optimization_barrier(
        (phi_sum, mixed, score_grad, dispatch)
    )
    grad_tokens = pl.pallas_call(
        token_grads,
        grid=(PIECES,),
        in_specs=[*whole, of_slots, of_slots, *of_tokens],
        out_specs=of_tokens[1],
        out_shape=token_shape,
        compiler_params=params,
        cost_estimate=pl.CostEstimate(
            flops=4 * experts * tok_in.size, bytes_accessed=4 * tok_in.size, transcendentals=0
        ),
        name="token_grads",
    )(phi, slots, score_grad, dispatch, tok_scale, tok_in)
    *earlier, final = rounds(size)
    for pair in earlier:
        phi_sum = added(round_terms(phi_sum, pair), pair)
    phi_sum, grad_tokens = lax.optimization_barrier((phi_sum, grad_tokens))
    terms = round_terms(phi_sum, final)
    grad_router = pl.pallas_call(
        finish,
        in_specs=[in_vmem] * (1 + len(terms)),
        out_shape=jax.ShapeDtypeStruct((experts, width), f32),
        compiler_params=params,
        name="finish",
    )(phi, terms.pop(0), *[terms[mask] for mask in sorted(terms, reverse=True)])
    return (mixed[None], grad_tokens[None], grad_expert_in, grad_expert_out, grad_router.T)


def solution(mesh):
    return jax.shard_map(
        per_device,
        mesh=mesh,
        in_specs=(
            P("dp", "seq", None),
            P("dp", "seq", None),
            P(),
            P(),
            P(None, "seq"),
            P("seq", None),
        ),
        out_specs=(P("dp", "seq", None), P("dp", "seq", None), P("dp", "seq"), P("seq", "dp"), P()),
        check_vma=False,
    )
```

```python
import jax
import jax.numpy as jnp
from jax import lax
from jax.experimental import pallas as pl
from jax.experimental.pallas import tpu as pltpu
from jax.sharding import PartitionSpec as P

epsilon = 1e-06
AXES = ("seq", "dp")
LANES = 128
PIECES = 4
VMEM_BYTES = 10 * 2**20
ROWS = (((1,), (1,)), ((), ()))
COLUMNS = (((0,), (0,)), ((), ()))
f32, bf16 = jnp.float32, jnp.bfloat16


def exchange(value, mask):
    clips = lax.axis_size("dp")
    pairs = []
    for place in range(lax.axis_size("seq")):
        for clip in range(clips):
            there = (place ^ mask) * clips + (clip ^ 1 if clips % 2 == 0 else clip)
            pairs.append((place * clips + clip, there))
    return lax.ppermute(value, AXES, pairs)


def hop(value, step):
    return lax.ppermute(value, "dp", [(i, i ^ step) for i in range(lax.axis_size("dp"))])


def of_clips(value):
    clips = lax.axis_size("dp")
    apart = lax.broadcasted_iota(jnp.int32, (1, clips, 1), 1) ^ lax.axis_index("dp")
    merged = value[:, None]
    for step in range(1, clips):
        merged = jnp.where(apart == step, hop(value, step)[:, None], merged)
    return merged


def rounds(size):
    masks = [1 << bit for bit in range(size.bit_length() - 1)]
    return [masks[i : i + 2] for i in range(0, len(masks), 2)]


def narrow(value):
    lane = lax.broadcasted_iota(jnp.int32, value.shape, value.ndim - 1)
    lost = value - lax.reduce_precision(value, 8, 7)
    return jnp.where(lane < value.shape[-1] - LANES, value, lost).astype(bf16)


def swaps(pair):
    return pair if len(pair) == 1 else [pair[0], pair[0] | pair[1], pair[1]]


def added(terms, masks):
    if len(masks) == 1:
        return terms[masks[0]] + terms[0]
    low, high = masks
    return (terms[0] + terms[low]) + (terms[low | high] + terms[high])


def sum_to_owner(value, group):
    place = lax.axis_index("seq")
    for pair in reversed(rounds(lax.axis_size("seq"))):
        owner_masks = [mask for mask in pair if mask >= group]
        blocks = value.reshape((1 << len(owner_masks), -1) + value.shape[1:])

        def block_for(mask):
            index = 0
            for bit, owner_mask in enumerate(owner_masks):
                index = index + jnp.where((place ^ mask) & owner_mask != 0, 1 << bit, 0)
            return lax.dynamic_index_in_dim(blocks, index, 0, keepdims=False)

        terms = {0: block_for(0)}
        for mask in swaps(pair):
            terms[mask] = exchange(block_for(mask), mask)
        value = added({mask: term.astype(f32) for mask, term in terms.items()}, pair)
    return value


def round_terms(value, pair):
    terms = {0: value}
    for mask in swaps(pair):
        terms[mask] = exchange(value, mask)
    return terms


def sum_to_all(value, group, later=()):
    place = lax.axis_index("seq")
    for pair in rounds(lax.axis_size("seq")):
        terms = round_terms(value if pair[0] == 1 else narrow(value), pair)
        terms = {mask: term.astype(f32) for mask, term in terms.items()}
        inner = [mask for mask in pair if mask < group]
        outer = [mask for mask in pair if mask >= group]
        if inner:
            merged = {}
            for far in [0] + outer if len(outer) == 1 else [0]:
                merged[far] = added({mask ^ far: terms[mask] for mask in terms}, inner)
            terms = merged
        value = terms[0]
        for mask in outer:
            kept = {}
            for key in terms:
                if key & mask:
                    continue
                side = lax.broadcasted_iota(jnp.int32, (2,) + (1,) * value.ndim, 0)
                same = side == jnp.where((place & mask) != 0, 1, 0)
                both = jnp.where(same, terms[key][None], terms[key | mask][None])
                kept[key] = both.reshape((-1,) + both.shape[2:])
            terms = kept
            value = terms[0]
        if later and pair[0] == 1:
            value, *later = lax.optimization_barrier((value, *later))
    return (value, *later) if later else value


def token_sums(scale_ref, phi_ref, tok_ref, cot_ref, message_ref, exp_ref, combine_ref, tok_scale_ref, norm_ref, phi_buf, tok_buf, cot_buf, phi_sem, sems):
    experts, width = phi_ref.shape
    blocks = sems.shape[1]
    rows = tok_buf.shape[0] // blocks
    pieces = [pl.ds(index * rows, rows) for index in range(blocks)]
    phi_copy = pltpu.make_async_copy(phi_ref, phi_buf, phi_sem)
    tok_copies = [
        pltpu.make_async_copy(tok_ref.at[piece], tok_buf.at[piece], sems.at[0, index])
        for index, piece in enumerate(pieces)
    ]
    cot_copies = [
        pltpu.make_async_copy(cot_ref.at[piece], cot_buf.at[piece], sems.at[1, index])
        for index, piece in enumerate(pieces)
    ]
    for copy in tok_copies + [phi_copy] + cot_copies:
        copy.start()
    for copy, piece in zip(tok_copies, pieces):
        copy.wait()
        tok_f32 = tok_buf[piece, :].astype(f32)
        tok_scale = lax.rsqrt(jnp.sum(tok_f32 * tok_f32, axis=1, keepdims=True) + epsilon)
        norm_ref[piece, :] = (tok_f32 * tok_scale).astype(bf16)
        tok_scale_ref[piece, :] = tok_scale
    phi_copy.wait()
    phi = phi_buf[...].astype(f32)
    phi_scale = lax.rsqrt(jnp.sum(phi * phi, axis=1, keepdims=True) + epsilon)
    phi_norm = (phi * phi_scale).astype(bf16)
    logits = scale_ref[0] * lax.dot_general(phi_norm, norm_ref[...], ROWS, preferred_element_type=f32)
    exp_scores = jnp.exp(logits)
    combine = (exp_scores / jnp.sum(exp_scores, axis=0, keepdims=True)).astype(bf16)
    exp_high = exp_scores.astype(bf16).astype(f32)
    halves = jnp.concatenate([exp_high, exp_scores - exp_high], axis=0).astype(bf16)
    in_parts = jnp.dot(halves, tok_buf[...], preferred_element_type=f32)
    message_ref[:, :width] = (in_parts[:experts] + in_parts[experts:]).astype(bf16)
    total = as_row(jnp.sum(exp_scores, axis=1, keepdims=True), LANES)
    high = total.astype(bf16).astype(f32)
    total = jnp.concatenate([high, total - high], axis=1).astype(bf16)
    message_ref[:, 2 * width :] = jnp.broadcast_to(total, (experts, 2 * LANES))
    exp_ref[...] = exp_scores
    combine_ref[...] = combine
    for copy in cot_copies:
        copy.wait()
    cot_part = jnp.dot(combine, cot_buf[...], preferred_element_type=f32)
    message_ref[:, width : 2 * width] = cot_part.astype(bf16)


def fetch(in_ref, out_ref, in_buf, out_buf, sems):
    copies = []
    for which, (source, target) in enumerate([(in_ref, in_buf), (out_ref, out_buf)]):
        rows = source.shape[0] // sems.shape[1]
        for index in range(sems.shape[1]):
            piece = pl.ds(index * rows, rows)
            copies.append(
                pltpu.make_async_copy(source.at[piece], target.at[piece], sems.at[which, index])
            )
    for copy in copies:
        copy.start()
    for copy in copies:
        copy.wait()


def expert_rows(owned_ref, sums_ref, in_ref, out_ref, message_ref, totals_ref, row_x_ref, row_cot_ref, hidden_ref, pre_grad_ref):
    width, units = in_ref.shape
    totals = sums_ref[:, 2 * width : 2 * width + LANES] + sums_ref[:, 2 * width + LANES :]
    lane = lax.broadcasted_iota(jnp.int32, totals.shape, 1)
    own_total = jnp.sum(jnp.where(lane == owned_ref[0], totals, 0.0), axis=1, keepdims=True)
    own_in = sums_ref[:, :width] / own_total
    row_x = own_in.astype(bf16)
    row_cot = sums_ref[:, width : 2 * width].astype(bf16)
    pre_act = jnp.dot(row_x, in_ref[...], preferred_element_type=f32)
    hid_grad = lax.dot_general(row_cot, out_ref[...], ROWS, preferred_element_type=f32)
    cdf = 0.5 * (1.0 + lax.erf(pre_act * 0.7071067811865476))
    hidden = (pre_act * cdf).astype(bf16)
    slope = cdf + pre_act * jnp.exp(-0.5 * pre_act * pre_act) * 0.3989422804014327
    pre_grad = (hid_grad * slope).astype(bf16)
    part_out = jnp.dot(hidden, out_ref[...], preferred_element_type=f32)
    part_dx = lax.dot_general(pre_grad, in_ref[...], ROWS, preferred_element_type=f32)
    message_ref[:, :width] = part_out
    message_ref[:, width : 2 * width] = part_dx
    dot_part = jnp.sum(own_in * part_dx, axis=1, keepdims=True)
    message_ref[:, 2 * width :] = jnp.broadcast_to(dot_part, (totals.shape[0], 2 * LANES))
    totals_ref[...] = totals
    row_x_ref[...] = row_x
    row_cot_ref[...] = row_cot
    hidden_ref[...] = hidden
    pre_grad_ref[...] = pre_grad


def as_row(column, lanes):
    shape = (column.shape[0], lanes)
    same = lax.broadcasted_iota(jnp.int32, shape, 0) == lax.broadcasted_iota(jnp.int32, shape, 1)
    return jnp.sum(jnp.where(same, column, 0.0), axis=0, keepdims=True)


def as_column(row, slots):
    shape = (slots, row.shape[1])
    same = lax.broadcasted_iota(jnp.int32, shape, 0) == lax.broadcasted_iota(jnp.int32, shape, 1)
    return jnp.sum(jnp.where(same, row, 0.0), axis=1, keepdims=True)


def score_grads(scale_ref, slots_ref, totals_ref, tok_ref, cot_ref, norm_ref, exp_ref, grad_ref, dispatch_ref, phi_ref):
    width = tok_ref.shape[1]
    slot_y = slots_ref[:, :width].astype(bf16)
    slot_dx = slots_ref[:, width : 2 * width].astype(bf16)
    low = 2 * width + LANES
    column_stat = slots_ref[:, 2 * width : 2 * width + 1] + slots_ref[:, low : low + 1]
    totals = as_column(totals_ref[...], slot_y.shape[0])
    exp_scores = exp_ref[...]
    combine_f = exp_scores / jnp.sum(exp_scores, axis=0, keepdims=True)
    comb_dot = lax.dot_general(slot_y, cot_ref[...], ROWS, preferred_element_type=f32)
    grad_comb = combine_f * (comb_dot - jnp.sum(combine_f * comb_dot, axis=0, keepdims=True))
    disp_dot = lax.dot_general(slot_dx, tok_ref[...], ROWS, preferred_element_type=f32)
    dispatch_f = exp_scores / totals
    grad_disp = dispatch_f * (disp_dot - column_stat)
    score_grad = (scale_ref[0] * (grad_comb + grad_disp)).astype(bf16)
    phi_ref[...] = jnp.dot(score_grad, norm_ref[...], preferred_element_type=f32)
    grad_ref[...] = score_grad
    dispatch_ref[...] = dispatch_f.astype(bf16)


def finish(phi_ref, *refs):
    *term_refs, grad_ref = refs
    own, *others = [ref[0] for ref in term_refs]
    phi_grad = own + others[-1]
    if len(others) > 1:
        phi_grad = phi_grad + (others[0] + others[1])
    phi = phi_ref[...].astype(f32)
    phi_scale = lax.rsqrt(jnp.sum(phi * phi, axis=1, keepdims=True) + epsilon)
    phi_unit = phi * phi_scale
    along = jnp.sum(phi_unit * phi_grad, axis=1, keepdims=True)
    grad_ref[...] = phi_scale * (phi_grad - phi_unit * along)


def in_place(operand):
    return pltpu.with_memory_space_constraint(operand, pltpu.HBM)


def per_device(tokens, cotangent, router, logit_scale, expert_in, expert_out):
    tok_in = tokens[0]
    tok_cot = cotangent[0]
    count = tok_in.shape[0]
    width, experts = router.shape
    units = expert_in.shape[1]
    size = lax.axis_size("seq")
    group = size // experts
    clips = lax.axis_size("dp")
    clip = lax.axis_index("dp")
    owned = lax.axis_index("seq") // group
    length = 2 * width + 2 * LANES
    scalar = pl.BlockSpec(memory_space=pltpu.SMEM)
    in_vmem = pl.BlockSpec(memory_space=pltpu.VMEM)
    in_hbm = pl.BlockSpec(memory_space=pltpu.HBM)
    params = pltpu.CompilerParams(vmem_limit_bytes=VMEM_BYTES)
    phi = router.T
    message, exp_scores, combine, tok_scale, tok_norm = pl.pallas_call(
        token_sums,
        in_specs=[scalar, in_hbm, in_hbm, in_hbm],
        out_shape=[
            jax.ShapeDtypeStruct((experts, length), bf16),
            jax.ShapeDtypeStruct((experts, count), f32),
            jax.ShapeDtypeStruct((experts, count), bf16),
            jax.ShapeDtypeStruct((count, 1), f32),
            jax.ShapeDtypeStruct((count, width), bf16),
        ],
        scratch_shapes=[
            pltpu.VMEM((experts, width), bf16),
            pltpu.VMEM((count, width), bf16),
            pltpu.VMEM((count, width), bf16),
            pltpu.SemaphoreType.DMA,
            pltpu.SemaphoreType.DMA((2, 2 * PIECES)),
        ],
        compiler_params=params,
        name="token_sums",
    )(logit_scale, in_place(phi), in_place(tok_in), in_place(tok_cot))
    message = of_clips(message)
    message, expert_in, expert_out = lax.optimization_barrier((message, expert_in, expert_out))
    expert_in, expert_out = pl.pallas_call(
        fetch,
        in_specs=[in_hbm] * 2,
        out_specs=[in_vmem] * 2,
        out_shape=[
            jax.ShapeDtypeStruct(expert_in.shape, bf16),
            jax.ShapeDtypeStruct(expert_out.shape, bf16),
        ],
        scratch_shapes=[pltpu.SemaphoreType.DMA((2, PIECES))],
        compiler_params=params,
        cost_estimate=pl.CostEstimate(
            flops=0, bytes_accessed=4 * expert_in.size + 4 * expert_out.size, transcendentals=0
        ),
        name="fetch_weights",
    )(in_place(expert_in), in_place(expert_out))
    message = sum_to_owner(message, group)[0]
    message, totals, row_x, row_cot, hidden, pre_grad = pl.pallas_call(
        expert_rows,
        in_specs=[scalar] + [in_vmem] * 3,
        out_shape=[
            jax.ShapeDtypeStruct((clips, length), f32),
            jax.ShapeDtypeStruct((clips, LANES), f32),
            jax.ShapeDtypeStruct((clips, width), bf16),
            jax.ShapeDtypeStruct((clips, width), bf16),
            jax.ShapeDtypeStruct((clips, units), bf16),
            jax.ShapeDtypeStruct((clips, units), bf16),
        ],
        compiler_params=params,
        name="expert_rows",
    )(owned[None], message, expert_in, expert_out)
    message, hidden, row_cot = sum_to_all(message[None], group, (hidden, row_cot))
    slots = lax.dynamic_index_in_dim(message, clip, 1, keepdims=False)
    totals = lax.dynamic_index_in_dim(totals, clip, 0, keepdims=True)
    share = width // clips
    mine_x = lax.dynamic_slice_in_dim(row_x, clip * share, share, 1)
    mine_cot = lax.dynamic_slice_in_dim(row_cot, clip * share, share, 1)
    grad_expert_in = jnp.einsum("od,oh->dh", mine_x, pre_grad, preferred_element_type=f32)
    grad_expert_out = jnp.einsum("oh,od->hd", hidden, mine_cot, preferred_element_type=f32)
    score_grad, dispatch, phi_part = pl.pallas_call(
        score_grads,
        in_specs=[scalar] + [in_vmem] * 6,
        out_shape=[
            jax.ShapeDtypeStruct((experts, count), bf16),
            jax.ShapeDtypeStruct((experts, count), bf16),
            jax.ShapeDtypeStruct((experts, width), f32),
        ],
        compiler_params=params,
        name="score_grads",
    )(logit_scale, slots, totals, tok_in, tok_cot, tok_norm, exp_scores)
    phi_sum = phi_part
    for step in range(1, clips):
        phi_sum = phi_sum + hop(phi_part, step)
    phi_sum = phi_sum[None]
    *earlier, final = rounds(size)
    for pair in earlier:
        phi_sum = added(round_terms(phi_sum, pair), pair)
    terms = round_terms(phi_sum, final)
    grad_router = pl.pallas_call(
        finish,
        in_specs=[in_vmem] * (1 + len(terms)),
        out_shape=jax.ShapeDtypeStruct((experts, width), f32),
        compiler_params=params,
        name="finish",
    )(phi, terms[0], *[terms[mask] for mask in [*final[1:], sum(final), final[0]][-len(terms) + 1 :]])
    phi_f32 = phi.astype(f32)
    phi_scale = lax.rsqrt(jnp.sum(phi_f32 * phi_f32, axis=1, keepdims=True) + epsilon)
    phi_unit = phi_f32 * phi_scale
    phi_norm = phi_unit.astype(bf16)
    slot_y = slots[:, :width].astype(bf16)
    slot_dx = slots[:, width : 2 * width].astype(bf16)
    mixed = jnp.einsum("sn,sd->nd", combine, slot_y, preferred_element_type=f32).astype(bf16)
    norm_grad = jnp.einsum("sn,sd->nd", score_grad, phi_norm, preferred_element_type=f32)
    through = jnp.einsum("sn,sd->nd", dispatch, slot_dx, preferred_element_type=f32)
    tok_unit = tok_in.astype(f32) * tok_scale
    back_norm = tok_scale * (
        norm_grad - tok_unit * jnp.sum(tok_unit * norm_grad, axis=1, keepdims=True)
    )
    grad_tokens = (through + back_norm).astype(bf16)
    return (mixed[None], grad_tokens[None], grad_expert_in, grad_expert_out, grad_router.T)


def solution(mesh):
    return jax.shard_map(
        per_device,
        mesh=mesh,
        in_specs=(
            P("dp", "seq", None),
            P("dp", "seq", None),
            P(),
            P(),
            P(None, "seq"),
            P("seq", None),
        ),
        out_specs=(P("dp", "seq", None), P("dp", "seq", None), P("dp", "seq"), P("seq", "dp"), P()),
        check_vma=False,
    )
```

```python
import jax
import jax.numpy as jnp
from jax import lax
from jax.experimental import pallas as pl
from jax.experimental.pallas import tpu as pltpu
from jax.sharding import PartitionSpec as P

epsilon = 1e-06
AXES = ("seq", "dp")
LANES = 128
PIECES = 4
VMEM_BYTES = 10 * 2**20
ROWS = (((1,), (1,)), ((), ()))
COLUMNS = (((0,), (0,)), ((), ()))
f32, bf16 = jnp.float32, jnp.bfloat16


def exchange(value, mask):
    clips = lax.axis_size("dp")
    pairs = []
    for place in range(lax.axis_size("seq")):
        for clip in range(clips):
            there = (place ^ mask) * clips + (clip ^ 1 if clips % 2 == 0 else clip)
            pairs.append((place * clips + clip, there))
    return lax.ppermute(value, AXES, pairs)


def hop(value, step):
    return lax.ppermute(value, "dp", [(i, i ^ step) for i in range(lax.axis_size("dp"))])


def of_clips(value):
    clips = lax.axis_size("dp")
    apart = lax.broadcasted_iota(jnp.int32, (1, clips, 1), 1) ^ lax.axis_index("dp")
    merged = value[:, None]
    for step in range(1, clips):
        merged = jnp.where(apart == step, hop(value, step)[:, None], merged)
    return merged


def rounds(size):
    masks = [1 << bit for bit in range(size.bit_length() - 1)]
    return [masks[i : i + 2] for i in range(0, len(masks), 2)]


def narrow(value):
    lane = lax.broadcasted_iota(jnp.int32, value.shape, value.ndim - 1)
    lost = value - lax.reduce_precision(value, 8, 7)
    return jnp.where(lane < value.shape[-1] - LANES, value, lost).astype(bf16)


def swaps(pair):
    return pair if len(pair) == 1 else [pair[0], pair[0] | pair[1], pair[1]]


def added(terms, masks):
    if len(masks) == 1:
        return terms[masks[0]] + terms[0]
    low, high = masks
    return (terms[0] + terms[low]) + (terms[low | high] + terms[high])


def sum_to_owner(value, group):
    place = lax.axis_index("seq")
    for pair in reversed(rounds(lax.axis_size("seq"))):
        owner_masks = [mask for mask in pair if mask >= group]
        blocks = value.reshape((1 << len(owner_masks), -1) + value.shape[1:])

        def block_for(mask):
            index = 0
            for bit, owner_mask in enumerate(owner_masks):
                index = index + jnp.where((place ^ mask) & owner_mask != 0, 1 << bit, 0)
            return lax.dynamic_index_in_dim(blocks, index, 0, keepdims=False)

        terms = {0: block_for(0)}
        for mask in swaps(pair):
            terms[mask] = exchange(block_for(mask), mask)
        value = added({mask: term.astype(f32) for mask, term in terms.items()}, pair)
    return value


def round_terms(value, pair):
    terms = {0: value}
    for mask in swaps(pair):
        terms[mask] = exchange(value, mask)
    return terms


def sum_to_all(value, group, later=()):
    place = lax.axis_index("seq")
    for pair in rounds(lax.axis_size("seq")):
        terms = round_terms(value if pair[0] == 1 else narrow(value), pair)
        terms = {mask: term.astype(f32) for mask, term in terms.items()}
        inner = [mask for mask in pair if mask < group]
        outer = [mask for mask in pair if mask >= group]
        if inner:
            merged = {}
            for far in [0] + outer if len(outer) == 1 else [0]:
                merged[far] = added({mask ^ far: terms[mask] for mask in terms}, inner)
            terms = merged
        value = terms[0]
        for mask in outer:
            kept = {}
            for key in terms:
                if key & mask:
                    continue
                side = lax.broadcasted_iota(jnp.int32, (2,) + (1,) * value.ndim, 0)
                same = side == jnp.where((place & mask) != 0, 1, 0)
                both = jnp.where(same, terms[key][None], terms[key | mask][None])
                kept[key] = both.reshape((-1,) + both.shape[2:])
            terms = kept
            value = terms[0]
        if later and pair[0] == 1:
            value, *later = lax.optimization_barrier((value, *later))
    return (value, *later) if later else value


def token_sums(scale_ref, phi_ref, tok_ref, cot_ref, message_ref, exp_ref, combine_ref, tok_scale_ref, norm_ref, phi_buf, tok_buf, cot_buf, phi_sem, sems):
    experts, width = phi_ref.shape
    blocks = sems.shape[1]
    rows = tok_buf.shape[0] // blocks
    pieces = [pl.ds(index * rows, rows) for index in range(blocks)]
    phi_copy = pltpu.make_async_copy(phi_ref, phi_buf, phi_sem)
    tok_copies = [
        pltpu.make_async_copy(tok_ref.at[piece], tok_buf.at[piece], sems.at[0, index])
        for index, piece in enumerate(pieces)
    ]
    cot_copies = [
        pltpu.make_async_copy(cot_ref.at[piece], cot_buf.at[piece], sems.at[1, index])
        for index, piece in enumerate(pieces)
    ]
    for copy in tok_copies + [phi_copy] + cot_copies:
        copy.start()
    for index in range(0, blocks, 2):
        for copy in tok_copies[index : index + 2]:
            copy.wait()
        piece = pl.ds(index * rows, 2 * rows)
        tok_f32 = tok_buf[piece, :].astype(f32)
        tok_scale = lax.rsqrt(jnp.sum(tok_f32 * tok_f32, axis=1, keepdims=True) + epsilon)
        norm_ref[piece, :] = (tok_f32 * tok_scale).astype(bf16)
        tok_scale_ref[piece, :] = tok_scale
    phi_copy.wait()
    phi = phi_buf[...].astype(f32)
    phi_scale = lax.rsqrt(jnp.sum(phi * phi, axis=1, keepdims=True) + epsilon)
    phi_norm = (phi * phi_scale).astype(bf16)
    logits = scale_ref[0] * lax.dot_general(phi_norm, norm_ref[...], ROWS, preferred_element_type=f32)
    exp_scores = jnp.exp(logits)
    combine = (exp_scores / jnp.sum(exp_scores, axis=0, keepdims=True)).astype(bf16)
    exp_high = exp_scores.astype(bf16).astype(f32)
    halves = jnp.concatenate([exp_high, exp_scores - exp_high], axis=0).astype(bf16)
    in_parts = jnp.dot(halves, tok_buf[...], preferred_element_type=f32)
    message_ref[:, :width] = (in_parts[:experts] + in_parts[experts:]).astype(bf16)
    total = as_row(jnp.sum(exp_scores, axis=1, keepdims=True), LANES)
    high = total.astype(bf16).astype(f32)
    total = jnp.concatenate([high, total - high], axis=1).astype(bf16)
    message_ref[:, 2 * width :] = jnp.broadcast_to(total, (experts, 2 * LANES))
    exp_ref[...] = exp_scores
    combine_ref[...] = combine
    for copy in cot_copies:
        copy.wait()
    cot_part = jnp.dot(combine, cot_buf[...], preferred_element_type=f32)
    message_ref[:, width : 2 * width] = cot_part.astype(bf16)


def fetch(in_ref, out_ref, in_buf, out_buf, sems):
    copies = []
    for which, (source, target) in enumerate([(in_ref, in_buf), (out_ref, out_buf)]):
        rows = source.shape[0] // sems.shape[1]
        for index in range(sems.shape[1]):
            piece = pl.ds(index * rows, rows)
            copies.append(
                pltpu.make_async_copy(source.at[piece], target.at[piece], sems.at[which, index])
            )
    for copy in copies:
        copy.start()
    for copy in copies:
        copy.wait()


def expert_rows(owned_ref, sums_ref, in_ref, out_ref, message_ref, totals_ref, row_x_ref, row_cot_ref, hidden_ref, pre_grad_ref):
    width, units = in_ref.shape
    totals = sums_ref[:, 2 * width : 2 * width + LANES] + sums_ref[:, 2 * width + LANES :]
    lane = lax.broadcasted_iota(jnp.int32, totals.shape, 1)
    own_total = jnp.sum(jnp.where(lane == owned_ref[0], totals, 0.0), axis=1, keepdims=True)
    own_in = sums_ref[:, :width] / own_total
    row_x = own_in.astype(bf16)
    row_cot = sums_ref[:, width : 2 * width].astype(bf16)
    pre_act = jnp.dot(row_x, in_ref[...], preferred_element_type=f32)
    hid_grad = lax.dot_general(row_cot, out_ref[...], ROWS, preferred_element_type=f32)
    cdf = 0.5 * (1.0 + lax.erf(pre_act * 0.7071067811865476))
    hidden = (pre_act * cdf).astype(bf16)
    slope = cdf + pre_act * jnp.exp(-0.5 * pre_act * pre_act) * 0.3989422804014327
    pre_grad = (hid_grad * slope).astype(bf16)
    part_out = jnp.dot(hidden, out_ref[...], preferred_element_type=f32)
    part_dx = lax.dot_general(pre_grad, in_ref[...], ROWS, preferred_element_type=f32)
    message_ref[:, :width] = part_out
    message_ref[:, width : 2 * width] = part_dx
    dot_part = jnp.sum(own_in * part_dx, axis=1, keepdims=True)
    message_ref[:, 2 * width :] = jnp.broadcast_to(dot_part, (totals.shape[0], 2 * LANES))
    totals_ref[...] = totals
    row_x_ref[...] = row_x
    row_cot_ref[...] = row_cot
    hidden_ref[...] = hidden
    pre_grad_ref[...] = pre_grad


def as_row(column, lanes):
    shape = (column.shape[0], lanes)
    same = lax.broadcasted_iota(jnp.int32, shape, 0) == lax.broadcasted_iota(jnp.int32, shape, 1)
    return jnp.sum(jnp.where(same, column, 0.0), axis=0, keepdims=True)


def as_column(row, slots):
    shape = (slots, row.shape[1])
    same = lax.broadcasted_iota(jnp.int32, shape, 0) == lax.broadcasted_iota(jnp.int32, shape, 1)
    return jnp.sum(jnp.where(same, row, 0.0), axis=1, keepdims=True)


def score_grads(scale_ref, slots_ref, totals_ref, tok_ref, cot_ref, norm_ref, exp_ref, grad_ref, dispatch_ref, phi_ref):
    width = tok_ref.shape[1]
    slot_y = slots_ref[:, :width].astype(bf16)
    slot_dx = slots_ref[:, width : 2 * width].astype(bf16)
    low = 2 * width + LANES
    column_stat = slots_ref[:, 2 * width : 2 * width + 1] + slots_ref[:, low : low + 1]
    totals = as_column(totals_ref[...], slot_y.shape[0])
    exp_scores = exp_ref[...]
    combine_f = exp_scores / jnp.sum(exp_scores, axis=0, keepdims=True)
    comb_dot = lax.dot_general(slot_y, cot_ref[...], ROWS, preferred_element_type=f32)
    grad_comb = combine_f * (comb_dot - jnp.sum(combine_f * comb_dot, axis=0, keepdims=True))
    disp_dot = lax.dot_general(slot_dx, tok_ref[...], ROWS, preferred_element_type=f32)
    dispatch_f = exp_scores / totals
    grad_disp = dispatch_f * (disp_dot - column_stat)
    score_grad = (scale_ref[0] * (grad_comb + grad_disp)).astype(bf16)
    phi_ref[...] = jnp.dot(score_grad, norm_ref[...], preferred_element_type=f32)
    grad_ref[...] = score_grad
    dispatch_ref[...] = dispatch_f.astype(bf16)


def finish(phi_ref, *refs):
    *term_refs, grad_ref = refs
    own, *others = [ref[0] for ref in term_refs]
    phi_grad = own + others[-1]
    if len(others) > 1:
        phi_grad = phi_grad + (others[0] + others[1])
    phi = phi_ref[...].astype(f32)
    phi_scale = lax.rsqrt(jnp.sum(phi * phi, axis=1, keepdims=True) + epsilon)
    phi_unit = phi * phi_scale
    along = jnp.sum(phi_unit * phi_grad, axis=1, keepdims=True)
    grad_ref[...] = phi_scale * (phi_grad - phi_unit * along)


def in_place(operand):
    return pltpu.with_memory_space_constraint(operand, pltpu.HBM)


def per_device(tokens, cotangent, router, logit_scale, expert_in, expert_out):
    tok_in = tokens[0]
    tok_cot = cotangent[0]
    count = tok_in.shape[0]
    width, experts = router.shape
    units = expert_in.shape[1]
    size = lax.axis_size("seq")
    group = size // experts
    clips = lax.axis_size("dp")
    clip = lax.axis_index("dp")
    owned = lax.axis_index("seq") // group
    length = 2 * width + 2 * LANES
    scalar = pl.BlockSpec(memory_space=pltpu.SMEM)
    in_vmem = pl.BlockSpec(memory_space=pltpu.VMEM)
    in_hbm = pl.BlockSpec(memory_space=pltpu.HBM)
    params = pltpu.CompilerParams(vmem_limit_bytes=VMEM_BYTES)
    phi = router.T
    message, exp_scores, combine, tok_scale, tok_norm = pl.pallas_call(
        token_sums,
        in_specs=[scalar, in_hbm, in_hbm, in_hbm],
        out_shape=[
            jax.ShapeDtypeStruct((experts, length), bf16),
            jax.ShapeDtypeStruct((experts, count), f32),
            jax.ShapeDtypeStruct((experts, count), bf16),
            jax.ShapeDtypeStruct((count, 1), f32),
            jax.ShapeDtypeStruct((count, width), bf16),
        ],
        scratch_shapes=[
            pltpu.VMEM((experts, width), bf16),
            pltpu.VMEM((count, width), bf16),
            pltpu.VMEM((count, width), bf16),
            pltpu.SemaphoreType.DMA,
            pltpu.SemaphoreType.DMA((2, PIECES)),
        ],
        compiler_params=params,
        name="token_sums",
    )(logit_scale, in_place(phi), in_place(tok_in), in_place(tok_cot))
    message = of_clips(message)
    message, expert_in, expert_out = lax.optimization_barrier((message, expert_in, expert_out))
    expert_in, expert_out = pl.pallas_call(
        fetch,
        in_specs=[in_hbm] * 2,
        out_specs=[in_vmem] * 2,
        out_shape=[
            jax.ShapeDtypeStruct(expert_in.shape, bf16),
            jax.ShapeDtypeStruct(expert_out.shape, bf16),
        ],
        scratch_shapes=[pltpu.SemaphoreType.DMA((2, PIECES))],
        compiler_params=params,
        cost_estimate=pl.CostEstimate(
            flops=0, bytes_accessed=4 * expert_in.size + 4 * expert_out.size, transcendentals=0
        ),
        name="fetch_weights",
    )(in_place(expert_in), in_place(expert_out))
    message = sum_to_owner(message, group)[0]
    message, totals, row_x, row_cot, hidden, pre_grad = pl.pallas_call(
        expert_rows,
        in_specs=[scalar] + [in_vmem] * 3,
        out_shape=[
            jax.ShapeDtypeStruct((clips, length), f32),
            jax.ShapeDtypeStruct((clips, LANES), f32),
            jax.ShapeDtypeStruct((clips, width), bf16),
            jax.ShapeDtypeStruct((clips, width), bf16),
            jax.ShapeDtypeStruct((clips, units), bf16),
            jax.ShapeDtypeStruct((clips, units), bf16),
        ],
        compiler_params=params,
        name="expert_rows",
    )(owned[None], message, expert_in, expert_out)
    message, hidden, row_cot = sum_to_all(message[None], group, (hidden, row_cot))
    slots = lax.dynamic_index_in_dim(message, clip, 1, keepdims=False)
    totals = lax.dynamic_index_in_dim(totals, clip, 0, keepdims=True)
    share = width // clips
    mine_x = lax.dynamic_slice_in_dim(row_x, clip * share, share, 1)
    mine_cot = lax.dynamic_slice_in_dim(row_cot, clip * share, share, 1)
    grad_expert_in = jnp.einsum("od,oh->dh", mine_x, pre_grad, preferred_element_type=f32)
    grad_expert_out = jnp.einsum("oh,od->hd", hidden, mine_cot, preferred_element_type=f32)
    score_grad, dispatch, phi_part = pl.pallas_call(
        score_grads,
        in_specs=[scalar] + [in_vmem] * 6,
        out_shape=[
            jax.ShapeDtypeStruct((experts, count), bf16),
            jax.ShapeDtypeStruct((experts, count), bf16),
            jax.ShapeDtypeStruct((experts, width), f32),
        ],
        compiler_params=params,
        name="score_grads",
    )(logit_scale, slots, totals, tok_in, tok_cot, tok_norm, exp_scores)
    phi_sum = phi_part
    for step in range(1, clips):
        phi_sum = phi_sum + hop(phi_part, step)
    phi_sum = phi_sum[None]
    *earlier, final = rounds(size)
    for pair in earlier:
        phi_sum = added(round_terms(phi_sum, pair), pair)
    terms = round_terms(phi_sum, final)
    grad_router = pl.pallas_call(
        finish,
        in_specs=[in_vmem] * (1 + len(terms)),
        out_shape=jax.ShapeDtypeStruct((experts, width), f32),
        compiler_params=params,
        name="finish",
    )(phi, terms[0], *[terms[mask] for mask in [*final[1:], sum(final), final[0]][-len(terms) + 1 :]])
    phi_f32 = phi.astype(f32)
    phi_scale = lax.rsqrt(jnp.sum(phi_f32 * phi_f32, axis=1, keepdims=True) + epsilon)
    phi_unit = phi_f32 * phi_scale
    phi_norm = phi_unit.astype(bf16)
    slot_y = slots[:, :width].astype(bf16)
    slot_dx = slots[:, width : 2 * width].astype(bf16)
    mixed = jnp.einsum("sn,sd->nd", combine, slot_y, preferred_element_type=f32).astype(bf16)
    norm_grad = jnp.einsum("sn,sd->nd", score_grad, phi_norm, preferred_element_type=f32)
    through = jnp.einsum("sn,sd->nd", dispatch, slot_dx, preferred_element_type=f32)
    tok_unit = tok_in.astype(f32) * tok_scale
    back_norm = tok_scale * (
        norm_grad - tok_unit * jnp.sum(tok_unit * norm_grad, axis=1, keepdims=True)
    )
    grad_tokens = (through + back_norm).astype(bf16)
    return (mixed[None], grad_tokens[None], grad_expert_in, grad_expert_out, grad_router.T)


def solution(mesh):
    return jax.shard_map(
        per_device,
        mesh=mesh,
        in_specs=(
            P("dp", "seq", None),
            P("dp", "seq", None),
            P(),
            P(),
            P(None, "seq"),
            P("seq", None),
        ),
        out_specs=(P("dp", "seq", None), P("dp", "seq", None), P("dp", "seq"), P("seq", "dp"), P()),
        check_vma=False,
    )
```

```python
import jax
import jax.numpy as jnp
from jax import lax
from jax.experimental import pallas as pl
from jax.experimental.pallas import tpu as pltpu
from jax.sharding import PartitionSpec as P

epsilon = 1e-06
AXES = ("seq", "dp")
LANES = 128
PIECES = 4
VMEM_BYTES = 10 * 2**20
ROWS = (((1,), (1,)), ((), ()))
COLUMNS = (((0,), (0,)), ((), ()))
f32, bf16 = jnp.float32, jnp.bfloat16


def exchange(value, mask):
    clips = lax.axis_size("dp")
    pairs = []
    for place in range(lax.axis_size("seq")):
        for clip in range(clips):
            there = (place ^ mask) * clips + (clip ^ 1 if clips % 2 == 0 else clip)
            pairs.append((place * clips + clip, there))
    return lax.ppermute(value, AXES, pairs)


def hop(value, step):
    return lax.ppermute(value, "dp", [(i, i ^ step) for i in range(lax.axis_size("dp"))])


def of_clips(value):
    clips = lax.axis_size("dp")
    apart = lax.broadcasted_iota(jnp.int32, (1, clips, 1), 1) ^ lax.axis_index("dp")
    merged = value[:, None]
    for step in range(1, clips):
        merged = jnp.where(apart == step, hop(value, step)[:, None], merged)
    return merged


def rounds(size):
    masks = [1 << bit for bit in range(size.bit_length() - 1)]
    return [masks[i : i + 2] for i in range(0, len(masks), 2)]


def narrow(value):
    lane = lax.broadcasted_iota(jnp.int32, value.shape, value.ndim - 1)
    lost = value - lax.reduce_precision(value, 8, 7)
    return jnp.where(lane < value.shape[-1] - LANES, value, lost).astype(bf16)


def swaps(pair):
    return pair if len(pair) == 1 else [pair[0], pair[0] | pair[1], pair[1]]


def added(terms, masks):
    if len(masks) == 1:
        return terms[masks[0]] + terms[0]
    low, high = masks
    return (terms[0] + terms[low]) + (terms[low | high] + terms[high])


def sum_to_owner(value, group):
    place = lax.axis_index("seq")
    for pair in reversed(rounds(lax.axis_size("seq"))):
        owner_masks = [mask for mask in pair if mask >= group]
        blocks = value.reshape((1 << len(owner_masks), -1) + value.shape[1:])

        def block_for(mask):
            index = 0
            for bit, owner_mask in enumerate(owner_masks):
                index = index + jnp.where((place ^ mask) & owner_mask != 0, 1 << bit, 0)
            return lax.dynamic_index_in_dim(blocks, index, 0, keepdims=False)

        terms = {0: block_for(0)}
        for mask in swaps(pair):
            terms[mask] = exchange(block_for(mask), mask)
        value = added({mask: term.astype(f32) for mask, term in terms.items()}, pair)
    return value


def round_terms(value, pair):
    terms = {0: value}
    for mask in swaps(pair):
        terms[mask] = exchange(value, mask)
    return terms


def sum_to_all(value, group, later=()):
    place = lax.axis_index("seq")
    for pair in rounds(lax.axis_size("seq")):
        terms = round_terms(value if pair[0] == 1 else narrow(value), pair)
        terms = {mask: term.astype(f32) for mask, term in terms.items()}
        inner = [mask for mask in pair if mask < group]
        outer = [mask for mask in pair if mask >= group]
        if inner:
            merged = {}
            for far in [0] + outer if len(outer) == 1 else [0]:
                merged[far] = added({mask ^ far: terms[mask] for mask in terms}, inner)
            terms = merged
        value = terms[0]
        for mask in outer:
            kept = {}
            for key in terms:
                if key & mask:
                    continue
                side = lax.broadcasted_iota(jnp.int32, (2,) + (1,) * value.ndim, 0)
                same = side == jnp.where((place & mask) != 0, 1, 0)
                both = jnp.where(same, terms[key][None], terms[key | mask][None])
                kept[key] = both.reshape((-1,) + both.shape[2:])
            terms = kept
            value = terms[0]
        if later and pair[0] == 1:
            value, *later = lax.optimization_barrier((value, *later))
    return (value, *later) if later else value


def token_sums(scale_ref, phi_ref, tok_ref, cot_ref, message_ref, exp_ref, combine_ref, tok_scale_ref, norm_ref, phi_buf, tok_buf, cot_buf, phi_sem, sems):
    experts, width = phi_ref.shape
    blocks = sems.shape[1]
    rows = tok_buf.shape[0] // blocks
    pieces = [pl.ds(index * rows, rows) for index in range(blocks)]
    phi_copy = pltpu.make_async_copy(phi_ref, phi_buf, phi_sem)
    tok_copies = [
        pltpu.make_async_copy(tok_ref.at[piece], tok_buf.at[piece], sems.at[0, index])
        for index, piece in enumerate(pieces)
    ]
    cot_copies = [
        pltpu.make_async_copy(cot_ref.at[piece], cot_buf.at[piece], sems.at[1, index])
        for index, piece in enumerate(pieces)
    ]
    for copy in tok_copies + [phi_copy] + cot_copies:
        copy.start()
    for copy in tok_copies:
        copy.wait()
    tok_f32 = tok_buf[...].astype(f32)
    tok_scale = lax.rsqrt(jnp.sum(tok_f32 * tok_f32, axis=1, keepdims=True) + epsilon)
    norm_ref[...] = (tok_f32 * tok_scale).astype(bf16)
    tok_scale_ref[...] = tok_scale
    phi_copy.wait()
    phi = phi_buf[...].astype(f32)
    phi_scale = lax.rsqrt(jnp.sum(phi * phi, axis=1, keepdims=True) + epsilon)
    phi_norm = (phi * phi_scale).astype(bf16)
    logits = scale_ref[0] * lax.dot_general(phi_norm, norm_ref[...], ROWS, preferred_element_type=f32)
    exp_scores = jnp.exp(logits)
    combine = (exp_scores / jnp.sum(exp_scores, axis=0, keepdims=True)).astype(bf16)
    exp_high = exp_scores.astype(bf16).astype(f32)
    halves = jnp.concatenate([exp_high, exp_scores - exp_high], axis=0).astype(bf16)
    in_parts = jnp.dot(halves, tok_buf[...], preferred_element_type=f32)
    message_ref[:, :width] = (in_parts[:experts] + in_parts[experts:]).astype(bf16)
    total = as_row(jnp.sum(exp_scores, axis=1, keepdims=True), LANES)
    high = total.astype(bf16).astype(f32)
    total = jnp.concatenate([high, total - high], axis=1).astype(bf16)
    message_ref[:, 2 * width :] = jnp.broadcast_to(total, (experts, 2 * LANES))
    exp_ref[...] = exp_scores
    combine_ref[...] = combine
    for copy in cot_copies:
        copy.wait()
    cot_part = jnp.dot(combine, cot_buf[...], preferred_element_type=f32)
    message_ref[:, width : 2 * width] = cot_part.astype(bf16)


def fetch(in_ref, out_ref, in_buf, out_buf, sems):
    copies = []
    for which, (source, target) in enumerate([(in_ref, in_buf), (out_ref, out_buf)]):
        rows = source.shape[0] // sems.shape[1]
        for index in range(sems.shape[1]):
            piece = pl.ds(index * rows, rows)
            copies.append(
                pltpu.make_async_copy(source.at[piece], target.at[piece], sems.at[which, index])
            )
    for copy in copies:
        copy.start()
    for copy in copies:
        copy.wait()


def expert_rows(owned_ref, sums_ref, in_ref, out_ref, message_ref, totals_ref, row_x_ref, row_cot_ref, hidden_ref, pre_grad_ref):
    width, units = in_ref.shape
    totals = sums_ref[:, 2 * width : 2 * width + LANES] + sums_ref[:, 2 * width + LANES :]
    lane = lax.broadcasted_iota(jnp.int32, totals.shape, 1)
    own_total = jnp.sum(jnp.where(lane == owned_ref[0], totals, 0.0), axis=1, keepdims=True)
    own_in = sums_ref[:, :width] / own_total
    row_x = own_in.astype(bf16)
    row_cot = sums_ref[:, width : 2 * width].astype(bf16)
    pre_act = jnp.dot(row_x, in_ref[...], preferred_element_type=f32)
    hid_grad = lax.dot_general(row_cot, out_ref[...], ROWS, preferred_element_type=f32)
    cdf = 0.5 * (1.0 + lax.erf(pre_act * 0.7071067811865476))
    hidden = (pre_act * cdf).astype(bf16)
    slope = cdf + pre_act * jnp.exp(-0.5 * pre_act * pre_act) * 0.3989422804014327
    pre_grad = (hid_grad * slope).astype(bf16)
    part_out = jnp.dot(hidden, out_ref[...], preferred_element_type=f32)
    part_dx = lax.dot_general(pre_grad, in_ref[...], ROWS, preferred_element_type=f32)
    message_ref[:, :width] = part_out
    message_ref[:, width : 2 * width] = part_dx
    dot_part = jnp.sum(own_in * part_dx, axis=1, keepdims=True)
    message_ref[:, 2 * width :] = jnp.broadcast_to(dot_part, (totals.shape[0], 2 * LANES))
    totals_ref[...] = totals
    row_x_ref[...] = row_x
    row_cot_ref[...] = row_cot
    hidden_ref[...] = hidden
    pre_grad_ref[...] = pre_grad


def as_row(column, lanes):
    shape = (column.shape[0], lanes)
    same = lax.broadcasted_iota(jnp.int32, shape, 0) == lax.broadcasted_iota(jnp.int32, shape, 1)
    return jnp.sum(jnp.where(same, column, 0.0), axis=0, keepdims=True)


def as_column(row, slots):
    shape = (slots, row.shape[1])
    same = lax.broadcasted_iota(jnp.int32, shape, 0) == lax.broadcasted_iota(jnp.int32, shape, 1)
    return jnp.sum(jnp.where(same, row, 0.0), axis=1, keepdims=True)


def score_grads(clip_ref, scale_ref, message_ref, totals_ref, tok_ref, cot_ref, norm_ref, exp_ref, grad_ref, dispatch_ref, phi_ref, slot_y_ref, slot_dx_ref):
    width = tok_ref.shape[1]
    experts = message_ref.shape[0]

    def of_clip(values):
        mine = lax.broadcasted_iota(jnp.int32, values.shape, 0) == clip_ref[0]
        return jnp.sum(jnp.where(mine, values, 0.0), axis=0, keepdims=True)

    slots = jnp.concatenate([of_clip(message_ref[slot]) for slot in range(experts)], axis=0)
    slot_y = slots[:, :width].astype(bf16)
    slot_dx = slots[:, width : 2 * width].astype(bf16)
    slot_y_ref[...] = slot_y
    slot_dx_ref[...] = slot_dx
    low = 2 * width + LANES
    column_stat = slots[:, 2 * width : 2 * width + 1] + slots[:, low : low + 1]
    totals = as_column(of_clip(totals_ref[...]), experts)
    exp_scores = exp_ref[...]
    combine_f = exp_scores / jnp.sum(exp_scores, axis=0, keepdims=True)
    comb_dot = lax.dot_general(slot_y, cot_ref[...], ROWS, preferred_element_type=f32)
    grad_comb = combine_f * (comb_dot - jnp.sum(combine_f * comb_dot, axis=0, keepdims=True))
    disp_dot = lax.dot_general(slot_dx, tok_ref[...], ROWS, preferred_element_type=f32)
    dispatch_f = exp_scores / totals
    grad_disp = dispatch_f * (disp_dot - column_stat)
    score_grad = (scale_ref[0] * (grad_comb + grad_disp)).astype(bf16)
    phi_ref[...] = jnp.dot(score_grad, norm_ref[...], preferred_element_type=f32)
    grad_ref[...] = score_grad
    dispatch_ref[...] = dispatch_f.astype(bf16)


def finish(phi_ref, *refs):
    *term_refs, grad_ref = refs
    own, *others = [ref[0] for ref in term_refs]
    phi_grad = own + others[-1]
    if len(others) > 1:
        phi_grad = phi_grad + (others[0] + others[1])
    phi = phi_ref[...].astype(f32)
    phi_scale = lax.rsqrt(jnp.sum(phi * phi, axis=1, keepdims=True) + epsilon)
    phi_unit = phi * phi_scale
    along = jnp.sum(phi_unit * phi_grad, axis=1, keepdims=True)
    grad_ref[...] = phi_scale * (phi_grad - phi_unit * along)


def in_place(operand):
    return pltpu.with_memory_space_constraint(operand, pltpu.HBM)


def per_device(tokens, cotangent, router, logit_scale, expert_in, expert_out):
    tok_in = tokens[0]
    tok_cot = cotangent[0]
    count = tok_in.shape[0]
    width, experts = router.shape
    units = expert_in.shape[1]
    size = lax.axis_size("seq")
    group = size // experts
    clips = lax.axis_size("dp")
    clip = lax.axis_index("dp")
    owned = lax.axis_index("seq") // group
    length = 2 * width + 2 * LANES
    scalar = pl.BlockSpec(memory_space=pltpu.SMEM)
    in_vmem = pl.BlockSpec(memory_space=pltpu.VMEM)
    in_hbm = pl.BlockSpec(memory_space=pltpu.HBM)
    params = pltpu.CompilerParams(vmem_limit_bytes=VMEM_BYTES)
    phi = router.T
    message, exp_scores, combine, tok_scale, tok_norm = pl.pallas_call(
        token_sums,
        in_specs=[scalar, in_hbm, in_hbm, in_hbm],
        out_shape=[
            jax.ShapeDtypeStruct((experts, length), bf16),
            jax.ShapeDtypeStruct((experts, count), f32),
            jax.ShapeDtypeStruct((experts, count), bf16),
            jax.ShapeDtypeStruct((count, 1), f32),
            jax.ShapeDtypeStruct((count, width), bf16),
        ],
        scratch_shapes=[
            pltpu.VMEM((experts, width), bf16),
            pltpu.VMEM((count, width), bf16),
            pltpu.VMEM((count, width), bf16),
            pltpu.SemaphoreType.DMA,
            pltpu.SemaphoreType.DMA((2, PIECES)),
        ],
        compiler_params=params,
        name="token_sums",
    )(logit_scale, in_place(phi), in_place(tok_in), in_place(tok_cot))
    message = of_clips(message)
    message, expert_in, expert_out = lax.optimization_barrier((message, expert_in, expert_out))
    expert_in, expert_out = pl.pallas_call(
        fetch,
        in_specs=[in_hbm] * 2,
        out_specs=[in_vmem] * 2,
        out_shape=[
            jax.ShapeDtypeStruct(expert_in.shape, bf16),
            jax.ShapeDtypeStruct(expert_out.shape, bf16),
        ],
        scratch_shapes=[pltpu.SemaphoreType.DMA((2, PIECES))],
        compiler_params=params,
        cost_estimate=pl.CostEstimate(
            flops=0, bytes_accessed=4 * expert_in.size + 4 * expert_out.size, transcendentals=0
        ),
        name="fetch_weights",
    )(in_place(expert_in), in_place(expert_out))
    message = sum_to_owner(message, group)[0]
    message, totals, row_x, row_cot, hidden, pre_grad = pl.pallas_call(
        expert_rows,
        in_specs=[scalar] + [in_vmem] * 3,
        out_shape=[
            jax.ShapeDtypeStruct((clips, length), f32),
            jax.ShapeDtypeStruct((clips, LANES), f32),
            jax.ShapeDtypeStruct((clips, width), bf16),
            jax.ShapeDtypeStruct((clips, width), bf16),
            jax.ShapeDtypeStruct((clips, units), bf16),
            jax.ShapeDtypeStruct((clips, units), bf16),
        ],
        compiler_params=params,
        name="expert_rows",
    )(owned[None], message, expert_in, expert_out)
    message, hidden, row_cot = sum_to_all(message[None], group, (hidden, row_cot))
    share = width // clips
    mine_x = lax.dynamic_slice_in_dim(row_x, clip * share, share, 1)
    mine_cot = lax.dynamic_slice_in_dim(row_cot, clip * share, share, 1)
    grad_expert_in = jnp.einsum("od,oh->dh", mine_x, pre_grad, preferred_element_type=f32)
    grad_expert_out = jnp.einsum("oh,od->hd", hidden, mine_cot, preferred_element_type=f32)
    score_grad, dispatch, phi_part, slot_y, slot_dx = pl.pallas_call(
        score_grads,
        in_specs=[scalar, scalar] + [in_vmem] * 6,
        out_shape=[
            jax.ShapeDtypeStruct((experts, count), bf16),
            jax.ShapeDtypeStruct((experts, count), bf16),
            jax.ShapeDtypeStruct((experts, width), f32),
            jax.ShapeDtypeStruct((experts, width), bf16),
            jax.ShapeDtypeStruct((experts, width), bf16),
        ],
        compiler_params=params,
        name="score_grads",
    )(clip[None], logit_scale, message, totals, tok_in, tok_cot, tok_norm, exp_scores)
    phi_sum = phi_part
    for step in range(1, clips):
        phi_sum = phi_sum + hop(phi_part, step)
    phi_sum = phi_sum[None]
    *earlier, final = rounds(size)
    for pair in earlier:
        phi_sum = added(round_terms(phi_sum, pair), pair)
    terms = round_terms(phi_sum, final)
    grad_router = pl.pallas_call(
        finish,
        in_specs=[in_vmem] * (1 + len(terms)),
        out_shape=jax.ShapeDtypeStruct((experts, width), f32),
        compiler_params=params,
        name="finish",
    )(phi, terms[0], *[terms[mask] for mask in [*final[1:], sum(final), final[0]][-len(terms) + 1 :]])
    phi_f32 = phi.astype(f32)
    phi_scale = lax.rsqrt(jnp.sum(phi_f32 * phi_f32, axis=1, keepdims=True) + epsilon)
    phi_unit = phi_f32 * phi_scale
    phi_norm = phi_unit.astype(bf16)
    mixed = jnp.einsum("sn,sd->nd", combine, slot_y, preferred_element_type=f32).astype(bf16)
    norm_grad = jnp.einsum("sn,sd->nd", score_grad, phi_norm, preferred_element_type=f32)
    through = jnp.einsum("sn,sd->nd", dispatch, slot_dx, preferred_element_type=f32)
    tok_unit = tok_in.astype(f32) * tok_scale
    back_norm = tok_scale * (
        norm_grad - tok_unit * jnp.sum(tok_unit * norm_grad, axis=1, keepdims=True)
    )
    grad_tokens = (through + back_norm).astype(bf16)
    return (mixed[None], grad_tokens[None], grad_expert_in, grad_expert_out, grad_router.T)


def solution(mesh):
    return jax.shard_map(
        per_device,
        mesh=mesh,
        in_specs=(
            P("dp", "seq", None),
            P("dp", "seq", None),
            P(),
            P(),
            P(None, "seq"),
            P("seq", None),
        ),
        out_specs=(P("dp", "seq", None), P("dp", "seq", None), P("dp", "seq"), P("seq", "dp"), P()),
        check_vma=False,
    )
```

```python
import jax
import jax.numpy as jnp
from jax import lax
from jax.experimental import pallas as pl
from jax.experimental.pallas import tpu as pltpu
from jax.sharding import PartitionSpec as P

epsilon = 1e-06
AXES = ("seq", "dp")
LANES = 128
PIECES = 4
VMEM_BYTES = 10 * 2**20
ROWS = (((1,), (1,)), ((), ()))
COLUMNS = (((0,), (0,)), ((), ()))
f32, bf16 = jnp.float32, jnp.bfloat16


def exchange(value, mask):
    clips = lax.axis_size("dp")
    pairs = []
    for place in range(lax.axis_size("seq")):
        for clip in range(clips):
            there = (place ^ mask) * clips + (clip ^ 1 if clips % 2 == 0 else clip)
            pairs.append((place * clips + clip, there))
    return lax.ppermute(value, AXES, pairs)


def hop(value, step):
    return lax.ppermute(value, "dp", [(i, i ^ step) for i in range(lax.axis_size("dp"))])


def of_clips(value):
    clips = lax.axis_size("dp")
    apart = lax.broadcasted_iota(jnp.int32, (1, clips, 1), 1) ^ lax.axis_index("dp")
    merged = value[:, None]
    for step in range(1, clips):
        merged = jnp.where(apart == step, hop(value, step)[:, None], merged)
    return merged


def rounds(size):
    masks = [1 << bit for bit in range(size.bit_length() - 1)]
    return [masks[i : i + 2] for i in range(0, len(masks), 2)]


def narrow(value):
    lane = lax.broadcasted_iota(jnp.int32, value.shape, value.ndim - 1)
    lost = value - lax.reduce_precision(value, 8, 7)
    return jnp.where(lane < value.shape[-1] - LANES, value, lost).astype(bf16)


def swaps(pair):
    return pair if len(pair) == 1 else [pair[0], pair[0] | pair[1], pair[1]]


def added(terms, masks):
    if len(masks) == 1:
        return terms[masks[0]] + terms[0]
    low, high = masks
    return (terms[0] + terms[low]) + (terms[low | high] + terms[high])


def sum_to_owner(value, group, beside):
    place = lax.axis_index("seq")
    for pair in reversed(rounds(lax.axis_size("seq"))):
        owner_masks = [mask for mask in pair if mask >= group]
        blocks = value.reshape((1 << len(owner_masks), -1) + value.shape[1:])

        def block_for(mask):
            index = 0
            for bit, owner_mask in enumerate(owner_masks):
                index = index + jnp.where((place ^ mask) & owner_mask != 0, 1 << bit, 0)
            return lax.dynamic_index_in_dim(blocks, index, 0, keepdims=False)

        terms = {0: block_for(0)}
        for mask in swaps(pair):
            terms[mask] = exchange(block_for(mask), mask)
        value = added({mask: term.astype(f32) for mask, term in terms.items()}, pair)
        value, *beside = lax.optimization_barrier((value, *beside))
    return (value, *beside)


def round_terms(value, pair):
    terms = {0: value}
    for mask in swaps(pair):
        terms[mask] = exchange(value, mask)
    return terms


def sum_to_all(value, group, later=()):
    place = lax.axis_index("seq")
    for pair in rounds(lax.axis_size("seq")):
        terms = round_terms(value if pair[0] == 1 else narrow(value), pair)
        terms = {mask: term.astype(f32) for mask, term in terms.items()}
        inner = [mask for mask in pair if mask < group]
        outer = [mask for mask in pair if mask >= group]
        if inner:
            merged = {}
            for far in [0] + outer if len(outer) == 1 else [0]:
                merged[far] = added({mask ^ far: terms[mask] for mask in terms}, inner)
            terms = merged
        value = terms[0]
        for mask in outer:
            kept = {}
            for key in terms:
                if key & mask:
                    continue
                side = lax.broadcasted_iota(jnp.int32, (2,) + (1,) * value.ndim, 0)
                same = side == jnp.where((place & mask) != 0, 1, 0)
                both = jnp.where(same, terms[key][None], terms[key | mask][None])
                kept[key] = both.reshape((-1,) + both.shape[2:])
            terms = kept
            value = terms[0]
        if later and pair[0] == 1:
            value, *later = lax.optimization_barrier((value, *later))
    return (value, *later) if later else value


def token_sums(scale_ref, phi_ref, tok_ref, cot_ref, message_ref, exp_ref, combine_ref, tok_scale_ref, norm_ref, phi_buf, tok_buf, cot_buf, phi_sem, sems):
    experts, width = phi_ref.shape
    blocks = sems.shape[1]
    rows = tok_buf.shape[0] // blocks
    pieces = [pl.ds(index * rows, rows) for index in range(blocks)]
    phi_copy = pltpu.make_async_copy(phi_ref, phi_buf, phi_sem)
    tok_copies = [
        pltpu.make_async_copy(tok_ref.at[piece], tok_buf.at[piece], sems.at[0, index])
        for index, piece in enumerate(pieces)
    ]
    cot_copies = [
        pltpu.make_async_copy(cot_ref.at[piece], cot_buf.at[piece], sems.at[1, index])
        for index, piece in enumerate(pieces)
    ]
    for copy in tok_copies + [phi_copy] + cot_copies:
        copy.start()
    for index in range(0, blocks, 2):
        for copy in tok_copies[index : index + 2]:
            copy.wait()
        piece = pl.ds(index * rows, 2 * rows)
        tok_f32 = tok_buf[piece, :].astype(f32)
        tok_scale = lax.rsqrt(jnp.sum(tok_f32 * tok_f32, axis=1, keepdims=True) + epsilon)
        norm_ref[piece, :] = (tok_f32 * tok_scale).astype(bf16)
        tok_scale_ref[piece, :] = tok_scale
    phi_copy.wait()
    phi = phi_buf[...].astype(f32)
    phi_scale = lax.rsqrt(jnp.sum(phi * phi, axis=1, keepdims=True) + epsilon)
    phi_norm = (phi * phi_scale).astype(bf16)
    logits = scale_ref[0] * lax.dot_general(phi_norm, norm_ref[...], ROWS, preferred_element_type=f32)
    exp_scores = jnp.exp(logits)
    combine = (exp_scores / jnp.sum(exp_scores, axis=0, keepdims=True)).astype(bf16)
    exp_high = exp_scores.astype(bf16).astype(f32)
    halves = jnp.concatenate([exp_high, exp_scores - exp_high], axis=0).astype(bf16)
    in_parts = jnp.dot(halves, tok_buf[...], preferred_element_type=f32)
    message_ref[:, :width] = (in_parts[:experts] + in_parts[experts:]).astype(bf16)
    total = as_row(jnp.sum(exp_scores, axis=1, keepdims=True), LANES)
    high = total.astype(bf16).astype(f32)
    total = jnp.concatenate([high, total - high], axis=1).astype(bf16)
    message_ref[:, 2 * width :] = jnp.broadcast_to(total, (experts, 2 * LANES))
    exp_ref[...] = exp_scores
    combine_ref[...] = combine
    for copy in cot_copies:
        copy.wait()
    cot_part = jnp.dot(combine, cot_buf[...], preferred_element_type=f32)
    message_ref[:, width : 2 * width] = cot_part.astype(bf16)


def fetch(in_ref, out_ref, in_buf, out_buf, sems):
    copies = []
    for which, (source, target) in enumerate([(in_ref, in_buf), (out_ref, out_buf)]):
        rows = source.shape[0] // sems.shape[1]
        for index in range(sems.shape[1]):
            piece = pl.ds(index * rows, rows)
            copies.append(
                pltpu.make_async_copy(source.at[piece], target.at[piece], sems.at[which, index])
            )
    for copy in copies:
        copy.start()
    for copy in copies:
        copy.wait()


def expert_rows(owned_ref, sums_ref, in_ref, out_ref, message_ref, totals_ref, row_x_ref, row_cot_ref, hidden_ref, pre_grad_ref):
    width, units = in_ref.shape
    totals = sums_ref[:, 2 * width : 2 * width + LANES] + sums_ref[:, 2 * width + LANES :]
    lane = lax.broadcasted_iota(jnp.int32, totals.shape, 1)
    own_total = jnp.sum(jnp.where(lane == owned_ref[0], totals, 0.0), axis=1, keepdims=True)
    own_in = sums_ref[:, :width] / own_total
    row_x = own_in.astype(bf16)
    row_cot = sums_ref[:, width : 2 * width].astype(bf16)
    pre_act = jnp.dot(row_x, in_ref[...], preferred_element_type=f32)
    hid_grad = lax.dot_general(row_cot, out_ref[...], ROWS, preferred_element_type=f32)
    cdf = 0.5 * (1.0 + lax.erf(pre_act * 0.7071067811865476))
    hidden = (pre_act * cdf).astype(bf16)
    slope = cdf + pre_act * jnp.exp(-0.5 * pre_act * pre_act) * 0.3989422804014327
    pre_grad = (hid_grad * slope).astype(bf16)
    part_out = jnp.dot(hidden, out_ref[...], preferred_element_type=f32)
    part_dx = lax.dot_general(pre_grad, in_ref[...], ROWS, preferred_element_type=f32)
    message_ref[:, :width] = part_out
    message_ref[:, width : 2 * width] = part_dx
    dot_part = jnp.sum(own_in * part_dx, axis=1, keepdims=True)
    message_ref[:, 2 * width :] = jnp.broadcast_to(dot_part, (totals.shape[0], 2 * LANES))
    totals_ref[...] = totals
    row_x_ref[...] = row_x
    row_cot_ref[...] = row_cot
    hidden_ref[...] = hidden
    pre_grad_ref[...] = pre_grad


def as_row(column, lanes):
    shape = (column.shape[0], lanes)
    same = lax.broadcasted_iota(jnp.int32, shape, 0) == lax.broadcasted_iota(jnp.int32, shape, 1)
    return jnp.sum(jnp.where(same, column, 0.0), axis=0, keepdims=True)


def as_column(row, slots):
    shape = (slots, row.shape[1])
    same = lax.broadcasted_iota(jnp.int32, shape, 0) == lax.broadcasted_iota(jnp.int32, shape, 1)
    return jnp.sum(jnp.where(same, row, 0.0), axis=1, keepdims=True)


def score_grads(scale_ref, slots_ref, totals_ref, tok_ref, cot_ref, norm_ref, exp_ref, grad_ref, dispatch_ref, phi_ref):
    width = tok_ref.shape[1]
    slot_y = slots_ref[:, :width].astype(bf16)
    slot_dx = slots_ref[:, width : 2 * width].astype(bf16)
    low = 2 * width + LANES
    column_stat = slots_ref[:, 2 * width : 2 * width + 1] + slots_ref[:, low : low + 1]
    totals = as_column(totals_ref[...], slot_y.shape[0])
    exp_scores = exp_ref[...]
    combine_f = exp_scores / jnp.sum(exp_scores, axis=0, keepdims=True)
    comb_dot = lax.dot_general(slot_y, cot_ref[...], ROWS, preferred_element_type=f32)
    grad_comb = combine_f * (comb_dot - jnp.sum(combine_f * comb_dot, axis=0, keepdims=True))
    disp_dot = lax.dot_general(slot_dx, tok_ref[...], ROWS, preferred_element_type=f32)
    dispatch_f = exp_scores / totals
    grad_disp = dispatch_f * (disp_dot - column_stat)
    score_grad = (scale_ref[0] * (grad_comb + grad_disp)).astype(bf16)
    phi_ref[...] = jnp.dot(score_grad, norm_ref[...], preferred_element_type=f32)
    grad_ref[...] = score_grad
    dispatch_ref[...] = dispatch_f.astype(bf16)


def finish(phi_ref, *refs):
    *term_refs, grad_ref = refs
    own, *others = [ref[0] for ref in term_refs]
    phi_grad = own + others[-1]
    if len(others) > 1:
        phi_grad = phi_grad + (others[0] + others[1])
    phi = phi_ref[...].astype(f32)
    phi_scale = lax.rsqrt(jnp.sum(phi * phi, axis=1, keepdims=True) + epsilon)
    phi_unit = phi * phi_scale
    along = jnp.sum(phi_unit * phi_grad, axis=1, keepdims=True)
    grad_ref[...] = phi_scale * (phi_grad - phi_unit * along)


def in_place(operand):
    return pltpu.with_memory_space_constraint(operand, pltpu.HBM)


def per_device(tokens, cotangent, router, logit_scale, expert_in, expert_out):
    tok_in = tokens[0]
    tok_cot = cotangent[0]
    count = tok_in.shape[0]
    width, experts = router.shape
    units = expert_in.shape[1]
    size = lax.axis_size("seq")
    group = size // experts
    clips = lax.axis_size("dp")
    clip = lax.axis_index("dp")
    owned = lax.axis_index("seq") // group
    length = 2 * width + 2 * LANES
    scalar = pl.BlockSpec(memory_space=pltpu.SMEM)
    in_vmem = pl.BlockSpec(memory_space=pltpu.VMEM)
    in_hbm = pl.BlockSpec(memory_space=pltpu.HBM)
    params = pltpu.CompilerParams(vmem_limit_bytes=VMEM_BYTES)
    phi = router.T
    message, exp_scores, combine, tok_scale, tok_norm = pl.pallas_call(
        token_sums,
        in_specs=[scalar, in_hbm, in_hbm, in_hbm],
        out_shape=[
            jax.ShapeDtypeStruct((experts, length), bf16),
            jax.ShapeDtypeStruct((experts, count), f32),
            jax.ShapeDtypeStruct((experts, count), bf16),
            jax.ShapeDtypeStruct((count, 1), f32),
            jax.ShapeDtypeStruct((count, width), bf16),
        ],
        scratch_shapes=[
            pltpu.VMEM((experts, width), bf16),
            pltpu.VMEM((count, width), bf16),
            pltpu.VMEM((count, width), bf16),
            pltpu.SemaphoreType.DMA,
            pltpu.SemaphoreType.DMA((2, PIECES)),
        ],
        compiler_params=params,
        name="token_sums",
    )(logit_scale, in_place(phi), in_place(tok_in), in_place(tok_cot))
    message = of_clips(message)
    message, expert_in, expert_out = lax.optimization_barrier((message, expert_in, expert_out))
    expert_in, expert_out = pl.pallas_call(
        fetch,
        in_specs=[in_hbm] * 2,
        out_specs=[in_vmem] * 2,
        out_shape=[
            jax.ShapeDtypeStruct(expert_in.shape, bf16),
            jax.ShapeDtypeStruct(expert_out.shape, bf16),
        ],
        scratch_shapes=[pltpu.SemaphoreType.DMA((2, PIECES))],
        compiler_params=params,
        cost_estimate=pl.CostEstimate(
            flops=0, bytes_accessed=4 * expert_in.size + 4 * expert_out.size, transcendentals=0
        ),
        name="fetch_weights",
    )(in_place(expert_in), in_place(expert_out))
    message, expert_in, expert_out = sum_to_owner(message, group, (expert_in, expert_out))
    message = message[0]
    message, totals, row_x, row_cot, hidden, pre_grad = pl.pallas_call(
        expert_rows,
        in_specs=[scalar] + [in_vmem] * 3,
        out_shape=[
            jax.ShapeDtypeStruct((clips, length), f32),
            jax.ShapeDtypeStruct((clips, LANES), f32),
            jax.ShapeDtypeStruct((clips, width), bf16),
            jax.ShapeDtypeStruct((clips, width), bf16),
            jax.ShapeDtypeStruct((clips, units), bf16),
            jax.ShapeDtypeStruct((clips, units), bf16),
        ],
        compiler_params=params,
        name="expert_rows",
    )(owned[None], message, expert_in, expert_out)
    message, hidden, row_cot = sum_to_all(message[None], group, (hidden, row_cot))
    slots = lax.dynamic_index_in_dim(message, clip, 1, keepdims=False)
    totals = lax.dynamic_index_in_dim(totals, clip, 0, keepdims=True)
    share = width // clips
    mine_x = lax.dynamic_slice_in_dim(row_x, clip * share, share, 1)
    mine_cot = lax.dynamic_slice_in_dim(row_cot, clip * share, share, 1)
    grad_expert_in = jnp.einsum("od,oh->dh", mine_x, pre_grad, preferred_element_type=f32)
    grad_expert_out = jnp.einsum("oh,od->hd", hidden, mine_cot, preferred_element_type=f32)
    score_grad, dispatch, phi_part = pl.pallas_call(
        score_grads,
        in_specs=[scalar] + [in_vmem] * 6,
        out_shape=[
            jax.ShapeDtypeStruct((experts, count), bf16),
            jax.ShapeDtypeStruct((experts, count), bf16),
            jax.ShapeDtypeStruct((experts, width), f32),
        ],
        compiler_params=params,
        name="score_grads",
    )(logit_scale, slots, totals, tok_in, tok_cot, tok_norm, exp_scores)
    phi_sum = phi_part
    for step in range(1, clips):
        phi_sum = phi_sum + hop(phi_part, step)
    phi_sum = phi_sum[None]
    *earlier, final = rounds(size)
    for pair in earlier:
        phi_sum = added(round_terms(phi_sum, pair), pair)
    terms = round_terms(phi_sum, final)
    grad_router = pl.pallas_call(
        finish,
        in_specs=[in_vmem] * (1 + len(terms)),
        out_shape=jax.ShapeDtypeStruct((experts, width), f32),
        compiler_params=params,
        name="finish",
    )(phi, terms[0], *[terms[mask] for mask in [*final[1:], sum(final), final[0]][-len(terms) + 1 :]])
    phi_f32 = phi.astype(f32)
    phi_scale = lax.rsqrt(jnp.sum(phi_f32 * phi_f32, axis=1, keepdims=True) + epsilon)
    phi_unit = phi_f32 * phi_scale
    phi_norm = phi_unit.astype(bf16)
    slot_y = slots[:, :width].astype(bf16)
    slot_dx = slots[:, width : 2 * width].astype(bf16)
    mixed = jnp.einsum("sn,sd->nd", combine, slot_y, preferred_element_type=f32).astype(bf16)
    norm_grad = jnp.einsum("sn,sd->nd", score_grad, phi_norm, preferred_element_type=f32)
    through = jnp.einsum("sn,sd->nd", dispatch, slot_dx, preferred_element_type=f32)
    tok_unit = tok_in.astype(f32) * tok_scale
    back_norm = tok_scale * (
        norm_grad - tok_unit * jnp.sum(tok_unit * norm_grad, axis=1, keepdims=True)
    )
    grad_tokens = (through + back_norm).astype(bf16)
    return (mixed[None], grad_tokens[None], grad_expert_in, grad_expert_out, grad_router.T)


def solution(mesh):
    return jax.shard_map(
        per_device,
        mesh=mesh,
        in_specs=(
            P("dp", "seq", None),
            P("dp", "seq", None),
            P(),
            P(),
            P(None, "seq"),
            P("seq", None),
        ),
        out_specs=(P("dp", "seq", None), P("dp", "seq", None), P("dp", "seq"), P("seq", "dp"), P()),
        check_vma=False,
    )
```

```python
import jax
import jax.numpy as jnp
from jax import lax
from jax.experimental import pallas as pl
from jax.experimental.pallas import tpu as pltpu
from jax.sharding import PartitionSpec as P

epsilon = 1e-06
AXES = ("seq", "dp")
LANES = 128
PIECES = 4
VMEM_BYTES = 10 * 2**20
ROWS = (((1,), (1,)), ((), ()))
COLUMNS = (((0,), (0,)), ((), ()))
f32, bf16 = jnp.float32, jnp.bfloat16


def exchange(value, mask):
    clips = lax.axis_size("dp")
    pairs = []
    for place in range(lax.axis_size("seq")):
        for clip in range(clips):
            there = (place ^ mask) * clips + (clip ^ 1 if clips % 2 == 0 else clip)
            pairs.append((place * clips + clip, there))
    return lax.ppermute(value, AXES, pairs)


def hop(value, step):
    return lax.ppermute(value, "dp", [(i, i ^ step) for i in range(lax.axis_size("dp"))])


def of_clips(value):
    clips = lax.axis_size("dp")
    apart = lax.broadcasted_iota(jnp.int32, (1, clips, 1), 1) ^ lax.axis_index("dp")
    merged = value[:, None]
    for step in range(1, clips):
        merged = jnp.where(apart == step, hop(value, step)[:, None], merged)
    return merged


def rounds(size):
    masks = [1 << bit for bit in range(size.bit_length() - 1)]
    return [masks[i : i + 2] for i in range(0, len(masks), 2)]


def swaps(pair):
    return pair if len(pair) == 1 else [pair[0], pair[0] | pair[1], pair[1]]


def added(terms, masks):
    if len(masks) == 1:
        return terms[0] + terms[masks[0]]
    low, high = masks
    return (terms[0] + terms[low]) + (terms[high] + terms[low | high])


def sum_to_owner(value, group):
    place = lax.axis_index("seq")
    for pair in reversed(rounds(lax.axis_size("seq"))):
        owner_masks = [mask for mask in pair if mask >= group]
        blocks = value.reshape((1 << len(owner_masks), -1) + value.shape[1:])

        def block_for(mask):
            index = 0
            for bit, owner_mask in enumerate(owner_masks):
                index = index + jnp.where((place ^ mask) & owner_mask != 0, 1 << bit, 0)
            return lax.dynamic_index_in_dim(blocks, index, 0, keepdims=False)

        terms = {0: block_for(0)}
        for mask in swaps(pair):
            terms[mask] = exchange(block_for(mask), mask)
        value = added(terms, pair)
    return value


def round_terms(value, pair):
    terms = {0: value}
    for mask in swaps(pair):
        terms[mask] = exchange(value, mask)
    return terms


def sum_to_all(value, group, later=()):
    place = lax.axis_index("seq")
    for pair in rounds(lax.axis_size("seq")):
        terms = round_terms(value, pair)
        inner = [mask for mask in pair if mask < group]
        outer = [mask for mask in pair if mask >= group]
        if inner:
            merged = {}
            for far in [0] + outer if len(outer) == 1 else [0]:
                merged[far] = added({mask ^ far: terms[mask] for mask in terms}, inner)
            terms = merged
        value = terms[0]
        for mask in outer:
            kept = {}
            for key in terms:
                if key & mask:
                    continue
                side = lax.broadcasted_iota(jnp.int32, (2,) + (1,) * value.ndim, 0)
                same = side == jnp.where((place & mask) != 0, 1, 0)
                both = jnp.where(same, terms[key][None], terms[key | mask][None])
                kept[key] = both.reshape((-1,) + both.shape[2:])
            terms = kept
            value = terms[0]
        if later and pair[0] == 1:
            value, *later = lax.optimization_barrier((value, *later))
    return (value, *later) if later else value


def token_sums(scale_ref, phi_ref, tok_ref, cot_ref, message_ref, exp_ref, combine_ref, tok_scale_ref, norm_ref, phi_buf, tok_buf, cot_buf, phi_sem, sems):
    experts, width = phi_ref.shape
    blocks = sems.shape[1]
    rows = tok_buf.shape[0] // blocks
    pieces = [pl.ds(index * rows, rows) for index in range(blocks)]
    phi_copy = pltpu.make_async_copy(phi_ref, phi_buf, phi_sem)
    tok_copies = [
        pltpu.make_async_copy(tok_ref.at[piece], tok_buf.at[piece], sems.at[0, index])
        for index, piece in enumerate(pieces)
    ]
    cot_copies = [
        pltpu.make_async_copy(cot_ref.at[piece], cot_buf.at[piece], sems.at[1, index])
        for index, piece in enumerate(pieces)
    ]
    for copy in tok_copies + [phi_copy] + cot_copies:
        copy.start()
    for index in range(0, blocks, 2):
        for copy in tok_copies[index : index + 2]:
            copy.wait()
        piece = pl.ds(index * rows, 2 * rows)
        tok_f32 = tok_buf[piece, :].astype(f32)
        tok_scale = lax.rsqrt(jnp.sum(tok_f32 * tok_f32, axis=1, keepdims=True) + epsilon)
        norm_ref[piece, :] = (tok_f32 * tok_scale).astype(bf16)
        tok_scale_ref[piece, :] = tok_scale
    phi_copy.wait()
    phi = phi_buf[...].astype(f32)
    phi_scale = lax.rsqrt(jnp.sum(phi * phi, axis=1, keepdims=True) + epsilon)
    phi_norm = (phi * phi_scale).astype(bf16)
    logits = scale_ref[0] * lax.dot_general(phi_norm, norm_ref[...], ROWS, preferred_element_type=f32)
    exp_scores = jnp.exp(logits)
    combine = (exp_scores / jnp.sum(exp_scores, axis=0, keepdims=True)).astype(bf16)
    exp_high = exp_scores.astype(bf16).astype(f32)
    halves = jnp.concatenate([exp_high, exp_scores - exp_high], axis=0).astype(bf16)
    in_parts = jnp.dot(halves, tok_buf[...], preferred_element_type=f32)
    message_ref[:, :width] = in_parts[:experts] + in_parts[experts:]
    spare = message_ref.shape[1] - 2 * width
    total = as_row(jnp.sum(exp_scores, axis=1, keepdims=True), spare)
    message_ref[:, 2 * width :] = jnp.broadcast_to(total, (experts, spare))
    exp_ref[...] = exp_scores
    combine_ref[...] = combine
    for copy in cot_copies:
        copy.wait()
    message_ref[:, width : 2 * width] = jnp.dot(combine, cot_buf[...], preferred_element_type=f32)


def fetch(in_ref, out_ref, in_buf, out_buf, sems):
    copies = []
    for which, (source, target) in enumerate([(in_ref, in_buf), (out_ref, out_buf)]):
        rows = source.shape[0] // sems.shape[1]
        for index in range(sems.shape[1]):
            piece = pl.ds(index * rows, rows)
            copies.append(
                pltpu.make_async_copy(source.at[piece], target.at[piece], sems.at[which, index])
            )
    for copy in copies:
        copy.start()
    for copy in copies:
        copy.wait()


def expert_rows(owned_ref, sums_ref, in_ref, out_ref, message_ref, row_x_ref, row_cot_ref, hidden_ref, pre_grad_ref):
    width, units = in_ref.shape
    spare = sums_ref[:, 2 * width :]
    lane = lax.broadcasted_iota(jnp.int32, spare.shape, 1)
    own_total = jnp.sum(jnp.where(lane == owned_ref[0], spare, 0.0), axis=1, keepdims=True)
    own_in = sums_ref[:, :width] / own_total
    row_x = own_in.astype(bf16)
    row_cot = sums_ref[:, width : 2 * width].astype(bf16)
    pre_act = jnp.dot(row_x, in_ref[...], preferred_element_type=f32)
    hid_grad = lax.dot_general(row_cot, out_ref[...], ROWS, preferred_element_type=f32)
    cdf = 0.5 * (1.0 + lax.erf(pre_act * 0.7071067811865476))
    hidden = (pre_act * cdf).astype(bf16)
    slope = cdf + pre_act * jnp.exp(-0.5 * pre_act * pre_act) * 0.3989422804014327
    pre_grad = (hid_grad * slope).astype(bf16)
    part_out = jnp.dot(hidden, out_ref[...], preferred_element_type=f32)
    part_dx = lax.dot_general(pre_grad, in_ref[...], ROWS, preferred_element_type=f32)
    message_ref[:, :width] = part_out
    message_ref[:, width : 2 * width] = part_dx
    dot_part = jnp.sum(own_in * part_dx, axis=1, keepdims=True)
    message_ref[:, 2 * width :] = jnp.broadcast_to(dot_part, spare.shape)
    row_x_ref[...] = row_x
    row_cot_ref[...] = row_cot
    hidden_ref[...] = hidden
    pre_grad_ref[...] = pre_grad


def as_row(column, lanes):
    shape = (column.shape[0], lanes)
    same = lax.broadcasted_iota(jnp.int32, shape, 0) == lax.broadcasted_iota(jnp.int32, shape, 1)
    return jnp.sum(jnp.where(same, column, 0.0), axis=0, keepdims=True)


def as_column(row, slots):
    shape = (slots, row.shape[1])
    same = lax.broadcasted_iota(jnp.int32, shape, 0) == lax.broadcasted_iota(jnp.int32, shape, 1)
    return jnp.sum(jnp.where(same, row, 0.0), axis=1, keepdims=True)


def score_grads(scale_ref, slots_ref, totals_ref, tok_ref, cot_ref, norm_ref, exp_ref, grad_ref, dispatch_ref, phi_ref):
    width = tok_ref.shape[1]
    slot_y = slots_ref[:, :width].astype(bf16)
    slot_dx = slots_ref[:, width : 2 * width].astype(bf16)
    column_stat = slots_ref[:, 2 * width : 2 * width + 1]
    totals = as_column(totals_ref[...], slot_y.shape[0])
    exp_scores = exp_ref[...]
    combine_f = exp_scores / jnp.sum(exp_scores, axis=0, keepdims=True)
    comb_dot = lax.dot_general(slot_y, cot_ref[...], ROWS, preferred_element_type=f32)
    grad_comb = combine_f * (comb_dot - jnp.sum(combine_f * comb_dot, axis=0, keepdims=True))
    disp_dot = lax.dot_general(slot_dx, tok_ref[...], ROWS, preferred_element_type=f32)
    dispatch_f = exp_scores / totals
    grad_disp = dispatch_f * (disp_dot - column_stat)
    score_grad = (scale_ref[0] * (grad_comb + grad_disp)).astype(bf16)
    phi_ref[...] = jnp.dot(score_grad, norm_ref[...], preferred_element_type=f32)
    grad_ref[...] = score_grad
    dispatch_ref[...] = dispatch_f.astype(bf16)


def finish(phi_ref, *refs):
    *term_refs, grad_ref = refs
    own, *others = [ref[0] for ref in term_refs]
    phi_grad = own + others[-1]
    if len(others) > 1:
        phi_grad = phi_grad + (others[0] + others[1])
    phi = phi_ref[...].astype(f32)
    phi_scale = lax.rsqrt(jnp.sum(phi * phi, axis=1, keepdims=True) + epsilon)
    phi_unit = phi * phi_scale
    along = jnp.sum(phi_unit * phi_grad, axis=1, keepdims=True)
    grad_ref[...] = phi_scale * (phi_grad - phi_unit * along)


def in_place(operand):
    return pltpu.with_memory_space_constraint(operand, pltpu.HBM)


def per_device(tokens, cotangent, router, logit_scale, expert_in, expert_out):
    tok_in = tokens[0]
    tok_cot = cotangent[0]
    count = tok_in.shape[0]
    width, experts = router.shape
    units = expert_in.shape[1]
    size = lax.axis_size("seq")
    group = size // experts
    clips = lax.axis_size("dp")
    clip = lax.axis_index("dp")
    owned = lax.axis_index("seq") // group
    length = 2 * width + -(-experts // LANES) * LANES
    scalar = pl.BlockSpec(memory_space=pltpu.SMEM)
    in_vmem = pl.BlockSpec(memory_space=pltpu.VMEM)
    in_hbm = pl.BlockSpec(memory_space=pltpu.HBM)
    params = pltpu.CompilerParams(vmem_limit_bytes=VMEM_BYTES)
    phi = router.T
    message, exp_scores, combine, tok_scale, tok_norm = pl.pallas_call(
        token_sums,
        in_specs=[scalar, in_hbm, in_hbm, in_hbm],
        out_shape=[
            jax.ShapeDtypeStruct((experts, length), f32),
            jax.ShapeDtypeStruct((experts, count), f32),
            jax.ShapeDtypeStruct((experts, count), bf16),
            jax.ShapeDtypeStruct((count, 1), f32),
            jax.ShapeDtypeStruct((count, width), bf16),
        ],
        scratch_shapes=[
            pltpu.VMEM((experts, width), bf16),
            pltpu.VMEM((count, width), bf16),
            pltpu.VMEM((count, width), bf16),
            pltpu.SemaphoreType.DMA,
            pltpu.SemaphoreType.DMA((2, PIECES)),
        ],
        compiler_params=params,
        name="token_sums",
    )(logit_scale, in_place(phi), in_place(tok_in), in_place(tok_cot))
    message = of_clips(message)
    message, expert_in, expert_out = lax.optimization_barrier((message, expert_in, expert_out))
    expert_in, expert_out = pl.pallas_call(
        fetch,
        in_specs=[in_hbm] * 2,
        out_specs=[in_vmem] * 2,
        out_shape=[
            jax.ShapeDtypeStruct(expert_in.shape, bf16),
            jax.ShapeDtypeStruct(expert_out.shape, bf16),
        ],
        scratch_shapes=[pltpu.SemaphoreType.DMA((2, PIECES))],
        compiler_params=params,
        cost_estimate=pl.CostEstimate(
            flops=0, bytes_accessed=4 * expert_in.size + 4 * expert_out.size, transcendentals=0
        ),
        name="fetch_weights",
    )(in_place(expert_in), in_place(expert_out))
    message = sum_to_owner(message, group)[0]
    totals = message[:, 2 * width :]
    message, row_x, row_cot, hidden, pre_grad = pl.pallas_call(
        expert_rows,
        in_specs=[scalar] + [in_vmem] * 3,
        out_shape=[
            jax.ShapeDtypeStruct((clips, length), f32),
            jax.ShapeDtypeStruct((clips, width), bf16),
            jax.ShapeDtypeStruct((clips, width), bf16),
            jax.ShapeDtypeStruct((clips, units), bf16),
            jax.ShapeDtypeStruct((clips, units), bf16),
        ],
        compiler_params=params,
        name="expert_rows",
    )(owned[None], message, expert_in, expert_out)
    message, hidden, row_cot = sum_to_all(message[None], group, (hidden, row_cot))
    slots = lax.dynamic_index_in_dim(message, clip, 1, keepdims=False)
    totals = lax.dynamic_index_in_dim(totals, clip, 0, keepdims=True)
    share = width // clips
    mine_x = lax.dynamic_slice_in_dim(row_x, clip * share, share, 1)
    mine_cot = lax.dynamic_slice_in_dim(row_cot, clip * share, share, 1)
    grad_expert_in = jnp.einsum("od,oh->dh", mine_x, pre_grad, preferred_element_type=f32)
    grad_expert_out = jnp.einsum("oh,od->hd", hidden, mine_cot, preferred_element_type=f32)
    score_grad, dispatch, phi_part = pl.pallas_call(
        score_grads,
        in_specs=[scalar] + [in_vmem] * 6,
        out_shape=[
            jax.ShapeDtypeStruct((experts, count), bf16),
            jax.ShapeDtypeStruct((experts, count), bf16),
            jax.ShapeDtypeStruct((experts, width), f32),
        ],
        compiler_params=params,
        name="score_grads",
    )(logit_scale, slots, totals, tok_in, tok_cot, tok_norm, exp_scores)
    phi_sum = phi_part
    for step in range(1, clips):
        phi_sum = phi_sum + hop(phi_part, step)
    phi_sum = phi_sum[None]
    *earlier, final = rounds(size)
    for pair in earlier:
        phi_sum = added(round_terms(phi_sum, pair), pair)
    terms = round_terms(phi_sum, final)
    grad_router = pl.pallas_call(
        finish,
        in_specs=[in_vmem] * (1 + len(terms)),
        out_shape=jax.ShapeDtypeStruct((experts, width), f32),
        compiler_params=params,
        name="finish",
    )(phi, terms[0], *[terms[mask] for mask in [*final[1:], sum(final), final[0]][-len(terms) + 1 :]])
    phi_f32 = phi.astype(f32)
    phi_scale = lax.rsqrt(jnp.sum(phi_f32 * phi_f32, axis=1, keepdims=True) + epsilon)
    phi_unit = phi_f32 * phi_scale
    phi_norm = phi_unit.astype(bf16)
    slot_y = slots[:, :width].astype(bf16)
    slot_dx = slots[:, width : 2 * width].astype(bf16)
    mixed = jnp.einsum("sn,sd->nd", combine, slot_y, preferred_element_type=f32).astype(bf16)
    norm_grad = jnp.einsum("sn,sd->nd", score_grad, phi_norm, preferred_element_type=f32)
    through = jnp.einsum("sn,sd->nd", dispatch, slot_dx, preferred_element_type=f32)
    tok_unit = tok_in.astype(f32) * tok_scale
    back_norm = tok_scale * (
        norm_grad - tok_unit * jnp.sum(tok_unit * norm_grad, axis=1, keepdims=True)
    )
    grad_tokens = (through + back_norm).astype(bf16)
    return (mixed[None], grad_tokens[None], grad_expert_in, grad_expert_out, grad_router.T)


def solution(mesh):
    return jax.shard_map(
        per_device,
        mesh=mesh,
        in_specs=(
            P("dp", "seq", None),
            P("dp", "seq", None),
            P(),
            P(),
            P(None, "seq"),
            P("seq", None),
        ),
        out_specs=(P("dp", "seq", None), P("dp", "seq", None), P("dp", "seq"), P("seq", "dp"), P()),
        check_vma=False,
    )
```

```python
import jax
import jax.numpy as jnp
from jax import lax
from jax.experimental import pallas as pl
from jax.experimental.pallas import tpu as pltpu
from jax.sharding import PartitionSpec as P

epsilon = 1e-06
AXES = ("seq", "dp")
LANES = 128
PIECES = 4
VMEM_BYTES = 10 * 2**20
ROWS = (((1,), (1,)), ((), ()))
COLUMNS = (((0,), (0,)), ((), ()))
f32, bf16 = jnp.float32, jnp.bfloat16


def exchange(value, mask):
    clips = lax.axis_size("dp")
    pairs = []
    for place in range(lax.axis_size("seq")):
        for clip in range(clips):
            there = (place ^ mask) * clips + (clip ^ 1 if clips % 2 == 0 else clip)
            pairs.append((place * clips + clip, there))
    return lax.ppermute(value, AXES, pairs)


def hop(value, step):
    return lax.ppermute(value, "dp", [(i, i ^ step) for i in range(lax.axis_size("dp"))])


def of_clips(value):
    clips = lax.axis_size("dp")
    apart = lax.broadcasted_iota(jnp.int32, (1, clips, 1), 1) ^ lax.axis_index("dp")
    merged = value[:, None]
    for step in range(1, clips):
        merged = jnp.where(apart == step, hop(value, step)[:, None], merged)
    return merged


def rounds(size):
    masks = [1 << bit for bit in range(size.bit_length() - 1)]
    return [masks[i : i + 2] for i in range(0, len(masks), 2)]


def swaps(pair):
    return pair if len(pair) == 1 else [pair[0], pair[0] | pair[1], pair[1]]


def added(terms, masks):
    if len(masks) == 1:
        return terms[0] + terms[masks[0]]
    low, high = masks
    others = [terms[low | high], terms[high]]
    first, second = others if low == 1 else others[::-1]
    return (terms[0] + terms[low]) + (first + second)


def sum_to_owner(value, group):
    place = lax.axis_index("seq")
    for pair in reversed(rounds(lax.axis_size("seq"))):
        owner_masks = [mask for mask in pair if mask >= group]
        blocks = value.reshape((1 << len(owner_masks), -1) + value.shape[1:])

        def block_for(mask):
            index = 0
            for bit, owner_mask in enumerate(owner_masks):
                index = index + jnp.where((place ^ mask) & owner_mask != 0, 1 << bit, 0)
            return lax.dynamic_index_in_dim(blocks, index, 0, keepdims=False)

        terms = {0: block_for(0)}
        for mask in swaps(pair):
            terms[mask] = exchange(block_for(mask), mask)
        value = added(terms, pair)
    return value


def round_terms(value, pair):
    terms = {0: value}
    for mask in swaps(pair):
        terms[mask] = exchange(value, mask)
    return terms


def sum_to_all(value, group, later=()):
    place = lax.axis_index("seq")
    for pair in rounds(lax.axis_size("seq")):
        terms = round_terms(value, pair)
        inner = [mask for mask in pair if mask < group]
        outer = [mask for mask in pair if mask >= group]
        if inner:
            merged = {}
            for far in [0] + outer if len(outer) == 1 else [0]:
                merged[far] = added({mask ^ far: terms[mask] for mask in terms}, inner)
            terms = merged
        value = terms[0]
        for mask in outer:
            kept = {}
            for key in terms:
                if key & mask:
                    continue
                side = lax.broadcasted_iota(jnp.int32, (2,) + (1,) * value.ndim, 0)
                same = side == jnp.where((place & mask) != 0, 1, 0)
                both = jnp.where(same, terms[key][None], terms[key | mask][None])
                kept[key] = both.reshape((-1,) + both.shape[2:])
            terms = kept
            value = terms[0]
        if later and pair[0] == 1:
            value, *later = lax.optimization_barrier((value, *later))
    return (value, *later) if later else value


def token_sums(scale_ref, phi_ref, tok_ref, cot_ref, message_ref, exp_ref, combine_ref, tok_scale_ref, norm_ref, phi_buf, tok_buf, cot_buf, phi_sem, sems):
    experts, width = phi_ref.shape
    blocks = sems.shape[1]
    rows = tok_buf.shape[0] // blocks
    pieces = [pl.ds(index * rows, rows) for index in range(blocks)]
    phi_copy = pltpu.make_async_copy(phi_ref, phi_buf, phi_sem)
    tok_copies = [
        pltpu.make_async_copy(tok_ref.at[piece], tok_buf.at[piece], sems.at[0, index])
        for index, piece in enumerate(pieces)
    ]
    cot_copies = [
        pltpu.make_async_copy(cot_ref.at[piece], cot_buf.at[piece], sems.at[1, index])
        for index, piece in enumerate(pieces)
    ]
    for copy in tok_copies + [phi_copy] + cot_copies:
        copy.start()
    for index in range(0, blocks, 2):
        for copy in tok_copies[index : index + 2]:
            copy.wait()
        piece = pl.ds(index * rows, 2 * rows)
        tok_f32 = tok_buf[piece, :].astype(f32)
        tok_scale = lax.rsqrt(jnp.sum(tok_f32 * tok_f32, axis=1, keepdims=True) + epsilon)
        norm_ref[piece, :] = (tok_f32 * tok_scale).astype(bf16)
        tok_scale_ref[piece, :] = tok_scale
    phi_copy.wait()
    phi = phi_buf[...].astype(f32)
    phi_scale = lax.rsqrt(jnp.sum(phi * phi, axis=1, keepdims=True) + epsilon)
    phi_norm = (phi * phi_scale).astype(bf16)
    logits = scale_ref[0] * lax.dot_general(phi_norm, norm_ref[...], ROWS, preferred_element_type=f32)
    exp_scores = jnp.exp(logits)
    combine = (exp_scores / jnp.sum(exp_scores, axis=0, keepdims=True)).astype(bf16)
    exp_high = exp_scores.astype(bf16).astype(f32)
    halves = jnp.concatenate([exp_high, exp_scores - exp_high], axis=0).astype(bf16)
    in_parts = jnp.dot(halves, tok_buf[...], preferred_element_type=f32)
    message_ref[:, :width] = in_parts[:experts] + in_parts[experts:]
    spare = message_ref.shape[1] - 2 * width
    total = as_row(jnp.sum(exp_scores, axis=1, keepdims=True), spare)
    message_ref[:, 2 * width :] = jnp.broadcast_to(total, (experts, spare))
    exp_ref[...] = exp_scores
    combine_ref[...] = combine
    for copy in cot_copies:
        copy.wait()
    message_ref[:, width : 2 * width] = jnp.dot(combine, cot_buf[...], preferred_element_type=f32)


def fetch(in_ref, out_ref, in_buf, out_buf, sems):
    copies = []
    for which, (source, target) in enumerate([(in_ref, in_buf), (out_ref, out_buf)]):
        rows = source.shape[0] // sems.shape[1]
        for index in range(sems.shape[1]):
            piece = pl.ds(index * rows, rows)
            copies.append(
                pltpu.make_async_copy(source.at[piece], target.at[piece], sems.at[which, index])
            )
    for copy in copies:
        copy.start()
    for copy in copies:
        copy.wait()


def expert_rows(owned_ref, sums_ref, in_ref, out_ref, message_ref, row_x_ref, row_cot_ref, hidden_ref, pre_grad_ref):
    width, units = in_ref.shape
    spare = sums_ref[:, 2 * width :]
    lane = lax.broadcasted_iota(jnp.int32, spare.shape, 1)
    own_total = jnp.sum(jnp.where(lane == owned_ref[0], spare, 0.0), axis=1, keepdims=True)
    own_in = sums_ref[:, :width] / own_total
    row_x = own_in.astype(bf16)
    row_cot = sums_ref[:, width : 2 * width].astype(bf16)
    pre_act = jnp.dot(row_x, in_ref[...], preferred_element_type=f32)
    hid_grad = lax.dot_general(row_cot, out_ref[...], ROWS, preferred_element_type=f32)
    cdf = 0.5 * (1.0 + lax.erf(pre_act * 0.7071067811865476))
    hidden = (pre_act * cdf).astype(bf16)
    slope = cdf + pre_act * jnp.exp(-0.5 * pre_act * pre_act) * 0.3989422804014327
    pre_grad = (hid_grad * slope).astype(bf16)
    part_out = jnp.dot(hidden, out_ref[...], preferred_element_type=f32)
    part_dx = lax.dot_general(pre_grad, in_ref[...], ROWS, preferred_element_type=f32)
    message_ref[:, :width] = part_out
    message_ref[:, width : 2 * width] = part_dx
    dot_part = jnp.sum(own_in * part_dx, axis=1, keepdims=True)
    message_ref[:, 2 * width :] = jnp.broadcast_to(dot_part, spare.shape)
    row_x_ref[...] = row_x
    row_cot_ref[...] = row_cot
    hidden_ref[...] = hidden
    pre_grad_ref[...] = pre_grad


def as_row(column, lanes):
    shape = (column.shape[0], lanes)
    same = lax.broadcasted_iota(jnp.int32, shape, 0) == lax.broadcasted_iota(jnp.int32, shape, 1)
    return jnp.sum(jnp.where(same, column, 0.0), axis=0, keepdims=True)


def as_column(row, slots):
    shape = (slots, row.shape[1])
    same = lax.broadcasted_iota(jnp.int32, shape, 0) == lax.broadcasted_iota(jnp.int32, shape, 1)
    return jnp.sum(jnp.where(same, row, 0.0), axis=1, keepdims=True)


def score_grads(scale_ref, slots_ref, totals_ref, tok_ref, cot_ref, norm_ref, exp_ref, grad_ref, dispatch_ref, phi_ref):
    width = tok_ref.shape[1]
    slot_y = slots_ref[:, :width].astype(bf16)
    slot_dx = slots_ref[:, width : 2 * width].astype(bf16)
    column_stat = slots_ref[:, 2 * width : 2 * width + 1]
    totals = as_column(totals_ref[...], slot_y.shape[0])
    exp_scores = exp_ref[...]
    combine_f = exp_scores / jnp.sum(exp_scores, axis=0, keepdims=True)
    comb_dot = lax.dot_general(slot_y, cot_ref[...], ROWS, preferred_element_type=f32)
    grad_comb = combine_f * (comb_dot - jnp.sum(combine_f * comb_dot, axis=0, keepdims=True))
    disp_dot = lax.dot_general(slot_dx, tok_ref[...], ROWS, preferred_element_type=f32)
    dispatch_f = exp_scores / totals
    grad_disp = dispatch_f * (disp_dot - column_stat)
    score_grad = (scale_ref[0] * (grad_comb + grad_disp)).astype(bf16)
    phi_ref[...] = jnp.dot(score_grad, norm_ref[...], preferred_element_type=f32)
    grad_ref[...] = score_grad
    dispatch_ref[...] = dispatch_f.astype(bf16)


def finish(phi_ref, *refs):
    *term_refs, grad_ref = refs
    own, *others = [ref[0] for ref in term_refs]
    phi_grad = own + others[-1]
    if len(others) > 1:
        phi_grad = phi_grad + (others[0] + others[1])
    phi = phi_ref[...].astype(f32)
    phi_scale = lax.rsqrt(jnp.sum(phi * phi, axis=1, keepdims=True) + epsilon)
    phi_unit = phi * phi_scale
    along = jnp.sum(phi_unit * phi_grad, axis=1, keepdims=True)
    grad_ref[...] = phi_scale * (phi_grad - phi_unit * along)


def in_place(operand):
    return pltpu.with_memory_space_constraint(operand, pltpu.HBM)


def per_device(tokens, cotangent, router, logit_scale, expert_in, expert_out):
    tok_in = tokens[0]
    tok_cot = cotangent[0]
    count = tok_in.shape[0]
    width, experts = router.shape
    units = expert_in.shape[1]
    size = lax.axis_size("seq")
    group = size // experts
    clips = lax.axis_size("dp")
    clip = lax.axis_index("dp")
    owned = lax.axis_index("seq") // group
    length = 2 * width + -(-experts // LANES) * LANES
    scalar = pl.BlockSpec(memory_space=pltpu.SMEM)
    in_vmem = pl.BlockSpec(memory_space=pltpu.VMEM)
    in_hbm = pl.BlockSpec(memory_space=pltpu.HBM)
    params = pltpu.CompilerParams(vmem_limit_bytes=VMEM_BYTES)
    phi = router.T
    message, exp_scores, combine, tok_scale, tok_norm = pl.pallas_call(
        token_sums,
        in_specs=[scalar, in_hbm, in_hbm, in_hbm],
        out_shape=[
            jax.ShapeDtypeStruct((experts, length), f32),
            jax.ShapeDtypeStruct((experts, count), f32),
            jax.ShapeDtypeStruct((experts, count), bf16),
            jax.ShapeDtypeStruct((count, 1), f32),
            jax.ShapeDtypeStruct((count, width), bf16),
        ],
        scratch_shapes=[
            pltpu.VMEM((experts, width), bf16),
            pltpu.VMEM((count, width), bf16),
            pltpu.VMEM((count, width), bf16),
            pltpu.SemaphoreType.DMA,
            pltpu.SemaphoreType.DMA((2, PIECES)),
        ],
        compiler_params=params,
        name="token_sums",
    )(logit_scale, in_place(phi), in_place(tok_in), in_place(tok_cot))
    message = of_clips(message)
    message, expert_in, expert_out = lax.optimization_barrier((message, expert_in, expert_out))
    expert_in, expert_out = pl.pallas_call(
        fetch,
        in_specs=[in_hbm] * 2,
        out_specs=[in_vmem] * 2,
        out_shape=[
            jax.ShapeDtypeStruct(expert_in.shape, bf16),
            jax.ShapeDtypeStruct(expert_out.shape, bf16),
        ],
        scratch_shapes=[pltpu.SemaphoreType.DMA((2, PIECES))],
        compiler_params=params,
        cost_estimate=pl.CostEstimate(
            flops=0, bytes_accessed=4 * expert_in.size + 4 * expert_out.size, transcendentals=0
        ),
        name="fetch_weights",
    )(in_place(expert_in), in_place(expert_out))
    message = sum_to_owner(message, group)[0]
    totals = message[:, 2 * width :]
    message, row_x, row_cot, hidden, pre_grad = pl.pallas_call(
        expert_rows,
        in_specs=[scalar] + [in_vmem] * 3,
        out_shape=[
            jax.ShapeDtypeStruct((clips, length), f32),
            jax.ShapeDtypeStruct((clips, width), bf16),
            jax.ShapeDtypeStruct((clips, width), bf16),
            jax.ShapeDtypeStruct((clips, units), bf16),
            jax.ShapeDtypeStruct((clips, units), bf16),
        ],
        compiler_params=params,
        name="expert_rows",
    )(owned[None], message, expert_in, expert_out)
    message, hidden, row_cot = sum_to_all(message[None], group, (hidden, row_cot))
    slots = lax.dynamic_index_in_dim(message, clip, 1, keepdims=False)
    totals = lax.dynamic_index_in_dim(totals, clip, 0, keepdims=True)
    share = width // clips
    mine_x = lax.dynamic_slice_in_dim(row_x, clip * share, share, 1)
    mine_cot = lax.dynamic_slice_in_dim(row_cot, clip * share, share, 1)
    grad_expert_in = jnp.einsum("od,oh->dh", mine_x, pre_grad, preferred_element_type=f32)
    grad_expert_out = jnp.einsum("oh,od->hd", hidden, mine_cot, preferred_element_type=f32)
    score_grad, dispatch, phi_part = pl.pallas_call(
        score_grads,
        in_specs=[scalar] + [in_vmem] * 6,
        out_shape=[
            jax.ShapeDtypeStruct((experts, count), bf16),
            jax.ShapeDtypeStruct((experts, count), bf16),
            jax.ShapeDtypeStruct((experts, width), f32),
        ],
        compiler_params=params,
        name="score_grads",
    )(logit_scale, slots, totals, tok_in, tok_cot, tok_norm, exp_scores)
    phi_sum = phi_part
    for step in range(1, clips):
        phi_sum = phi_sum + hop(phi_part, step)
    phi_sum = phi_sum[None]
    *earlier, final = rounds(size)
    for pair in earlier:
        phi_sum = added(round_terms(phi_sum, pair), pair)
    terms = round_terms(phi_sum, final)
    grad_router = pl.pallas_call(
        finish,
        in_specs=[in_vmem] * (1 + len(terms)),
        out_shape=jax.ShapeDtypeStruct((experts, width), f32),
        compiler_params=params,
        name="finish",
    )(phi, terms[0], *[terms[mask] for mask in [*final[1:], sum(final), final[0]][-len(terms) + 1 :]])
    phi_f32 = phi.astype(f32)
    phi_scale = lax.rsqrt(jnp.sum(phi_f32 * phi_f32, axis=1, keepdims=True) + epsilon)
    phi_unit = phi_f32 * phi_scale
    phi_norm = phi_unit.astype(bf16)
    slot_y = slots[:, :width].astype(bf16)
    slot_dx = slots[:, width : 2 * width].astype(bf16)
    mixed = jnp.einsum("sn,sd->nd", combine, slot_y, preferred_element_type=f32).astype(bf16)
    norm_grad = jnp.einsum("sn,sd->nd", score_grad, phi_norm, preferred_element_type=f32)
    through = jnp.einsum("sn,sd->nd", dispatch, slot_dx, preferred_element_type=f32)
    tok_unit = tok_in.astype(f32) * tok_scale
    back_norm = tok_scale * (
        norm_grad - tok_unit * jnp.sum(tok_unit * norm_grad, axis=1, keepdims=True)
    )
    grad_tokens = (through + back_norm).astype(bf16)
    return (mixed[None], grad_tokens[None], grad_expert_in, grad_expert_out, grad_router.T)


def solution(mesh):
    return jax.shard_map(
        per_device,
        mesh=mesh,
        in_specs=(
            P("dp", "seq", None),
            P("dp", "seq", None),
            P(),
            P(),
            P(None, "seq"),
            P("seq", None),
        ),
        out_specs=(P("dp", "seq", None), P("dp", "seq", None), P("dp", "seq"), P("seq", "dp"), P()),
        check_vma=False,
    )
```

```python
import jax
import jax.numpy as jnp
from jax import lax
from jax.experimental import pallas as pl
from jax.experimental.pallas import tpu as pltpu
from jax.sharding import PartitionSpec as P

epsilon = 1e-06
AXES = ("seq", "dp")
LANES = 128
PIECES = 4
VMEM_BYTES = 10 * 2**20
ROWS = (((1,), (1,)), ((), ()))
COLUMNS = (((0,), (0,)), ((), ()))
f32, bf16 = jnp.float32, jnp.bfloat16


def exchange(value, mask):
    clips = lax.axis_size("dp")
    pairs = []
    for place in range(lax.axis_size("seq")):
        for clip in range(clips):
            there = (place ^ mask) * clips + (clip ^ 1 if clips % 2 == 0 else clip)
            pairs.append((place * clips + clip, there))
    return lax.ppermute(value, AXES, pairs)


def hop(value, step):
    return lax.ppermute(value, "dp", [(i, i ^ step) for i in range(lax.axis_size("dp"))])


def of_clips(value):
    clips = lax.axis_size("dp")
    apart = lax.broadcasted_iota(jnp.int32, (1, clips, 1), 1) ^ lax.axis_index("dp")
    merged = value[:, None]
    for step in range(1, clips):
        merged = jnp.where(apart == step, hop(value, step)[:, None], merged)
    return merged


def rounds(size):
    masks = [1 << bit for bit in range(size.bit_length() - 1)]
    return [masks[i : i + 2] for i in range(0, len(masks), 2)]


def swaps(pair):
    return pair if len(pair) == 1 else [pair[0], pair[0] | pair[1], pair[1]]


def added(terms, masks):
    if len(masks) == 1:
        return terms[0] + terms[masks[0]]
    low, high = masks
    others = [terms[low | high], terms[high]]
    first, second = others if low == 1 else others[::-1]
    return (terms[0] + terms[low]) + (first + second)


def sum_to_owner(value, group):
    place = lax.axis_index("seq")
    for pair in reversed(rounds(lax.axis_size("seq"))):
        owner_masks = [mask for mask in pair if mask >= group]
        blocks = value.reshape((1 << len(owner_masks), -1) + value.shape[1:])

        def block_for(mask):
            index = 0
            for bit, owner_mask in enumerate(owner_masks):
                index = index + jnp.where((place ^ mask) & owner_mask != 0, 1 << bit, 0)
            return lax.dynamic_index_in_dim(blocks, index, 0, keepdims=False)

        terms = {0: block_for(0)}
        for mask in swaps(pair):
            terms[mask] = exchange(block_for(mask), mask)
        value = added(terms, pair)
    return value


def round_terms(value, pair):
    terms = {0: value}
    for mask in swaps(pair):
        terms[mask] = exchange(value, mask)
    return terms


def sum_to_all(value, group, later=()):
    place = lax.axis_index("seq")
    for pair in rounds(lax.axis_size("seq")):
        terms = round_terms(value, pair)
        inner = [mask for mask in pair if mask < group]
        outer = [mask for mask in pair if mask >= group]
        if inner:
            merged = {}
            for far in [0] + outer if len(outer) == 1 else [0]:
                merged[far] = added({mask ^ far: terms[mask] for mask in terms}, inner)
            terms = merged
        value = terms[0]
        for mask in outer:
            kept = {}
            for key in terms:
                if key & mask:
                    continue
                side = lax.broadcasted_iota(jnp.int32, (2,) + (1,) * value.ndim, 0)
                same = side == jnp.where((place & mask) != 0, 1, 0)
                both = jnp.where(same, terms[key][None], terms[key | mask][None])
                kept[key] = both.reshape((-1,) + both.shape[2:])
            terms = kept
            value = terms[0]
        if later and pair[0] == 1:
            value, *later = lax.optimization_barrier((value, *later))
    return (value, *later) if later else value


def token_sums(scale_ref, phi_ref, tok_ref, cot_ref, message_ref, exp_ref, combine_ref, tok_scale_ref, norm_ref, phi_buf, tok_buf, cot_buf, phi_sem, sems):
    experts, width = phi_ref.shape
    blocks = sems.shape[1]
    rows = tok_buf.shape[0] // blocks
    pieces = [pl.ds(index * rows, rows) for index in range(blocks)]
    phi_copy = pltpu.make_async_copy(phi_ref, phi_buf, phi_sem)
    tok_copies = [
        pltpu.make_async_copy(tok_ref.at[piece], tok_buf.at[piece], sems.at[0, index])
        for index, piece in enumerate(pieces)
    ]
    cot_copies = [
        pltpu.make_async_copy(cot_ref.at[piece], cot_buf.at[piece], sems.at[1, index])
        for index, piece in enumerate(pieces)
    ]
    for copy in tok_copies + [phi_copy] + cot_copies:
        copy.start()
    for index in range(0, blocks, 2):
        for copy in tok_copies[index : index + 2]:
            copy.wait()
        piece = pl.ds(index * rows, 2 * rows)
        tok_f32 = tok_buf[piece, :].astype(f32)
        tok_scale = lax.rsqrt(jnp.sum(tok_f32 * tok_f32, axis=1, keepdims=True) + epsilon)
        norm_ref[piece, :] = (tok_f32 * tok_scale).astype(bf16)
        tok_scale_ref[piece, :] = tok_scale
    phi_copy.wait()
    phi = phi_buf[...].astype(f32)
    phi_scale = lax.rsqrt(jnp.sum(phi * phi, axis=1, keepdims=True) + epsilon)
    phi_norm = (phi * phi_scale).astype(bf16)
    logits = scale_ref[0] * lax.dot_general(phi_norm, norm_ref[...], ROWS, preferred_element_type=f32)
    exp_scores = jnp.exp(logits)
    combine = (exp_scores / jnp.sum(exp_scores, axis=0, keepdims=True)).astype(bf16)
    exp_high = exp_scores.astype(bf16).astype(f32)
    halves = jnp.concatenate([exp_high, exp_scores - exp_high], axis=0).astype(bf16)
    in_parts = jnp.dot(halves, tok_buf[...], preferred_element_type=f32)
    message_ref[:, :width] = in_parts[:experts] + in_parts[experts:]
    spare = message_ref.shape[1] - 2 * width
    total = as_row(jnp.sum(exp_scores, axis=1, keepdims=True), spare)
    message_ref[:, 2 * width :] = jnp.broadcast_to(total, (experts, spare))
    exp_ref[...] = exp_scores
    combine_ref[...] = combine
    for copy in cot_copies:
        copy.wait()
    message_ref[:, width : 2 * width] = jnp.dot(combine, cot_buf[...], preferred_element_type=f32)


def fetch(in_ref, out_ref, in_buf, out_buf, sems):
    copies = []
    for which, (source, target) in enumerate([(in_ref, in_buf), (out_ref, out_buf)]):
        rows = source.shape[0] // sems.shape[1]
        for index in range(sems.shape[1]):
            piece = pl.ds(index * rows, rows)
            copies.append(
                pltpu.make_async_copy(source.at[piece], target.at[piece], sems.at[which, index])
            )
    for copy in copies:
        copy.start()
    for copy in copies:
        copy.wait()


def expert_rows(owned_ref, sums_ref, in_ref, out_ref, message_ref, row_x_ref, row_cot_ref, hidden_ref, pre_grad_ref):
    width, units = in_ref.shape
    spare = sums_ref[:, 2 * width :]
    lane = lax.broadcasted_iota(jnp.int32, spare.shape, 1)
    own_total = jnp.sum(jnp.where(lane == owned_ref[0], spare, 0.0), axis=1, keepdims=True)
    own_in = sums_ref[:, :width] / own_total
    row_x = own_in.astype(bf16)
    row_cot = sums_ref[:, width : 2 * width].astype(bf16)
    pre_act = jnp.dot(row_x, in_ref[...], preferred_element_type=f32)
    hid_grad = lax.dot_general(row_cot, out_ref[...], ROWS, preferred_element_type=f32)
    cdf = 0.5 * (1.0 + lax.erf(pre_act * 0.7071067811865476))
    hidden = (pre_act * cdf).astype(bf16)
    slope = cdf + pre_act * jnp.exp(-0.5 * pre_act * pre_act) * 0.3989422804014327
    pre_grad = (hid_grad * slope).astype(bf16)
    part_out = jnp.dot(hidden, out_ref[...], preferred_element_type=f32)
    part_dx = lax.dot_general(pre_grad, in_ref[...], ROWS, preferred_element_type=f32)
    message_ref[:, :width] = part_out
    message_ref[:, width : 2 * width] = part_dx
    dot_part = jnp.sum(own_in * part_dx, axis=1, keepdims=True)
    message_ref[:, 2 * width :] = jnp.broadcast_to(dot_part, spare.shape)
    row_x_ref[...] = row_x
    row_cot_ref[...] = row_cot
    hidden_ref[...] = hidden
    pre_grad_ref[...] = pre_grad


def as_row(column, lanes):
    shape = (column.shape[0], lanes)
    same = lax.broadcasted_iota(jnp.int32, shape, 0) == lax.broadcasted_iota(jnp.int32, shape, 1)
    return jnp.sum(jnp.where(same, column, 0.0), axis=0, keepdims=True)


def as_column(row, slots):
    shape = (slots, row.shape[1])
    same = lax.broadcasted_iota(jnp.int32, shape, 0) == lax.broadcasted_iota(jnp.int32, shape, 1)
    return jnp.sum(jnp.where(same, row, 0.0), axis=1, keepdims=True)


def score_grads(clip_ref, scale_ref, message_ref, totals_ref, tok_ref, cot_ref, norm_ref, exp_ref, grad_ref, dispatch_ref, phi_ref, slot_y_ref, slot_dx_ref):
    width = tok_ref.shape[1]
    experts = message_ref.shape[0]

    def of_clip(values):
        mine = lax.broadcasted_iota(jnp.int32, values.shape, 0) == clip_ref[0]
        return jnp.sum(jnp.where(mine, values, 0.0), axis=0, keepdims=True)

    slots = jnp.concatenate([of_clip(message_ref[slot]) for slot in range(experts)], axis=0)
    slot_y = slots[:, :width].astype(bf16)
    slot_dx = slots[:, width : 2 * width].astype(bf16)
    slot_y_ref[...] = slot_y
    slot_dx_ref[...] = slot_dx
    column_stat = slots[:, 2 * width : 2 * width + 1]
    totals = as_column(of_clip(totals_ref[...]), experts)
    exp_scores = exp_ref[...]
    combine_f = exp_scores / jnp.sum(exp_scores, axis=0, keepdims=True)
    comb_dot = lax.dot_general(slot_y, cot_ref[...], ROWS, preferred_element_type=f32)
    grad_comb = combine_f * (comb_dot - jnp.sum(combine_f * comb_dot, axis=0, keepdims=True))
    disp_dot = lax.dot_general(slot_dx, tok_ref[...], ROWS, preferred_element_type=f32)
    dispatch_f = exp_scores / totals
    grad_disp = dispatch_f * (disp_dot - column_stat)
    score_grad = (scale_ref[0] * (grad_comb + grad_disp)).astype(bf16)
    phi_ref[...] = jnp.dot(score_grad, norm_ref[...], preferred_element_type=f32)
    grad_ref[...] = score_grad
    dispatch_ref[...] = dispatch_f.astype(bf16)


def finish(phi_ref, *refs):
    *term_refs, grad_ref = refs
    own, *others = [ref[0] for ref in term_refs]
    phi_grad = own + others[-1]
    if len(others) > 1:
        phi_grad = phi_grad + (others[0] + others[1])
    phi = phi_ref[...].astype(f32)
    phi_scale = lax.rsqrt(jnp.sum(phi * phi, axis=1, keepdims=True) + epsilon)
    phi_unit = phi * phi_scale
    along = jnp.sum(phi_unit * phi_grad, axis=1, keepdims=True)
    grad_ref[...] = phi_scale * (phi_grad - phi_unit * along)


def in_place(operand):
    return pltpu.with_memory_space_constraint(operand, pltpu.HBM)


def per_device(tokens, cotangent, router, logit_scale, expert_in, expert_out):
    tok_in = tokens[0]
    tok_cot = cotangent[0]
    count = tok_in.shape[0]
    width, experts = router.shape
    units = expert_in.shape[1]
    size = lax.axis_size("seq")
    group = size // experts
    clips = lax.axis_size("dp")
    clip = lax.axis_index("dp")
    owned = lax.axis_index("seq") // group
    length = 2 * width + -(-experts // LANES) * LANES
    scalar = pl.BlockSpec(memory_space=pltpu.SMEM)
    in_vmem = pl.BlockSpec(memory_space=pltpu.VMEM)
    in_hbm = pl.BlockSpec(memory_space=pltpu.HBM)
    params = pltpu.CompilerParams(vmem_limit_bytes=VMEM_BYTES)
    phi = router.T
    message, exp_scores, combine, tok_scale, tok_norm = pl.pallas_call(
        token_sums,
        in_specs=[scalar, in_hbm, in_hbm, in_hbm],
        out_shape=[
            jax.ShapeDtypeStruct((experts, length), f32),
            jax.ShapeDtypeStruct((experts, count), f32),
            jax.ShapeDtypeStruct((experts, count), bf16),
            jax.ShapeDtypeStruct((count, 1), f32),
            jax.ShapeDtypeStruct((count, width), bf16),
        ],
        scratch_shapes=[
            pltpu.VMEM((experts, width), bf16),
            pltpu.VMEM((count, width), bf16),
            pltpu.VMEM((count, width), bf16),
            pltpu.SemaphoreType.DMA,
            pltpu.SemaphoreType.DMA((2, PIECES)),
        ],
        compiler_params=params,
        name="token_sums",
    )(logit_scale, in_place(phi), in_place(tok_in), in_place(tok_cot))
    message = of_clips(message)
    message, expert_in, expert_out = lax.optimization_barrier((message, expert_in, expert_out))
    expert_in, expert_out = pl.pallas_call(
        fetch,
        in_specs=[in_hbm] * 2,
        out_specs=[in_vmem] * 2,
        out_shape=[
            jax.ShapeDtypeStruct(expert_in.shape, bf16),
            jax.ShapeDtypeStruct(expert_out.shape, bf16),
        ],
        scratch_shapes=[pltpu.SemaphoreType.DMA((2, PIECES))],
        compiler_params=params,
        cost_estimate=pl.CostEstimate(
            flops=0, bytes_accessed=4 * expert_in.size + 4 * expert_out.size, transcendentals=0
        ),
        name="fetch_weights",
    )(in_place(expert_in), in_place(expert_out))
    message = sum_to_owner(message, group)[0]
    totals = message[:, 2 * width :]
    message, row_x, row_cot, hidden, pre_grad = pl.pallas_call(
        expert_rows,
        in_specs=[scalar] + [in_vmem] * 3,
        out_shape=[
            jax.ShapeDtypeStruct((clips, length), f32),
            jax.ShapeDtypeStruct((clips, width), bf16),
            jax.ShapeDtypeStruct((clips, width), bf16),
            jax.ShapeDtypeStruct((clips, units), bf16),
            jax.ShapeDtypeStruct((clips, units), bf16),
        ],
        compiler_params=params,
        name="expert_rows",
    )(owned[None], message, expert_in, expert_out)
    message, hidden, row_cot = sum_to_all(message[None], group, (hidden, row_cot))
    share = width // clips
    mine_x = lax.dynamic_slice_in_dim(row_x, clip * share, share, 1)
    mine_cot = lax.dynamic_slice_in_dim(row_cot, clip * share, share, 1)
    grad_expert_in = jnp.einsum("od,oh->dh", mine_x, pre_grad, preferred_element_type=f32)
    grad_expert_out = jnp.einsum("oh,od->hd", hidden, mine_cot, preferred_element_type=f32)
    score_grad, dispatch, phi_part, slot_y, slot_dx = pl.pallas_call(
        score_grads,
        in_specs=[scalar, scalar] + [in_vmem] * 6,
        out_shape=[
            jax.ShapeDtypeStruct((experts, count), bf16),
            jax.ShapeDtypeStruct((experts, count), bf16),
            jax.ShapeDtypeStruct((experts, width), f32),
            jax.ShapeDtypeStruct((experts, width), bf16),
            jax.ShapeDtypeStruct((experts, width), bf16),
        ],
        compiler_params=params,
        name="score_grads",
    )(clip[None], logit_scale, message, totals, tok_in, tok_cot, tok_norm, exp_scores)
    phi_sum = phi_part
    for step in range(1, clips):
        phi_sum = phi_sum + hop(phi_part, step)
    phi_sum = phi_sum[None]
    *earlier, final = rounds(size)
    for pair in earlier:
        phi_sum = added(round_terms(phi_sum, pair), pair)
    terms = round_terms(phi_sum, final)
    grad_router = pl.pallas_call(
        finish,
        in_specs=[in_vmem] * (1 + len(terms)),
        out_shape=jax.ShapeDtypeStruct((experts, width), f32),
        compiler_params=params,
        name="finish",
    )(phi, terms[0], *[terms[mask] for mask in [*final[1:], sum(final), final[0]][-len(terms) + 1 :]])
    phi_f32 = phi.astype(f32)
    phi_scale = lax.rsqrt(jnp.sum(phi_f32 * phi_f32, axis=1, keepdims=True) + epsilon)
    phi_unit = phi_f32 * phi_scale
    phi_norm = phi_unit.astype(bf16)
    mixed = jnp.einsum("sn,sd->nd", combine, slot_y, preferred_element_type=f32).astype(bf16)
    norm_grad = jnp.einsum("sn,sd->nd", score_grad, phi_norm, preferred_element_type=f32)
    through = jnp.einsum("sn,sd->nd", dispatch, slot_dx, preferred_element_type=f32)
    tok_unit = tok_in.astype(f32) * tok_scale
    back_norm = tok_scale * (
        norm_grad - tok_unit * jnp.sum(tok_unit * norm_grad, axis=1, keepdims=True)
    )
    grad_tokens = (through + back_norm).astype(bf16)
    return (mixed[None], grad_tokens[None], grad_expert_in, grad_expert_out, grad_router.T)


def solution(mesh):
    return jax.shard_map(
        per_device,
        mesh=mesh,
        in_specs=(
            P("dp", "seq", None),
            P("dp", "seq", None),
            P(),
            P(),
            P(None, "seq"),
            P("seq", None),
        ),
        out_specs=(P("dp", "seq", None), P("dp", "seq", None), P("dp", "seq"), P("seq", "dp"), P()),
        check_vma=False,
    )
```

```python
import jax
import jax.numpy as jnp
from jax import lax
from jax.experimental import pallas as pl
from jax.experimental.pallas import tpu as pltpu
from jax.sharding import PartitionSpec as P

epsilon = 1e-06
AXES = ("seq", "dp")
LANES = 128
PIECES = 4
VMEM_BYTES = 10 * 2**20
ROWS = (((1,), (1,)), ((), ()))
COLUMNS = (((0,), (0,)), ((), ()))
f32, bf16 = jnp.float32, jnp.bfloat16


def exchange(value, mask):
    clips = lax.axis_size("dp")
    pairs = []
    for place in range(lax.axis_size("seq")):
        for clip in range(clips):
            there = (place ^ mask) * clips + (clip ^ 1 if clips % 2 == 0 else clip)
            pairs.append((place * clips + clip, there))
    return lax.ppermute(value, AXES, pairs)


def hop(value, step):
    return lax.ppermute(value, "dp", [(i, i ^ step) for i in range(lax.axis_size("dp"))])


def of_clips(value):
    clips = lax.axis_size("dp")
    apart = lax.broadcasted_iota(jnp.int32, (1, clips, 1), 1) ^ lax.axis_index("dp")
    merged = value[:, None]
    for step in range(1, clips):
        merged = jnp.where(apart == step, hop(value, step)[:, None], merged)
    return merged


def rounds(size):
    masks = [1 << bit for bit in range(size.bit_length() - 1)]
    return [masks[i : i + 2] for i in range(0, len(masks), 2)]


def swaps(pair):
    return pair if len(pair) == 1 else [pair[0], pair[0] | pair[1], pair[1]]


def added(terms, masks):
    if len(masks) == 1:
        return terms[0] + terms[masks[0]]
    low, high = masks
    others = [terms[low | high], terms[high]]
    first, second = others if low == 1 else others[::-1]
    return (terms[0] + terms[low]) + (first + second)


def sum_to_owner(value, group):
    place = lax.axis_index("seq")
    for pair in reversed(rounds(lax.axis_size("seq"))):
        owner_masks = [mask for mask in pair if mask >= group]
        blocks = value.reshape((1 << len(owner_masks), -1) + value.shape[1:])

        def block_for(mask):
            index = 0
            for bit, owner_mask in enumerate(owner_masks):
                index = index + jnp.where((place ^ mask) & owner_mask != 0, 1 << bit, 0)
            return lax.dynamic_index_in_dim(blocks, index, 0, keepdims=False)

        terms = {0: block_for(0)}
        for mask in swaps(pair):
            terms[mask] = exchange(block_for(mask), mask)
        value = added(terms, pair)
    return value


def round_terms(value, pair):
    terms = {0: value}
    for mask in swaps(pair):
        terms[mask] = exchange(value, mask)
    return terms


def sum_to_all(value, group, later=()):
    place = lax.axis_index("seq")
    for pair in rounds(lax.axis_size("seq")):
        terms = round_terms(value, pair)
        inner = [mask for mask in pair if mask < group]
        outer = [mask for mask in pair if mask >= group]
        if inner:
            merged = {}
            for far in [0] + outer if len(outer) == 1 else [0]:
                merged[far] = added({mask ^ far: terms[mask] for mask in terms}, inner)
            terms = merged
        value = terms[0]
        for mask in outer:
            kept = {}
            for key in terms:
                if key & mask:
                    continue
                side = lax.broadcasted_iota(jnp.int32, (2,) + (1,) * value.ndim, 0)
                same = side == jnp.where((place & mask) != 0, 1, 0)
                both = jnp.where(same, terms[key][None], terms[key | mask][None])
                kept[key] = both.reshape((-1,) + both.shape[2:])
            terms = kept
            value = terms[0]
        if later and pair[0] == 1:
            value, *later = lax.optimization_barrier((value, *later))
    return (value, *later) if later else value


def token_sums(scale_ref, phi_ref, tok_ref, cot_ref, message_ref, exp_ref, combine_ref, tok_scale_ref, norm_ref, phi_buf, tok_buf, cot_buf, phi_sem, sems):
    experts, width = phi_ref.shape
    blocks = sems.shape[1]
    rows = tok_buf.shape[0] // blocks
    pieces = [pl.ds(index * rows, rows) for index in range(blocks)]
    phi_copy = pltpu.make_async_copy(phi_ref, phi_buf, phi_sem)
    tok_copies = [
        pltpu.make_async_copy(tok_ref.at[piece], tok_buf.at[piece], sems.at[0, index])
        for index, piece in enumerate(pieces)
    ]
    cot_copies = [
        pltpu.make_async_copy(cot_ref.at[piece], cot_buf.at[piece], sems.at[1, index])
        for index, piece in enumerate(pieces)
    ]
    for copy in tok_copies + [phi_copy] + cot_copies:
        copy.start()
    cosines = []
    for index in range(0, blocks, 2):
        for copy in tok_copies[index : index + 2]:
            copy.wait()
        piece = pl.ds(index * rows, 2 * rows)
        tok_f32 = tok_buf[piece, :].astype(f32)
        tok_scale = lax.rsqrt(jnp.sum(tok_f32 * tok_f32, axis=1, keepdims=True) + epsilon)
        tok_norm = (tok_f32 * tok_scale).astype(bf16)
        norm_ref[piece, :] = tok_norm
        tok_scale_ref[piece, :] = tok_scale
        if not index:
            phi_copy.wait()
            phi = phi_buf[...].astype(f32)
            phi_scale = lax.rsqrt(jnp.sum(phi * phi, axis=1, keepdims=True) + epsilon)
            phi_norm = (phi * phi_scale).astype(bf16)
        cosines.append(lax.dot_general(phi_norm, tok_norm, ROWS, preferred_element_type=f32))
    logits = scale_ref[0] * jnp.concatenate(cosines, axis=1)
    exp_scores = jnp.exp(logits)
    combine = (exp_scores / jnp.sum(exp_scores, axis=0, keepdims=True)).astype(bf16)
    exp_high = exp_scores.astype(bf16).astype(f32)
    halves = jnp.concatenate([exp_high, exp_scores - exp_high], axis=0).astype(bf16)
    in_parts = jnp.dot(halves, tok_buf[...], preferred_element_type=f32)
    message_ref[:, :width] = in_parts[:experts] + in_parts[experts:]
    spare = message_ref.shape[1] - 2 * width
    total = as_row(jnp.sum(exp_scores, axis=1, keepdims=True), spare)
    message_ref[:, 2 * width :] = jnp.broadcast_to(total, (experts, spare))
    exp_ref[...] = exp_scores
    combine_ref[...] = combine
    for copy in cot_copies:
        copy.wait()
    message_ref[:, width : 2 * width] = jnp.dot(combine, cot_buf[...], preferred_element_type=f32)


def fetch(in_ref, out_ref, in_buf, out_buf, sems):
    copies = []
    for which, (source, target) in enumerate([(in_ref, in_buf), (out_ref, out_buf)]):
        rows = source.shape[0] // sems.shape[1]
        for index in range(sems.shape[1]):
            piece = pl.ds(index * rows, rows)
            copies.append(
                pltpu.make_async_copy(source.at[piece], target.at[piece], sems.at[which, index])
            )
    for copy in copies:
        copy.start()
    for copy in copies:
        copy.wait()


def expert_rows(owned_ref, sums_ref, in_ref, out_ref, message_ref, row_x_ref, row_cot_ref, hidden_ref, pre_grad_ref):
    width, units = in_ref.shape
    spare = sums_ref[:, 2 * width :]
    lane = lax.broadcasted_iota(jnp.int32, spare.shape, 1)
    own_total = jnp.sum(jnp.where(lane == owned_ref[0], spare, 0.0), axis=1, keepdims=True)
    own_in = sums_ref[:, :width] / own_total
    row_x = own_in.astype(bf16)
    row_cot = sums_ref[:, width : 2 * width].astype(bf16)
    pre_act = jnp.dot(row_x, in_ref[...], preferred_element_type=f32)
    hid_grad = lax.dot_general(row_cot, out_ref[...], ROWS, preferred_element_type=f32)
    cdf = 0.5 * (1.0 + lax.erf(pre_act * 0.7071067811865476))
    hidden = (pre_act * cdf).astype(bf16)
    slope = cdf + pre_act * jnp.exp(-0.5 * pre_act * pre_act) * 0.3989422804014327
    pre_grad = (hid_grad * slope).astype(bf16)
    part_out = jnp.dot(hidden, out_ref[...], preferred_element_type=f32)
    part_dx = lax.dot_general(pre_grad, in_ref[...], ROWS, preferred_element_type=f32)
    message_ref[:, :width] = part_out
    message_ref[:, width : 2 * width] = part_dx
    dot_part = jnp.sum(own_in * part_dx, axis=1, keepdims=True)
    message_ref[:, 2 * width :] = jnp.broadcast_to(dot_part, spare.shape)
    row_x_ref[...] = row_x
    row_cot_ref[...] = row_cot
    hidden_ref[...] = hidden
    pre_grad_ref[...] = pre_grad


def as_row(column, lanes):
    shape = (column.shape[0], lanes)
    same = lax.broadcasted_iota(jnp.int32, shape, 0) == lax.broadcasted_iota(jnp.int32, shape, 1)
    return jnp.sum(jnp.where(same, column, 0.0), axis=0, keepdims=True)


def as_column(row, slots):
    shape = (slots, row.shape[1])
    same = lax.broadcasted_iota(jnp.int32, shape, 0) == lax.broadcasted_iota(jnp.int32, shape, 1)
    return jnp.sum(jnp.where(same, row, 0.0), axis=1, keepdims=True)


def score_grads(scale_ref, slots_ref, totals_ref, tok_ref, cot_ref, norm_ref, exp_ref, grad_ref, dispatch_ref, phi_ref):
    width = tok_ref.shape[1]
    slot_y = slots_ref[:, :width].astype(bf16)
    slot_dx = slots_ref[:, width : 2 * width].astype(bf16)
    column_stat = slots_ref[:, 2 * width : 2 * width + 1]
    totals = as_column(totals_ref[...], slot_y.shape[0])
    exp_scores = exp_ref[...]
    combine_f = exp_scores / jnp.sum(exp_scores, axis=0, keepdims=True)
    comb_dot = lax.dot_general(slot_y, cot_ref[...], ROWS, preferred_element_type=f32)
    grad_comb = combine_f * (comb_dot - jnp.sum(combine_f * comb_dot, axis=0, keepdims=True))
    disp_dot = lax.dot_general(slot_dx, tok_ref[...], ROWS, preferred_element_type=f32)
    dispatch_f = exp_scores / totals
    grad_disp = dispatch_f * (disp_dot - column_stat)
    score_grad = (scale_ref[0] * (grad_comb + grad_disp)).astype(bf16)
    phi_ref[...] = jnp.dot(score_grad, norm_ref[...], preferred_element_type=f32)
    grad_ref[...] = score_grad
    dispatch_ref[...] = dispatch_f.astype(bf16)


def finish(phi_ref, *refs):
    *term_refs, grad_ref = refs
    own, *others = [ref[0] for ref in term_refs]
    phi_grad = own + others[-1]
    if len(others) > 1:
        phi_grad = phi_grad + (others[0] + others[1])
    phi = phi_ref[...].astype(f32)
    phi_scale = lax.rsqrt(jnp.sum(phi * phi, axis=1, keepdims=True) + epsilon)
    phi_unit = phi * phi_scale
    along = jnp.sum(phi_unit * phi_grad, axis=1, keepdims=True)
    grad_ref[...] = phi_scale * (phi_grad - phi_unit * along)


def in_place(operand):
    return pltpu.with_memory_space_constraint(operand, pltpu.HBM)


def per_device(tokens, cotangent, router, logit_scale, expert_in, expert_out):
    tok_in = tokens[0]
    tok_cot = cotangent[0]
    count = tok_in.shape[0]
    width, experts = router.shape
    units = expert_in.shape[1]
    size = lax.axis_size("seq")
    group = size // experts
    clips = lax.axis_size("dp")
    clip = lax.axis_index("dp")
    owned = lax.axis_index("seq") // group
    length = 2 * width + -(-experts // LANES) * LANES
    scalar = pl.BlockSpec(memory_space=pltpu.SMEM)
    in_vmem = pl.BlockSpec(memory_space=pltpu.VMEM)
    in_hbm = pl.BlockSpec(memory_space=pltpu.HBM)
    params = pltpu.CompilerParams(vmem_limit_bytes=VMEM_BYTES)
    phi = router.T
    message, exp_scores, combine, tok_scale, tok_norm = pl.pallas_call(
        token_sums,
        in_specs=[scalar, in_hbm, in_hbm, in_hbm],
        out_shape=[
            jax.ShapeDtypeStruct((experts, length), f32),
            jax.ShapeDtypeStruct((experts, count), f32),
            jax.ShapeDtypeStruct((experts, count), bf16),
            jax.ShapeDtypeStruct((count, 1), f32),
            jax.ShapeDtypeStruct((count, width), bf16),
        ],
        scratch_shapes=[
            pltpu.VMEM((experts, width), bf16),
            pltpu.VMEM((count, width), bf16),
            pltpu.VMEM((count, width), bf16),
            pltpu.SemaphoreType.DMA,
            pltpu.SemaphoreType.DMA((2, PIECES)),
        ],
        compiler_params=params,
        name="token_sums",
    )(logit_scale, in_place(phi), in_place(tok_in), in_place(tok_cot))
    message = of_clips(message)
    message, expert_in, expert_out = lax.optimization_barrier((message, expert_in, expert_out))
    expert_in, expert_out = pl.pallas_call(
        fetch,
        in_specs=[in_hbm] * 2,
        out_specs=[in_vmem] * 2,
        out_shape=[
            jax.ShapeDtypeStruct(expert_in.shape, bf16),
            jax.ShapeDtypeStruct(expert_out.shape, bf16),
        ],
        scratch_shapes=[pltpu.SemaphoreType.DMA((2, PIECES))],
        compiler_params=params,
        cost_estimate=pl.CostEstimate(
            flops=0, bytes_accessed=4 * expert_in.size + 4 * expert_out.size, transcendentals=0
        ),
        name="fetch_weights",
    )(in_place(expert_in), in_place(expert_out))
    message = sum_to_owner(message, group)[0]
    totals = message[:, 2 * width :]
    message, row_x, row_cot, hidden, pre_grad = pl.pallas_call(
        expert_rows,
        in_specs=[scalar] + [in_vmem] * 3,
        out_shape=[
            jax.ShapeDtypeStruct((clips, length), f32),
            jax.ShapeDtypeStruct((clips, width), bf16),
            jax.ShapeDtypeStruct((clips, width), bf16),
            jax.ShapeDtypeStruct((clips, units), bf16),
            jax.ShapeDtypeStruct((clips, units), bf16),
        ],
        compiler_params=params,
        name="expert_rows",
    )(owned[None], message, expert_in, expert_out)
    message, hidden, row_cot = sum_to_all(message[None], group, (hidden, row_cot))
    slots = lax.dynamic_index_in_dim(message, clip, 1, keepdims=False)
    totals = lax.dynamic_index_in_dim(totals, clip, 0, keepdims=True)
    share = width // clips
    mine_x = lax.dynamic_slice_in_dim(row_x, clip * share, share, 1)
    mine_cot = lax.dynamic_slice_in_dim(row_cot, clip * share, share, 1)
    grad_expert_in = jnp.einsum("od,oh->dh", mine_x, pre_grad, preferred_element_type=f32)
    grad_expert_out = jnp.einsum("oh,od->hd", hidden, mine_cot, preferred_element_type=f32)
    score_grad, dispatch, phi_part = pl.pallas_call(
        score_grads,
        in_specs=[scalar] + [in_vmem] * 6,
        out_shape=[
            jax.ShapeDtypeStruct((experts, count), bf16),
            jax.ShapeDtypeStruct((experts, count), bf16),
            jax.ShapeDtypeStruct((experts, width), f32),
        ],
        compiler_params=params,
        name="score_grads",
    )(logit_scale, slots, totals, tok_in, tok_cot, tok_norm, exp_scores)
    phi_sum = phi_part
    for step in range(1, clips):
        phi_sum = phi_sum + hop(phi_part, step)
    phi_sum = phi_sum[None]
    *earlier, final = rounds(size)
    for pair in earlier:
        phi_sum = added(round_terms(phi_sum, pair), pair)
    terms = round_terms(phi_sum, final)
    grad_router = pl.pallas_call(
        finish,
        in_specs=[in_vmem] * (1 + len(terms)),
        out_shape=jax.ShapeDtypeStruct((experts, width), f32),
        compiler_params=params,
        name="finish",
    )(phi, terms[0], *[terms[mask] for mask in [*final[1:], sum(final), final[0]][-len(terms) + 1 :]])
    phi_f32 = phi.astype(f32)
    phi_scale = lax.rsqrt(jnp.sum(phi_f32 * phi_f32, axis=1, keepdims=True) + epsilon)
    phi_unit = phi_f32 * phi_scale
    phi_norm = phi_unit.astype(bf16)
    slot_y = slots[:, :width].astype(bf16)
    slot_dx = slots[:, width : 2 * width].astype(bf16)
    mixed = jnp.einsum("sn,sd->nd", combine, slot_y, preferred_element_type=f32).astype(bf16)
    norm_grad = jnp.einsum("sn,sd->nd", score_grad, phi_norm, preferred_element_type=f32)
    through = jnp.einsum("sn,sd->nd", dispatch, slot_dx, preferred_element_type=f32)
    tok_unit = tok_in.astype(f32) * tok_scale
    back_norm = tok_scale * (
        norm_grad - tok_unit * jnp.sum(tok_unit * norm_grad, axis=1, keepdims=True)
    )
    grad_tokens = (through + back_norm).astype(bf16)
    return (mixed[None], grad_tokens[None], grad_expert_in, grad_expert_out, grad_router.T)


def solution(mesh):
    return jax.shard_map(
        per_device,
        mesh=mesh,
        in_specs=(
            P("dp", "seq", None),
            P("dp", "seq", None),
            P(),
            P(),
            P(None, "seq"),
            P("seq", None),
        ),
        out_specs=(P("dp", "seq", None), P("dp", "seq", None), P("dp", "seq"), P("seq", "dp"), P()),
        check_vma=False,
    )
```
